512 devices in a mesh: dp: 4 (over x), expert: 128 (over y, z, core).
Axes of the slice: x: 4, y: 4, z: 16, core: 2. Of those that a mesh axis runs over, the one named last changes fastest.
Arguments:
- grad_out: bfloat16 [8192, 2048], P(('dp', 'expert')), may hold values from -4 to 4
- x_codes: bfloat16 [8192, 2048], P(('dp', 'expert')), may hold values from -6 to 6
- x_scales: bfloat16 [8192, 16], P(('dp', 'expert')), may hold values from 0.25 to 4
- combine: bfloat16 [8192, 8], P(('dp', 'expert')), may hold values from 0.049804688 to 1
- expert_ids: int32 [8192, 8], P(('dp', 'expert')), may hold values from 0 to 127, all different within a row; in each aligned block of 16 rows (0 to 15, 16 to 31, ...) at most 2 rows name the same one
- w_gate: bfloat16 [128, 768, 2048], P('expert', 'dp'), may hold values from -0.125 to 0.125
- w_up: bfloat16 [128, 768, 2048], P('expert', 'dp'), may hold values from -0.125 to 0.125
- w_down: bfloat16 [128, 768, 2048], P('expert', 'dp'), may hold values from -0.21875 to 0.21875
Outputs:
- grad_in: bfloat16 [8192, 2048], P(('dp', 'expert'))
- grad_combine: float32 [8192, 8], P(('dp', 'expert'))
- grad_gate: bfloat16 [128, 768, 2048], P('expert', 'dp')
- grad_up: bfloat16 [128, 768, 2048], P('expert', 'dp')
- grad_down: bfloat16 [128, 768, 2048], P('expert', 'dp')
The draws below stay inside these ranges and needn't reach their ends.
Inputs may be any that keep to these rules, and one draw needn't show every extreme that they name: `expert_ids`: each token names 8 different experts. Among the 16 tokens of one device no expert is named more than 2 times, and on some devices some expert is named exactly 2 times.
All inputs are finite; a program needn't handle non-finite values.
Results may differ from the reference program's by a relative error of at most 0.015.
Values may be sent and summed in bfloat16 or wider, within the bound.
No kernel may reach another device: no remote copies, remote signals or barrier semaphores. Data moves between devices by JAX's collectives and lax.ppermute only.
A program may use at most 128 MiB of HBM per device.

```python
import math
import jax
import jax.numpy as jnp
import numpy as np
from jax import lax

D = 2048
FF = 768
TOP = 8
BLOCK = 128
TOK_DEV = 16
EXPERTS = 128
CAP = 2
TOKENS = 8192
N_DP = 4


def level_of(stream_key, shape, pieces, least, largest):
    factor_of, own = 1.0, jax.random.fold_in(stream_key, 6)
    for dim, parts in pieces:
        draws = jnp.exp(jax.random.uniform(jax.random.fold_in(own, dim), (parts,), jnp.float32, least / len(pieces), largest / len(pieces)))
        factor_of = factor_of * jnp.repeat(draws, shape[dim] // parts).reshape([-1 if axis == dim else 1 for axis in range(len(shape))])
    return factor_of


def assign_block(rng, own, number, rows, count, top, limit, lean):
    ranking = jax.random.permutation(rng, count)
    packed, usual = load_shares(count, rows * top, limit, lean, True), load_shares(count, rows * top, limit, lean, False)
    places = jnp.arange(count)

    def named(sizes, offset_by):
        used = int((sizes > 0).sum())
        fixed = max(1, used // 4)
        shifted = fixed + (places - fixed + offset_by * (used - fixed)) % max(1, count - fixed)
        return jnp.zeros((count,), jnp.int32).at[ranking[jnp.where(places < fixed, places, shifted)]].set(jnp.asarray(sizes, jnp.int32))

    sizes = jnp.where(number % 4 == 0, named(packed, number // 4), named(usual, number - number // 4 - 1))
    mixed = jax.random.permutation(jax.random.fold_in(own, 3), count)
    donor, receiver = mixed[0:count // 2 * 2:2], mixed[1:count // 2 * 2:2]
    room = jnp.minimum(sizes[donor] - 1, limit - sizes[receiver]) // 2
    room = jnp.where((donor == ranking[0]) | (receiver == ranking[0]) | (sizes[receiver] == 0), 0, jnp.maximum(room, 0))
    shifted = jax.random.randint(jax.random.fold_in(own, 4), (count // 2,), 0, 1 << 20) % (room + 1)
    sizes = sizes.at[donor].add(-shifted).at[receiver].add(shifted)
    labels = jnp.searchsorted(jnp.cumsum(sizes), jnp.arange(rows * top), side="right").astype(jnp.int32)
    listing = labels.reshape(top, rows).T
    listing = listing[jax.random.permutation(jax.random.fold_in(own, 1), rows)]
    offset_by = jax.random.randint(jax.random.fold_in(own, 2), (rows, 1), 0, top)
    return jnp.take_along_axis(listing, (jnp.arange(top)[None, :] + offset_by) % top, axis=1)


def load_shares(count, total, limit, slope, full):
    weights = [(1 << 20) // math.isqrt(grade ** slope) + 1 for grade in range(1, count + 1)]
    largest = limit if full else min(limit, max(-(-total // count), total * weights[0] // sum(weights)))
    least = 1 if total - largest >= count - 1 else 0
    holding, rest = [largest] + [least] * (count - 1), total - largest - least * (count - 1)
    while rest > 0:
        movable = [i for i in range(1, count) if holding[i] < largest] or [i for i in range(1, count) if holding[i] < limit]
        pool, budget = sum([weights[i] for i in movable]), rest
        for i in movable:
            addition = min(limit - holding[i], max(1, budget * weights[i] // pool), rest)
            holding[i] = holding[i] + addition
            rest = rest - addition
    return np.array(holding)


def bell_draw(own_key, extent, deviation, reach, pieces=(), held_as=jnp.bfloat16):
    array = jax.random.normal(own_key, extent, jnp.float32) * deviation
    if len(pieces) > 0:
        array = level_of(own_key, extent, pieces, -0.22, 0.18) * array
    return jnp.clip(array, min=-reach, max=reach).astype(held_as)


def setup_inputs(seed: int = 0) -> dict:
    keys = jax.random.split(jax.random.key(seed), 9)
    grad_out = bell_draw(keys[0], (TOKENS, D), 0.3, 4.0, ((0, 512),))
    x_codes = bell_draw(keys[1], (TOKENS, D), 1.0, 6.0, ((0, 512),))
    x_scales = jnp.clip(jnp.exp(math.log(4.0) - 2.7725887 * jax.random.uniform(keys[2], (TOKENS, D // BLOCK), jnp.float32) ** level_of(keys[2], (TOKENS, D // BLOCK), ((0, 512),), -0.2, 0.2)), 0.25, 4.0).astype(jnp.bfloat16)
    combine = jnp.clip(jnp.exp(math.log(1.0) - 2.9996462 * jax.random.uniform(keys[3], (TOKENS, TOP), jnp.float32) ** level_of(keys[3], (TOKENS, TOP), ((0, 512),), -0.2, 0.2)), 0.049804688, 1.0).astype(jnp.bfloat16)
    expert_ids_keys = jax.random.split(jax.random.fold_in(keys[4], 1), TOKENS // TOK_DEV)
    expert_ids_turns = jax.random.permutation(jax.random.fold_in(keys[4], 3), TOKENS // TOK_DEV)
    expert_ids = jax.vmap(lambda own, number: assign_block(jax.random.fold_in(keys[4], 2), own, number, TOK_DEV, EXPERTS, TOP, CAP, 2))(expert_ids_keys, expert_ids_turns).reshape((TOKENS, TOP))
    w_gate = bell_draw(keys[5], (EXPERTS, FF, D), D ** -0.5, 0.125, ((0, 128), (1, 4)))
    w_up = bell_draw(keys[6], (EXPERTS, FF, D), D ** -0.5, 0.125, ((0, 128), (1, 4)))
    w_down = bell_draw(keys[7], (EXPERTS, FF, D), FF ** -0.5, 0.21875, ((0, 128), (1, 4)))
    return dict(grad_out=grad_out, x_codes=x_codes, x_scales=x_scales, combine=combine, expert_ids=expert_ids, w_gate=w_gate, w_up=w_up, w_down=w_down)


def slot_positions(block_ids):
    onehot = (block_ids[:, None] == jnp.arange(EXPERTS, dtype=jnp.int32)[None, :]).astype(jnp.int32)
    before = jnp.cumsum(onehot, axis=0) - onehot
    return jnp.sum(before * onehot, axis=1).astype(jnp.int32)


def reference(grad_out, x_codes, x_scales, combine, expert_ids, w_gate, w_up, w_down):
    blocks = TOKENS // TOK_DEV
    picks_all = TOKENS * TOP
    quarter = FF // N_DP
    flat_ids = expert_ids.reshape(-1).astype(jnp.int32)
    position = jax.vmap(slot_positions)(expert_ids.reshape(blocks, TOK_DEV * TOP).astype(jnp.int32)).reshape(-1)
    block_of = jnp.repeat(jnp.arange(blocks, dtype=jnp.int32), TOK_DEV * TOP)
    slot_index = (block_of * CAP + position).astype(jnp.int32)
    row_table = jnp.full((EXPERTS, blocks * CAP), picks_all, dtype=jnp.int32)
    row_table = row_table.at[flat_ids, slot_index].set(jnp.arange(picks_all, dtype=jnp.int32))
    x_all = (x_codes.astype(jnp.float32).reshape(TOKENS, D // BLOCK, BLOCK)
             * x_scales.astype(jnp.float32)[:, :, None]).reshape(TOKENS, D).astype(jnp.bfloat16)
    x_pad = jnp.concatenate([x_all, jnp.zeros((1, D), jnp.bfloat16)], axis=0)
    grad_pad = jnp.concatenate([grad_out, jnp.zeros((1, D), jnp.bfloat16)], axis=0)
    weight_pad = jnp.concatenate([combine.reshape(-1).astype(jnp.float32), jnp.zeros((1,), jnp.float32)], axis=0)

    def expert_step(totals, per_expert):
        input_total, combine_total = totals
        chosen, gate_w, up_w, down_w = per_expert
        token_index = chosen // TOP
        x_rows = x_pad[token_index]
        grad_rows = grad_pad[token_index]
        weight_rows = weight_pad[chosen]
        gate_pre = lax.dot_general(x_rows, gate_w, (((1,), (1,)), ((), ())), preferred_element_type=jnp.float32)
        up_pre = lax.dot_general(x_rows, up_w, (((1,), (1,)), ((), ())), preferred_element_type=jnp.float32)
        sigmoid_gate = jax.nn.sigmoid(gate_pre)
        activated = gate_pre * sigmoid_gate
        hidden = (activated * up_pre).astype(jnp.bfloat16)
        scaled = (weight_rows[:, None] * grad_rows.astype(jnp.float32)).astype(jnp.bfloat16)
        backward = lax.dot_general(grad_rows, down_w, (((1,), (1,)), ((), ())), preferred_element_type=jnp.float32)
        comb_rows = jnp.sum(backward * hidden.astype(jnp.float32), axis=1)
        grad_hidden = weight_rows[:, None] * backward
        grad_gate_pre = (grad_hidden * up_pre * sigmoid_gate * (1.0 + gate_pre * (1.0 - sigmoid_gate))).astype(jnp.bfloat16)
        grad_up_pre = (grad_hidden * activated).astype(jnp.bfloat16)
        grad_down_e = lax.dot_general(hidden, scaled, (((0,), (0,)), ((), ())), preferred_element_type=jnp.float32).astype(jnp.bfloat16)
        grad_gate_e = lax.dot_general(grad_gate_pre, x_rows, (((0,), (0,)), ((), ())), preferred_element_type=jnp.float32).astype(jnp.bfloat16)
        grad_up_e = lax.dot_general(grad_up_pre, x_rows, (((0,), (0,)), ((), ())), preferred_element_type=jnp.float32).astype(jnp.bfloat16)
        quarter_terms = jnp.einsum("sjf,jfd->jsd",
                                   grad_gate_pre.astype(jnp.float32).reshape(-1, N_DP, quarter),
                                   gate_w.astype(jnp.float32).reshape(N_DP, quarter, D))
        quarter_terms = quarter_terms + jnp.einsum("sjf,jfd->jsd",
                                                   grad_up_pre.astype(jnp.float32).reshape(-1, N_DP, quarter),
                                                   up_w.astype(jnp.float32).reshape(N_DP, quarter, D))
        rounded = lax.optimization_barrier(quarter_terms.astype(jnp.bfloat16)).astype(jnp.float32)
        input_rows = jnp.sum(rounded, axis=0)
        input_total = input_total.at[token_index].add(input_rows)
        combine_total = combine_total.at[chosen].add(comb_rows)
        return (input_total, combine_total), (grad_gate_e, grad_up_e, grad_down_e)

    initial = (jnp.zeros((TOKENS + 1, D), jnp.float32), jnp.zeros((picks_all + 1,), jnp.float32))
    (input_total, combine_total), (grad_gate, grad_up, grad_down) = lax.scan(
        expert_step, initial, (row_table, w_gate, w_up, w_down))
    grad_in = input_total[:TOKENS].astype(jnp.bfloat16)
    grad_combine = combine_total[:picks_all].reshape(TOKENS, TOP)
    return (grad_in, grad_combine, grad_gate, grad_up, grad_down)
```

```python
import jax
import jax.numpy as jnp
from jax import lax
from jax.sharding import Mesh, PartitionSpec as P

BLOCK = 128
Y, Z, CORE = 4, 16, 2
DP = 4
F32, BF16 = jnp.float32, jnp.bfloat16
WEIGHTS = "pp"
GRADS = "pp"


def shift(a, k):
    return lax.ppermute(a, "dp", [(i, (i + k) % DP) for i in range(DP)])


def nt(a, b):
    return lax.dot_general(a, b, (((1,), (1,)), ((), ())), preferred_element_type=F32)


def tn(a, b):
    return lax.dot_general(a, b, (((0,), (0,)), ((), ())), preferred_element_type=F32)


def gather_weights(mine):
    half = mine.shape[0] // 2
    from_prev, from_next = shift(mine, 1), shift(mine, -1)
    top, bottom = shift(from_prev[:half], 1), shift(from_next[half:], -1)
    return from_next, from_prev, jnp.concatenate([top, bottom], axis=0)


def scatter_grads(own, nxt, prv, far):
    half = own.shape[0] // 2
    far_top, far_bottom = shift(far[:half], 1), shift(far[half:], -1)
    next_bottom, prev_top = shift(nxt[half:], 1), shift(prv[:half], -1)
    next_top = shift((nxt[:half].astype(F32) + far_top.astype(F32)).astype(BF16), 1)
    prev_bottom = shift((prv[half:].astype(F32) + far_bottom.astype(F32)).astype(BF16), -1)
    top = own[:half].astype(F32) + prev_top.astype(F32) + next_top.astype(F32)
    bottom = own[half:].astype(F32) + next_bottom.astype(F32) + prev_bottom.astype(F32)
    return jnp.concatenate([top, bottom], axis=0).astype(BF16)


def expert_block(x_rows, grad_rows, scaled, weight, w):
    share = w.shape[0] // 3
    both = nt(x_rows, w[: 2 * share])
    gate, up = both[:, :share], both[:, share:]
    back = nt(grad_rows, w[2 * share :])
    sig = jax.nn.sigmoid(gate)
    act = gate * sig
    hidden = (act * up).astype(BF16)
    comb = jnp.sum(back * hidden.astype(F32), axis=1)
    gh = weight * back
    d_gate = (gh * up * sig * (1.0 + gate * (1.0 - sig))).astype(BF16)
    d_up = (gh * act).astype(BF16)
    d_both = jnp.concatenate([d_gate, d_up], axis=1)
    part = jnp.dot(d_both, w[: 2 * share], preferred_element_type=F32).astype(BF16)
    d_w = jnp.concatenate([tn(d_both, x_rows).astype(BF16), tn(hidden, scaled).astype(BF16)], axis=0)
    return part, comb, d_w


def body(grad_out, x_codes, x_scales, combine, expert_ids, w_gate, w_up, w_down):
    tokens, picks = expert_ids.shape
    width = grad_out.shape[1]
    share = w_gate.shape[1]
    experts = Y * Z * CORE
    capacity = 2
    z, y, core = lax.axis_index("z"), lax.axis_index("y"), lax.axis_index("core")
    mine = jnp.concatenate([w_gate[0], w_up[0], w_down[0]], axis=0)
    w_next, w_prev, w_far = gather_weights(mine)

    x = (
        (x_codes.astype(F32).reshape(tokens, width // BLOCK, BLOCK) * x_scales.astype(F32)[:, :, None])
        .reshape(tokens, width)
        .astype(BF16)
    )
    names = (expert_ids[:, :, None] == jnp.arange(experts, dtype=jnp.int32)).astype(F32)
    dense = jnp.sum(names * combine.astype(F32)[:, :, None], axis=1)
    payload = jnp.concatenate([x, grad_out, dense.astype(BF16)], axis=1)
    seen = lax.all_gather(payload, "z", axis=0, tiled=True)

    count = Z * tokens
    slots = Z * capacity
    lanes = lax.broadcasted_iota(jnp.int32, (experts, Y * CORE), 0)
    dest = lax.broadcasted_iota(jnp.int32, (experts, Y * CORE), 1)
    pick_dest = (lanes == ((dest // CORE) * Z + z) * CORE + dest % CORE).astype(BF16)
    member = (seen[:, 2 * width :] != 0).astype(BF16)
    local = jnp.dot(member, pick_dest, preferred_element_type=F32)
    ti = lax.broadcasted_iota(jnp.int32, (count, count), 0)
    tj = lax.broadcasted_iota(jnp.int32, (count, count), 1)
    earlier = ((ti // tokens == tj // tokens) & (tj < ti)).astype(BF16)
    before = jnp.dot(earlier, local.astype(BF16), preferred_element_type=F32)
    slot_of = before.astype(jnp.int32) + (lax.broadcasted_iota(jnp.int32, before.shape, 0) // tokens) * capacity
    slot_of = jnp.where(local > 0, slot_of, -1)
    select = (slot_of.T[:, None, :] == lax.broadcasted_iota(jnp.int32, (Y * CORE, slots, count), 1)).astype(BF16)
    sent = jnp.dot(select.reshape(Y * CORE * slots, count), seen, preferred_element_type=F32).astype(BF16)
    rows = lax.all_to_all(
        sent.reshape(Y * CORE, slots, -1), ("y", "core"), split_axis=0, concat_axis=0, tiled=True
    ).reshape(Y * CORE * slots, -1)

    x_rows, grad_rows = rows[:, :width], rows[:, width : 2 * width]
    me = (y * Z + z) * CORE + core
    at = lax.broadcasted_iota(jnp.int32, (1, experts), 1) == me
    weight = jnp.sum(jnp.where(at, rows[:, 2 * width :].astype(F32), 0.0), axis=1, keepdims=True)
    scaled = (weight * grad_rows.astype(F32)).astype(BF16)

    outs = [expert_block(x_rows, grad_rows, scaled, weight, w) for w in (w_far, w_next, w_prev, mine)]
    total = sum(o[0].astype(F32) for o in outs)
    comb = sum(o[1] for o in outs)
    far, nxt, prv, own = (o[2] for o in outs)
    d_w = scatter_grads(own, nxt, prv, far)

    high = comb.astype(BF16)
    low = (comb - high.astype(F32)).astype(BF16)
    tail = jnp.concatenate([high[:, None], low[:, None], jnp.zeros((comb.shape[0], 126), BF16)], axis=1)
    back = jnp.concatenate([total.astype(BF16), tail], axis=1)
    back = back.reshape(Y, CORE, Z, capacity, -1).transpose(0, 2, 1, 3, 4).reshape(experts, capacity, -1)
    home = lax.all_to_all(back, ("y", "z", "core"), split_axis=0, concat_axis=0, tiled=True)
    home = home.reshape(experts * capacity, -1)

    named = jnp.sum(names, axis=1)
    th = lax.broadcasted_iota(jnp.int32, (tokens, tokens), 0)
    tk = lax.broadcasted_iota(jnp.int32, (tokens, tokens), 1)
    prior = jnp.dot((tk < th).astype(F32), named)
    cap = lax.broadcasted_iota(jnp.int32, (1, 1, capacity), 2)
    owner = (named[:, :, None] > 0) & (prior[:, :, None].astype(jnp.int32) == cap)
    owner = owner.reshape(tokens, experts * capacity).astype(BF16)
    grad_in = jnp.dot(owner, home[:, :width], preferred_element_type=F32).astype(BF16)
    comb_rows = home[:, width].astype(F32) + home[:, width + 1].astype(F32)
    of_expert = jnp.sum((owner.astype(F32) * comb_rows[None, :]).reshape(tokens, experts, capacity), axis=2)
    grad_combine = jnp.sum(names * of_expert[:, None, :], axis=2)
    return (
        grad_in,
        grad_combine,
        d_w[None, :share],
        d_w[None, share : 2 * share],
        d_w[None, 2 * share :],
    )


def solution(mesh):
    fine = Mesh(mesh.devices.reshape(DP, Y, Z, CORE), ("dp", "y", "z", "core"))
    tok = P(("dp", "y", "z", "core"), None)
    wts = P(("y", "z", "core"), "dp", None)
    return jax.shard_map(
        body,
        mesh=fine,
        in_specs=(tok,) * 5 + (wts,) * 3,
        out_specs=(tok, tok, wts, wts, wts),
        check_vma=False,
    )
```

```python
import functools

import jax
import jax.numpy as jnp
from jax import lax
from jax.experimental import pallas as pl
from jax.experimental.pallas import tpu as pltpu
from jax.sharding import Mesh, PartitionSpec as P

BLOCK = 128
DP, Y, Z, CORE = 4, 4, 16, 2
STRIDE = 4
YC = Y * CORE
CAP = 2
F32, BF16 = jnp.float32, jnp.bfloat16


def shift(a, axis, size, k):
    return lax.ppermute(a, axis, [(i, (i + k) % size) for i in range(size)])


def nt(a, b):
    return lax.dot_general(a, b, (((1,), (1,)), ((), ())), preferred_element_type=F32)


def tn(a, b):
    return lax.dot_general(a, b, (((0,), (0,)), ((), ())), preferred_element_type=F32)


def nn(a, b):
    return jnp.dot(a, b, preferred_element_type=F32)


def gather_weights(mine):
    half = mine.shape[0] // 2
    from_prev, from_next = shift(mine, "dp", DP, 1), shift(mine, "dp", DP, -1)
    top, bottom = shift(from_prev[:half], "dp", DP, 1), shift(from_next[half:], "dp", DP, -1)
    return from_next, from_prev, top, bottom


def add(a, b):
    return (a.astype(F32) + b.astype(F32)).astype(BF16)


def block_kernel(last, rows_ref, own_ref, top_ref, bottom_ref, comb_ref, *refs):
    if last:
        part_a, part_b, part_c, perm_ref, d_top, d_bottom, back_ref = refs
    else:
        d_top, d_bottom, part_ref, comb_out = refs
    width = top_ref.shape[1]
    half = top_ref.shape[0]
    share = 2 * half // 3
    rest = half - share
    x = rows_ref[:, :width]
    grad = rows_ref[:, width : 2 * width]
    weight = jnp.sum(rows_ref[:, 2 * width :].astype(F32) * own_ref[...], axis=1, keepdims=True)
    w_gate = top_ref[:share]
    w_up = jnp.concatenate([top_ref[share:], bottom_ref[:rest]], axis=0)
    w_down = bottom_ref[rest:]
    gate = nt(x, w_gate)
    up = nt(x, w_up)
    back = nt(grad, w_down)
    sig = jax.nn.sigmoid(gate)
    act = gate * sig
    hidden = (act * up).astype(BF16)
    comb = comb_ref[...] + jnp.sum(back * hidden.astype(F32), axis=1, keepdims=True)
    gh = weight * back
    d_gate = (gh * up * sig * (1.0 + gate * (1.0 - sig))).astype(BF16)
    d_up = (gh * act).astype(BF16)
    scaled = (weight * grad.astype(F32)).astype(BF16)
    d_top[:share] = tn(d_gate, x).astype(BF16)
    d_up_w = tn(d_up, x).astype(BF16)
    d_top[share:] = d_up_w[:rest]
    d_bottom[:rest] = d_up_w[rest:]
    d_bottom[rest:] = tn(hidden, scaled).astype(BF16)
    part = (nn(d_gate, w_gate) + nn(d_up, w_up)).astype(BF16)
    if last:
        total = part.astype(F32) + part_a[...].astype(F32) + part_b[...].astype(F32) + part_c[...].astype(F32)
        perm = perm_ref[...]
        back_ref[:, :width] = nn(perm, total.astype(BF16)).astype(BF16)
        high = comb.astype(BF16)
        low = (comb - high.astype(F32)).astype(BF16)
        lane = lax.broadcasted_iota(jnp.int32, high.shape, 1)
        tail = jnp.where(lane == 0, high.astype(F32), jnp.where(lane == 1, low.astype(F32), 0.0))
        back_ref[:, width:] = nn(perm, tail.astype(BF16)).astype(BF16)
    else:
        part_ref[...] = part
        comb_out[...] = comb


def expert_block(rows, own, weights, comb, last=()):
    n, width = rows.shape[0], weights[0].shape[1]
    if len(weights) == 1:
        half = weights[0].shape[0] // 2
        w_specs = [pl.BlockSpec((half, width), lambda i, k=k: (k, 0)) for k in range(2)]
        weights = weights * 2
    else:
        half = weights[0].shape[0]
        w_specs = [pl.BlockSpec((half, width), lambda i: (0, 0))] * 2
    whole = lambda a: pl.BlockSpec(a.shape, lambda i: (0,) * a.ndim)
    sds = jax.ShapeDtypeStruct
    out = [sds((half, width), BF16), sds((half, width), BF16)]
    out += [sds((n, width + 128), BF16)] if last else [sds((n, width), BF16), sds((n, 128), F32)]
    return pl.pallas_call(
        functools.partial(block_kernel, bool(last)),
        grid=(1,),
        out_shape=out,
        in_specs=[whole(rows), whole(own), *w_specs, whole(comb), *[whole(a) for a in last]],
        out_specs=[whole(o) for o in out],
        compiler_params=pltpu.CompilerParams(vmem_limit_bytes=40 * 2**20),
        cost_estimate=pl.CostEstimate(flops=2 * 8 * n * 256 * width, bytes_accessed=9 * 2**20, transcendentals=n * 192),
    )(rows, own, *weights, comb, *last)


def dispatch(chunk, z, tokens, width):
    n = chunk.shape[0]
    lane = lax.broadcasted_iota(jnp.int32, (YC * Z, YC), 0)
    dest = lax.broadcasted_iota(jnp.int32, (YC * Z, YC), 1)
    member = (chunk[:, 2 * width :] != 0).astype(BF16)
    local = nn(member, (lane == dest * Z + z).astype(BF16))
    ti = lax.broadcasted_iota(jnp.int32, (n, n), 0)
    tj = lax.broadcasted_iota(jnp.int32, (n, n), 1)
    earlier = ((ti // tokens == tj // tokens) & (tj < ti)).astype(BF16)
    before = nn(earlier, local.astype(BF16)).astype(jnp.int32)
    slot = before + (lax.broadcasted_iota(jnp.int32, before.shape, 0) // tokens) * CAP
    slot = jnp.where(local > 0, slot, -1)
    slots = n // tokens * CAP
    select = slot.T[:, None, :] == lax.broadcasted_iota(jnp.int32, (YC, slots, n), 1)
    sent = nn(select.astype(BF16).reshape(YC * slots, n), chunk).astype(BF16)
    got = lax.all_to_all(sent.reshape(YC, slots, -1), ("y", "core"), split_axis=0, concat_axis=0, tiled=True)
    return got.reshape(YC * slots, -1)


def body(grad_out, x_codes, x_scales, combine, expert_ids, w_gate, w_up, w_down):
    tokens, picks = expert_ids.shape
    width = grad_out.shape[1]
    share = w_gate.shape[1]
    experts = YC * Z
    z = lax.axis_index("z")
    yc = lax.axis_index("y") * CORE + lax.axis_index("core")
    mine = jnp.concatenate([w_gate[0], w_up[0], w_down[0]], axis=0)
    w_next, w_prev, far_top, far_bottom = gather_weights(mine)

    x = (
        (x_codes.astype(F32).reshape(tokens, width // BLOCK, BLOCK) * x_scales.astype(F32)[:, :, None])
        .reshape(tokens, width)
        .astype(BF16)
    )
    ranks = expert_ids // (Z * CORE) * (Z * CORE) + expert_ids % CORE * Z + expert_ids // CORE % Z
    names = (ranks[:, :, None] == jnp.arange(experts, dtype=jnp.int32)).astype(F32)
    dense = jnp.sum(names * combine.astype(F32)[:, :, None], axis=1)
    payload = jnp.concatenate([x, grad_out, dense.astype(BF16)], axis=1)
    groups = [list(range(r, Z, STRIDE)) for r in range(STRIDE)]
    seen = lax.all_gather(payload, "z", axis=0, tiled=True, axis_index_groups=groups)
    mid = seen.shape[0] // 2
    others = (
        shift(seen, "z", Z, -1),
        shift(seen, "z", Z, 1),
        shift(seen[:mid], "z", Z, -2),
        shift(seen[mid:], "z", Z, 2),
    )
    first = dispatch(seen, z, tokens, width)
    rows = jnp.concatenate([first, dispatch(jnp.concatenate(others, axis=0), z, tokens, width)], axis=0)

    own = (lax.broadcasted_iota(jnp.int32, (1, experts), 1) == yc * Z + z).astype(F32)
    comb = jnp.zeros((rows.shape[0], 128), F32)
    f_top, f_bottom, part_f, comb = expert_block(rows, own, (far_top, far_bottom), comb)
    n_top, n_bottom, part_n, comb = expert_block(rows, own, (w_next,), comb)
    p_top, p_bottom, part_p, comb = expert_block(rows, own, (w_prev,), comb)
    q = lax.broadcasted_iota(jnp.int32, (rows.shape[0], 1), 0)
    q_yc, q_z, q_cap = q // (Z * CAP), q // CAP % Z, q % CAP
    kind = (q_z - z + Z) % STRIDE
    per = Z // STRIDE * CAP
    place = q_z // STRIDE * CAP + q_cap
    at = jnp.where(
        kind == 0,
        q_yc * per + place,
        YC * per + q_yc * 3 * per + jnp.where(kind == 1, 0, jnp.where(kind == 3, per, 2 * per)) + place,
    )
    perm = (at == lax.broadcasted_iota(jnp.int32, (rows.shape[0], rows.shape[0]), 1)).astype(BF16)
    o_top, o_bottom, back = expert_block(rows, own, (mine,), comb, (part_f, part_n, part_p, perm))

    got_f_top, got_f_bottom = shift(f_top, "dp", DP, 1), shift(f_bottom, "dp", DP, -1)
    got_n_bottom, got_p_top = shift(n_bottom, "dp", DP, 1), shift(p_top, "dp", DP, -1)
    got_n_top = shift(add(n_top, got_f_top), "dp", DP, 1)
    got_p_bottom = shift(add(p_bottom, got_f_bottom), "dp", DP, -1)

    home = lax.all_to_all(
        back.reshape(experts, CAP, -1), ("y", "core", "z"), split_axis=0, concat_axis=0, tiled=True
    ).reshape(experts * CAP, -1)
    named = jnp.sum(names, axis=1)
    th = lax.broadcasted_iota(jnp.int32, (tokens, tokens), 0)
    tk = lax.broadcasted_iota(jnp.int32, (tokens, tokens), 1)
    prior = nn((tk < th).astype(BF16), named.astype(BF16)).astype(jnp.int32)
    owner = (named[:, :, None] > 0) & (prior[:, :, None] == lax.broadcasted_iota(jnp.int32, (1, 1, CAP), 2))
    owner = owner.reshape(tokens, experts * CAP).astype(BF16)
    grad_in = nn(owner, home[:, :width]).astype(BF16)
    comb_rows = home[:, width].astype(F32) + home[:, width + 1].astype(F32)
    of_expert = jnp.sum((owner.astype(F32) * comb_rows[None, :]).reshape(tokens, experts, CAP), axis=2)
    grad_combine = jnp.sum(names * of_expert[:, None, :], axis=2)

    rest = f_top.shape[0] - share
    top = lambda s: (o_top[s].astype(F32) + got_p_top[s].astype(F32) + got_n_top[s].astype(F32)).astype(BF16)
    bottom = lambda s: (
        o_bottom[s].astype(F32) + got_n_bottom[s].astype(F32) + got_p_bottom[s].astype(F32)
    ).astype(BF16)
    grad_up = jnp.concatenate([top(slice(share, None)), bottom(slice(0, rest))], axis=0)
    return grad_in, grad_combine, top(slice(0, share))[None], grad_up[None], bottom(slice(rest, None))[None]


def solution(mesh):
    fine = Mesh(mesh.devices.reshape(DP, Y, Z, CORE), ("dp", "y", "z", "core"))
    tok = P(("dp", "y", "z", "core"), None)
    wts = P(("y", "z", "core"), "dp", None)
    return jax.shard_map(
        body,
        mesh=fine,
        in_specs=(tok,) * 5 + (wts,) * 3,
        out_specs=(tok, tok, wts, wts, wts),
        check_vma=False,
    )
```

```python
import functools

import jax
import jax.numpy as jnp
from jax import lax
from jax.experimental import pallas as pl
from jax.experimental.pallas import tpu as pltpu
from jax.sharding import Mesh, PartitionSpec as P

BLOCK = 128
DP, Y, Z, CORE = 4, 4, 16, 2
STRIDE = 4
YC = Y * CORE
CAP = 2
VM = 28
SUM_FLOPS = 10**12
F32, BF16 = jnp.float32, jnp.bfloat16


def shift(a, axis, size, k):
    return lax.ppermute(a, axis, [(i, (i + k) % size) for i in range(size)])


def nt(a, b):
    return lax.dot_general(a, b, (((1,), (1,)), ((), ())), preferred_element_type=F32)


def tn(a, b):
    return lax.dot_general(a, b, (((0,), (0,)), ((), ())), preferred_element_type=F32)


def nn(a, b):
    return jnp.dot(a, b, preferred_element_type=F32)


def gather_weights(mine):
    half = mine.shape[0] // 2
    from_prev, from_next = shift(mine, "dp", DP, 1), shift(mine, "dp", DP, -1)
    top, bottom = shift(from_prev[:half], "dp", DP, 1), shift(from_next[half:], "dp", DP, -1)
    return (from_next,), (from_prev,), (top, bottom)


def sum_kernel(n_ref, from_far_top, p_ref, from_far_bottom, _, __, gate_ref, low_ref, high_ref, down_ref):
    step = pl.program_id(0)
    top = (n_ref[...].astype(F32) + from_far_top[...].astype(F32)).astype(BF16)
    bottom = (p_ref[...].astype(F32) + from_far_bottom[...].astype(F32)).astype(BF16)

    @pl.when(step < 2)
    def _():
        gate_ref[...] = top

    @pl.when(step == 2)
    def _():
        low_ref[...] = top

    @pl.when(step == 0)
    def _():
        high_ref[...] = bottom

    @pl.when(step > 0)
    def _():
        down_ref[...] = bottom


def forward_sums(n_top, from_far_top, p_bottom, from_far_bottom, *arrived):
    half, width = n_top.shape
    part = half // 3
    block = (part, width)
    walk = pl.BlockSpec(block, lambda i: (i, 0))
    one = pl.BlockSpec(block, lambda i: (0, 0))
    sds = jax.ShapeDtypeStruct
    return pl.pallas_call(
        sum_kernel,
        grid=(3,),
        in_specs=[walk] * 4 + [pl.BlockSpec(memory_space=pl.ANY)] * 2,
        out_specs=[
            pl.BlockSpec(block, lambda i: (jnp.minimum(i, 1), 0)),
            one,
            one,
            pl.BlockSpec(block, lambda i: (jnp.maximum(i - 1, 0), 0)),
        ],
        out_shape=[sds((k * part, width), BF16) for k in (2, 1, 1, 2)],
        compiler_params=pltpu.CompilerParams(vmem_limit_bytes=16 * 2**20),
        cost_estimate=pl.CostEstimate(flops=SUM_FLOPS, bytes_accessed=2**20, transcendentals=0),
    )(n_top, from_far_top, p_bottom, from_far_bottom, *arrived)


def block_kernel(last, count, *refs):
    rows, (own_ref, top_ref, bottom_ref, comb_ref), refs = refs[:count], refs[count : count + 4], refs[count + 4 :]
    if last:
        part_a, part_b, part_c, perm_ref, d_top, d_bottom, back_ref = refs
    else:
        d_top, d_bottom, part_ref, comb_out = refs
    width = top_ref.shape[1]
    half = top_ref.shape[0]
    share = 2 * half // 3
    rest = half - share
    take = lambda a, b: jnp.concatenate([r[:, a:b] for r in rows], axis=0)
    x = take(0, width)
    grad = take(width, 2 * width)
    weight = jnp.sum(take(2 * width, 2 * width + 128).astype(F32) * own_ref[...], axis=1, keepdims=True)
    w_gate = top_ref[:share]
    w_up = jnp.concatenate([top_ref[share:], bottom_ref[:rest]], axis=0)
    w_down = bottom_ref[rest:]
    gate = nt(x, w_gate)
    up = nt(x, w_up)
    back = nt(grad, w_down)
    sig = jax.nn.sigmoid(gate)
    act = gate * sig
    hidden = (act * up).astype(BF16)
    comb = comb_ref[...] + jnp.sum(back * hidden.astype(F32), axis=1, keepdims=True)
    gh = weight * back
    d_gate = (gh * up * sig * (1.0 + gate * (1.0 - sig))).astype(BF16)
    d_up = (gh * act).astype(BF16)
    scaled = (weight * grad.astype(F32)).astype(BF16)
    d_top[:share] = tn(d_gate, x).astype(BF16)
    d_up_w = tn(d_up, x).astype(BF16)
    d_top[share:] = d_up_w[:rest]
    d_bottom[:rest] = d_up_w[rest:]
    d_bottom[rest:] = tn(hidden, scaled).astype(BF16)
    part = (nn(d_gate, w_gate) + nn(d_up, w_up)).astype(BF16)
    if last:
        total = part.astype(F32) + part_a[...].astype(F32) + part_b[...].astype(F32) + part_c[...].astype(F32)
        perm = perm_ref[...]
        back_ref[:, :width] = nn(perm, total.astype(BF16)).astype(BF16)
        high = comb.astype(BF16)
        low = (comb - high.astype(F32)).astype(BF16)
        lane = lax.broadcasted_iota(jnp.int32, high.shape, 1)
        tail = jnp.where(lane == 0, high.astype(F32), jnp.where(lane == 1, low.astype(F32), 0.0))
        back_ref[:, width:] = nn(perm, tail.astype(BF16)).astype(BF16)
    else:
        part_ref[...] = part
        comb_out[...] = comb


def expert_block(rows, own, weights, comb, last=()):
    n = sum(r.shape[0] for r in rows)
    whole = lambda a: pl.BlockSpec(a.shape, lambda i: (0,) * len(a.shape))
    if len(weights) == 1:
        half, width = weights[0].shape[0] // 2, weights[0].shape[1]
        w_specs = [pl.BlockSpec((half, width), lambda i, k=k: (k, 0)) for k in range(2)]
        weights = weights * 2
    else:
        half, width = weights[0].shape
        w_specs = [whole(w) for w in weights]
    operands = (*rows, own, *weights, comb, *last)
    sds = jax.ShapeDtypeStruct
    out = [pltpu.HBM((half, width), BF16), pltpu.HBM((half, width), BF16)]
    out += [sds((n, width + 128), BF16)] if last else [sds((n, width), BF16), sds((n, 128), F32)]
    return pl.pallas_call(
        functools.partial(block_kernel, bool(last), len(rows)),
        grid=(1,),
        out_shape=out,
        in_specs=[*[whole(r) for r in rows], whole(own), *w_specs, whole(comb), *[whole(a) for a in last]],
        out_specs=[whole(o) for o in out],
        compiler_params=pltpu.CompilerParams(vmem_limit_bytes=VM * 2**20),
        cost_estimate=pl.CostEstimate(flops=2 * 8 * n * 256 * width, bytes_accessed=9 * 2**20, transcendentals=n * 192),
    )(*operands)


def dispatch(chunk, z, tokens, width):
    n = chunk.shape[0]
    lane = lax.broadcasted_iota(jnp.int32, (YC * Z, YC), 0)
    dest = lax.broadcasted_iota(jnp.int32, (YC * Z, YC), 1)
    member = (chunk[:, 2 * width :] != 0).astype(BF16)
    local = nn(member, (lane == dest * Z + z).astype(BF16))
    ti = lax.broadcasted_iota(jnp.int32, (n, n), 0)
    tj = lax.broadcasted_iota(jnp.int32, (n, n), 1)
    earlier = ((ti // tokens == tj // tokens) & (tj < ti)).astype(BF16)
    before = nn(earlier, local.astype(BF16)).astype(jnp.int32)
    slot = before + (lax.broadcasted_iota(jnp.int32, before.shape, 0) // tokens) * CAP
    slot = jnp.where(local > 0, slot, -1)
    slots = n // tokens * CAP
    select = slot.T[:, None, :] == lax.broadcasted_iota(jnp.int32, (YC, slots, n), 1)
    sent = nn(select.astype(BF16).reshape(YC * slots, n), chunk).astype(BF16)
    got = lax.all_to_all(sent.reshape(YC, slots, -1), ("y", "core"), split_axis=0, concat_axis=0, tiled=True)
    return got.reshape(YC * slots, -1)


def body(grad_out, x_codes, x_scales, combine, expert_ids, w_gate, w_up, w_down):
    tokens, picks = expert_ids.shape
    width = grad_out.shape[1]
    share = w_gate.shape[1]
    experts = YC * Z
    z = lax.axis_index("z")
    yc = lax.axis_index("y") * CORE + lax.axis_index("core")
    mine = jnp.concatenate([w_gate[0], w_up[0], w_down[0]], axis=0)
    w_next, w_prev, w_far = gather_weights(mine)

    x = (
        (x_codes.astype(F32).reshape(tokens, width // BLOCK, BLOCK) * x_scales.astype(F32)[:, :, None])
        .reshape(tokens, width)
        .astype(BF16)
    )
    ranks = expert_ids // (Z * CORE) * (Z * CORE) + expert_ids % CORE * Z + expert_ids // CORE % Z
    names = (ranks[:, :, None] == jnp.arange(experts, dtype=jnp.int32)).astype(F32)
    dense = jnp.sum(names * combine.astype(F32)[:, :, None], axis=1)
    payload = jnp.concatenate([x, grad_out, dense.astype(BF16)], axis=1)
    groups = [list(range(r, Z, STRIDE)) for r in range(STRIDE)]
    copies = jnp.broadcast_to(payload, (Z // STRIDE, *payload.shape))
    seen = lax.all_to_all(copies, "z", split_axis=0, concat_axis=0, axis_index_groups=groups, tiled=True)
    seen = seen.reshape(-1, payload.shape[1])
    mid = seen.shape[0] // 2
    ahead, behind = shift(seen, "z", Z, -1), shift(seen, "z", Z, 1)
    across = jnp.concatenate([shift(seen[:mid], "z", Z, -2), shift(seen[mid:], "z", Z, 2)], axis=0)
    rows = tuple(dispatch(c, z, tokens, width) for c in (seen, ahead, behind, across))

    own = (lax.broadcasted_iota(jnp.int32, (1, experts), 1) == yc * Z + z).astype(F32)
    count = YC * Z * CAP
    comb = jnp.zeros((count, 128), F32)
    f_top, f_bottom, part_f, comb = expert_block(rows, own, w_far, comb)
    n_top, n_bottom, part_n, comb = expert_block(rows, own, w_next, comb)
    p_top, p_bottom, part_p, comb = expert_block(rows, own, w_prev, comb)
    q = lax.broadcasted_iota(jnp.int32, (count, 1), 0)
    q_yc, q_cap = q // (Z * CAP), q % CAP
    q_z = q // CAP % Z
    kind, index = (q_z - z + Z) % STRIDE, q_z // STRIDE
    base = jnp.where(kind == 0, 0, jnp.where(kind == 1, 1, jnp.where(kind == 3, 2, 3)))
    at = base * (count // STRIDE) + q_yc * (STRIDE * CAP) + index * CAP + q_cap
    perm = (at == lax.broadcasted_iota(jnp.int32, (count, count), 1)).astype(BF16)
    o_top, o_bottom, back = expert_block(rows, own, (mine,), comb, (part_f, part_n, part_p, perm))

    got_f_top, got_f_bottom = shift(f_top, "dp", DP, 1), shift(f_bottom, "dp", DP, -1)
    got_n_bottom, got_p_top = shift(n_bottom, "dp", DP, 1), shift(p_top, "dp", DP, -1)
    rest = f_top.shape[0] - share
    gate, low, high, down = forward_sums(n_top, got_f_top, p_bottom, got_f_bottom, got_n_bottom, got_p_top)
    got_gate, got_down = shift(gate, "dp", DP, 1), shift(down, "dp", DP, -1)
    got_low, got_high = shift(low, "dp", DP, 1), shift(high, "dp", DP, -1)

    home = lax.all_to_all(
        back.reshape(experts, CAP, -1), ("y", "core", "z"), split_axis=0, concat_axis=0, tiled=True
    ).reshape(experts * CAP, -1)
    named = jnp.sum(names, axis=1)
    th = lax.broadcasted_iota(jnp.int32, (tokens, tokens), 0)
    tk = lax.broadcasted_iota(jnp.int32, (tokens, tokens), 1)
    prior = nn((tk < th).astype(BF16), named.astype(BF16)).astype(jnp.int32)
    owner = (named[:, :, None] > 0) & (prior[:, :, None] == lax.broadcasted_iota(jnp.int32, (1, 1, CAP), 2))
    owner = owner.reshape(tokens, experts * CAP).astype(BF16)
    grad_in = nn(owner, home[:, :width]).astype(BF16)
    comb_rows = home[:, width].astype(F32) + home[:, width + 1].astype(F32)
    of_expert = jnp.sum((owner.astype(F32) * comb_rows[None, :]).reshape(tokens, experts, CAP), axis=2)
    grad_combine = jnp.sum(names * of_expert[:, None, :], axis=2)

    got_low, got_high, grad_in, grad_combine = lax.optimization_barrier((got_low, got_high, grad_in, grad_combine))
    three = lambda a, b, c: (a.astype(F32) + b.astype(F32) + c.astype(F32)).astype(BF16)
    grad_gate = three(o_top[:share], got_p_top[:share], got_gate)
    grad_down = three(o_bottom[rest:], got_n_bottom[rest:], got_down)
    low = three(o_top[share:], got_p_top[share:], got_low)
    high = three(o_bottom[:rest], got_n_bottom[:rest], got_high)
    grad_up = jnp.concatenate([low, high], axis=0)
    return grad_in, grad_combine, grad_gate[None], grad_up[None], grad_down[None]


def solution(mesh):
    fine = Mesh(mesh.devices.reshape(DP, Y, Z, CORE), ("dp", "y", "z", "core"))
    tok = P(("dp", "y", "z", "core"), None)
    wts = P(("y", "z", "core"), "dp", None)
    return jax.shard_map(
        body,
        mesh=fine,
        in_specs=(tok,) * 5 + (wts,) * 3,
        out_specs=(tok, tok, wts, wts, wts),
        check_vma=False,
    )
```

```python
import functools

import jax
import jax.numpy as jnp
from jax import lax
from jax.experimental import pallas as pl
from jax.experimental.pallas import tpu as pltpu
from jax.sharding import Mesh, PartitionSpec as P

BLOCK = 128
DP, Y, Z, CORE = 4, 4, 16, 2
YC = Y * CORE
CAP = 2
LANES = 128
MIB = 2**20
LONG = 10**12
F32, BF16, I32 = jnp.float32, jnp.bfloat16, jnp.int32
sds = jax.ShapeDtypeStruct


def shift(a, axis, size, k):
    return lax.ppermute(a, axis, [(i, (i + k) % size) for i in range(size)])


def nt(a, b):
    return lax.dot_general(a, b, (((1,), (1,)), ((), ())), preferred_element_type=F32)


def tn(a, b):
    return lax.dot_general(a, b, (((0,), (0,)), ((), ())), preferred_element_type=F32)


def nn(a, b):
    return jnp.dot(a, b, preferred_element_type=F32)


def iota(shape, dim):
    return lax.broadcasted_iota(I32, shape, dim)


def whole(a):
    return pl.BlockSpec(a.shape, lambda *_: (0,) * len(a.shape))


def call(kernel, operands, out_shape, in_specs=None, out_specs=None, grid=(1,), vmem=24, cost=1, scratch=()):
    return pl.pallas_call(
        kernel,
        grid=grid,
        out_shape=out_shape,
        in_specs=in_specs or [whole(a) for a in operands],
        out_specs=out_specs or [whole(o) for o in out_shape],
        scratch_shapes=scratch,
        compiler_params=pltpu.CompilerParams(vmem_limit_bytes=vmem * MIB),
        cost_estimate=pl.CostEstimate(flops=cost, bytes_accessed=MIB, transcendentals=0),
    )(*operands)


def rank_of(ids):
    return ids // (Z * CORE) * (Z * CORE) + ids % CORE * Z + ids // CORE % Z


def payload_kernel(codes_ref, scales_ref, grad_ref, combine_ref, rank_ref, out_ref):
    tokens, width = codes_ref.shape
    count = scales_ref.shape[1]
    spread = (iota((count, width), 1) // BLOCK == iota((count, width), 0)).astype(BF16)
    scale = nn(scales_ref[...], spread)
    out_ref[:, :width] = (codes_ref[...].astype(F32) * scale).astype(BF16)
    out_ref[:, width : 2 * width] = grad_ref[...]
    lane = iota((tokens, LANES), 1)
    dense = jnp.zeros((tokens, LANES), F32)
    for k in range(rank_ref.shape[1]):
        dense += jnp.where(rank_ref[:, k : k + 1] == lane, combine_ref[:, k : k + 1], 0.0)
    out_ref[:, 2 * width :] = dense.astype(BF16)


def dispatch_kernel(tokens, pick_ref, *refs):
    *pieces, out_ref = refs
    chunk = jnp.concatenate([r[...] for r in pieces], axis=0)
    n = chunk.shape[0]
    member = (chunk[:, -LANES:].astype(F32) != 0).astype(BF16)
    local = nt(pick_ref[...], member)
    ti, tj = iota((n, n), 0), iota((n, n), 1)
    earlier = ((ti // tokens == tj // tokens) & (ti < tj)).astype(BF16)
    slot = nn(local.astype(BF16), earlier).astype(I32) + iota(local.shape, 1) // tokens * CAP
    slot = jnp.where(local > 0, slot, -1)
    slots = n // tokens * CAP
    row = iota((slots, n), 0)
    select = jnp.concatenate([slot[d : d + 1] == row for d in range(YC)], axis=0).astype(F32).astype(BF16)
    out_ref[...] = nn(select, chunk).astype(BF16)


def dispatch(pieces, pick, tokens, cost=1):
    n, width = sum(p.shape[0] for p in pieces), pieces[0].shape[1]
    slots = n // tokens * CAP
    (sent,) = call(functools.partial(dispatch_kernel, tokens), (pick, *pieces), [sds((YC * slots, width), BF16)], vmem=16, cost=cost)
    got = lax.all_to_all(sent.reshape(YC, slots, width), ("y", "core"), split_axis=0, concat_axis=0, tiled=True)
    return got.reshape(YC * slots, width)


def load_rows(refs, own_ref, width):
    take = lambda a, b: jnp.concatenate([r[:, a:b] for r in refs], axis=0)
    weight = jnp.sum(take(2 * width, 2 * width + LANES).astype(F32) * own_ref[...], axis=1, keepdims=True)
    return take(0, width), take(width, 2 * width), weight


def forward(x, grad, weight, w_gate, w_up, w_down):
    gate, up, back = nt(x, w_gate), nt(x, w_up), nt(grad, w_down)
    sig = jax.nn.sigmoid(gate)
    act = gate * sig
    hidden = (act * up).astype(BF16)
    comb = jnp.sum(back * hidden.astype(F32), axis=1, keepdims=True)
    gh = weight * back
    d_gate = (gh * up * sig * (1.0 + gate * (1.0 - sig))).astype(BF16)
    d_up = (gh * act).astype(BF16)
    part = (nn(d_gate, w_gate) + nn(d_up, w_up)).astype(BF16)
    return hidden, d_gate, d_up, part, comb


def store_grads(d_top, d_bottom, hidden, d_gate, d_up, x, scaled):
    share = hidden.shape[1]
    rest = d_top.shape[0] - share
    d_top[:share] = tn(d_gate, x).astype(BF16)
    d_up_w = tn(d_up, x).astype(BF16)
    d_top[share:] = d_up_w[:rest]
    d_bottom[:rest] = d_up_w[rest:]
    d_bottom[rest:] = tn(hidden, scaled).astype(BF16)


def scaled_rows(weight, grad):
    return (weight * grad.astype(F32)).astype(BF16)


def far_kernel(count, *refs):
    rows, (own_ref, top_ref, bottom_ref, d_top, d_bottom, part_ref, comb_ref) = refs[:count], refs[count:]
    half, width = top_ref.shape
    share = 2 * half // 3
    x, grad, weight = load_rows(rows, own_ref, width)
    w_up = jnp.concatenate([top_ref[share:], bottom_ref[: half - share]], axis=0)
    hidden, d_gate, d_up, part, comb = forward(x, grad, weight, top_ref[:share], w_up, bottom_ref[half - share :])
    store_grads(d_top, d_bottom, hidden, d_gate, d_up, x, scaled_rows(weight, grad))
    part_ref[...] = part
    comb_ref[...] = jnp.broadcast_to(comb, comb_ref.shape)


def near_kernel(count, *refs):
    rows, refs = refs[:count], refs[count:]
    own_ref, part_ref, comb_ref, perm_ref, *refs = refs
    weights, (back_ref, acts_ref), grads, bufs, sems = refs[:3], refs[3:5], refs[5:9], refs[9], refs[10]
    copies = [pltpu.make_async_copy(w, bufs.at[k], sems.at[k]) for k, w in enumerate(weights)]
    for c in copies:
        c.start()
    width = bufs.shape[2]
    share = bufs.shape[1] // 3
    x, grad, weight = load_rows(rows, own_ref, width)
    scaled = scaled_rows(weight, grad)
    total, comb = part_ref[...].astype(F32), comb_ref[...]
    for k, c in enumerate(copies):
        c.wait()
        hidden, d_gate, d_up, part, term = forward(
            x, grad, weight, bufs[k, :share], bufs[k, share : 2 * share], bufs[k, 2 * share :]
        )
        if k < 2:
            store_grads(grads[2 * k], grads[2 * k + 1], hidden, d_gate, d_up, x, scaled)
        else:
            acts_ref[0], acts_ref[1], acts_ref[2] = hidden, d_gate, d_up
        total += part.astype(F32)
        comb += term
    perm = perm_ref[...]
    back_ref[:, :width] = nn(perm, total.astype(BF16)).astype(BF16)
    high = comb.astype(BF16)
    low = (comb - high.astype(F32)).astype(BF16)
    lane = iota(high.shape, 1)
    tail = jnp.where(lane == 0, high.astype(F32), jnp.where(lane == 1, low.astype(F32), 0.0))
    back_ref[:, width:] = nn(perm, tail.astype(BF16)).astype(BF16)


def own_kernel(count, *refs):
    rows, (own_ref, acts_ref, d_top, d_bottom) = refs[:count], refs[count:]
    x, grad, weight = load_rows(rows, own_ref, d_top.shape[1])
    store_grads(d_top, d_bottom, acts_ref[0], acts_ref[1], acts_ref[2], x, scaled_rows(weight, grad))


def sum_kernel(n_ref, from_far_top, p_ref, from_far_bottom, gate_ref, low_ref, high_ref, down_ref):
    step = pl.program_id(0)
    top = (n_ref[...].astype(F32) + from_far_top[...].astype(F32)).astype(BF16)
    bottom = (p_ref[...].astype(F32) + from_far_bottom[...].astype(F32)).astype(BF16)

    @pl.when(step < 2)
    def _():
        gate_ref[...] = top

    @pl.when(step == 2)
    def _():
        low_ref[...] = top

    @pl.when(step == 0)
    def _():
        high_ref[...] = bottom

    @pl.when(step > 0)
    def _():
        down_ref[...] = bottom


def forward_sums(n_top, from_far_top, p_bottom, from_far_bottom):
    half, width = n_top.shape
    part = half // 3
    block = (part, width)
    walk = pl.BlockSpec(block, lambda i: (i, 0))
    one = pl.BlockSpec(block, lambda i: (0, 0))
    return call(
        sum_kernel,
        (n_top, from_far_top, p_bottom, from_far_bottom),
        [sds((k * part, width), BF16) for k in (2, 1, 1, 2)],
        in_specs=[walk] * 4,
        out_specs=[
            pl.BlockSpec(block, lambda i: (jnp.minimum(i, 1), 0)),
            one,
            one,
            pl.BlockSpec(block, lambda i: (jnp.maximum(i - 1, 0), 0)),
        ],
        grid=(3,),
        vmem=16,
        cost=LONG,
    )


def body(grad_out, x_codes, x_scales, combine, expert_ids, w_gate, w_up, w_down):
    tokens, picks = expert_ids.shape
    width = grad_out.shape[1]
    share = w_gate.shape[1]
    half = 3 * share // 2
    experts = YC * Z
    count = experts * CAP
    z = lax.axis_index("z")
    yc = lax.axis_index("y") * CORE + lax.axis_index("core")
    rank = rank_of(expert_ids)
    (payload,) = call(
        payload_kernel,
        (x_codes, x_scales, grad_out, combine.astype(F32), rank),
        [sds((tokens, 2 * width + LANES), BF16)],
        vmem=8,
    )
    groups = [list(range(r, Z, 2)) for r in range(2)]
    seen = lax.all_gather(payload, "z", axis=0, tiled=True, axis_index_groups=groups)

    mine = jnp.concatenate([w_gate[0], w_up[0], w_down[0]], axis=0)
    from_prev, from_next = shift(mine, "dp", DP, 1), shift(mine, "dp", DP, -1)
    far_top, far_bottom = shift(from_prev[:half], "dp", DP, 1), shift(from_next[half:], "dp", DP, -1)

    mid = seen.shape[0] // 2
    other = shift(seen[:mid], "z", Z, -1), shift(seen[mid:], "z", Z, 1)
    dest = iota((2 * YC, experts), 0)
    pick = ((dest < YC) & (iota((2 * YC, experts), 1) == dest * Z + z)).astype(BF16)
    rows = dispatch((seen,), pick, tokens), dispatch(other, pick, tokens, LONG)

    own = (iota((1, experts), 1) == yc * Z + z).astype(F32)
    grads = [pltpu.HBM((half, width), BF16)] * 2
    f_top, f_bottom, part, comb = call(
        functools.partial(far_kernel, len(rows)),
        (*rows, own, far_top, far_bottom),
        [*grads, sds((count, width), BF16), sds((count, LANES), F32)],
        vmem=28,
    )
    got_f_top, got_f_bottom = shift(f_top, "dp", DP, 1), shift(f_bottom, "dp", DP, -1)

    q = iota((count, 1), 0)
    q_z = q // CAP % Z
    at = (q_z + z) % 2 * (count // 2) + q // (Z * CAP) * Z + q_z // 2 * CAP + q % CAP
    perm = (at == iota((count, count), 1)).astype(BF16)
    near = (*rows, own, part, comb, perm)
    back, acts, n_top, n_bottom, p_top, p_bottom = call(
        functools.partial(near_kernel, len(rows)),
        (*near, from_next, from_prev, mine),
        [sds((count, width + LANES), BF16), sds((3, count, share), BF16), *grads, *grads],
        in_specs=[*[whole(a) for a in near], *[pl.BlockSpec(memory_space=pl.ANY)] * 3],
        scratch=[pltpu.VMEM((3, *mine.shape), BF16), pltpu.SemaphoreType.DMA((3,))],
        vmem=44,
    )
    home = lax.all_to_all(
        back.reshape(experts, CAP, -1), ("y", "core", "z"), split_axis=0, concat_axis=0, tiled=True
    ).reshape(count, -1)

    o_top, o_bottom = call(functools.partial(own_kernel, len(rows)), (*rows, own, acts), grads, vmem=28)
    got_n_bottom, got_p_top = shift(n_bottom, "dp", DP, 1), shift(p_top, "dp", DP, -1)
    sums = forward_sums(n_top, got_f_top, p_bottom, got_f_bottom)
    (gate, low, high, down), got_n_bottom, got_p_top = lax.optimization_barrier((sums, got_n_bottom, got_p_top))
    got_gate, got_down = shift(gate, "dp", DP, 1), shift(down, "dp", DP, -1)
    got_low, got_high = shift(low, "dp", DP, 1), shift(high, "dp", DP, -1)

    names = (rank[:, :, None] == jnp.arange(experts, dtype=I32)).astype(F32)
    named = jnp.sum(names, axis=1)
    th, tk = iota((tokens, tokens), 0), iota((tokens, tokens), 1)
    prior = nn((tk < th).astype(BF16), named.astype(BF16)).astype(I32)
    owner = (named[:, :, None] > 0) & (prior[:, :, None] == iota((1, 1, CAP), 2))
    owner = owner.reshape(tokens, count).astype(BF16)
    grad_in = nn(owner, home[:, :width]).astype(BF16)
    comb_rows = home[:, width].astype(F32) + home[:, width + 1].astype(F32)
    of_expert = jnp.sum((owner.astype(F32) * comb_rows[None, :]).reshape(tokens, experts, CAP), axis=2)
    grad_combine = jnp.sum(names * of_expert[:, None, :], axis=2)

    rest = half - share
    got_low, got_high, grad_in, grad_combine = lax.optimization_barrier((got_low, got_high, grad_in, grad_combine))
    three = lambda a, b, c: (a.astype(F32) + b.astype(F32) + c.astype(F32)).astype(BF16)
    grad_gate = three(o_top[:share], got_p_top[:share], got_gate)
    grad_down = three(o_bottom[rest:], got_n_bottom[rest:], got_down)
    low = three(o_top[share:], got_p_top[share:], got_low)
    high = three(o_bottom[:rest], got_n_bottom[:rest], got_high)
    grad_up = jnp.concatenate([low, high], axis=0)
    return grad_in, grad_combine, grad_gate[None], grad_up[None], grad_down[None]


def solution(mesh):
    fine = Mesh(mesh.devices.reshape(DP, Y, Z, CORE), ("dp", "y", "z", "core"))
    tok = P(("dp", "y", "z", "core"), None)
    wts = P(("y", "z", "core"), "dp", None)
    return jax.shard_map(
        body,
        mesh=fine,
        in_specs=(tok,) * 5 + (wts,) * 3,
        out_specs=(tok, tok, wts, wts, wts),
        check_vma=False,
    )
```

```python
import functools

import jax
import jax.numpy as jnp
from jax import lax
from jax.experimental import pallas as pl
from jax.experimental.pallas import tpu as pltpu
from jax.sharding import Mesh, PartitionSpec as P

BLOCK = 128
DP, Y, Z, CORE = 4, 4, 16, 2
YC = Y * CORE
CAP = 2
LANES = 128
MIB = 2**20
LONG = 10**12
MEDIUM = 3 * 10**10
F32, BF16, I32 = jnp.float32, jnp.bfloat16, jnp.int32
sds = jax.ShapeDtypeStruct


def shift(a, axis, size, k):
    return lax.ppermute(a, axis, [(i, (i + k) % size) for i in range(size)])


def nt(a, b):
    return lax.dot_general(a, b, (((1,), (1,)), ((), ())), preferred_element_type=F32)


def tn(a, b):
    return lax.dot_general(a, b, (((0,), (0,)), ((), ())), preferred_element_type=F32)


def nn(a, b):
    return jnp.dot(a, b, preferred_element_type=F32)


def iota(shape, dim):
    return lax.broadcasted_iota(I32, shape, dim)


def whole(a):
    return pl.BlockSpec(a.shape, lambda *_: (0,) * len(a.shape))


def call(kernel, operands, out_shape, in_specs=None, out_specs=None, grid=(1,), vmem=24, cost=1, scratch=()):
    return pl.pallas_call(
        kernel,
        grid=grid,
        out_shape=out_shape,
        in_specs=in_specs or [whole(a) for a in operands],
        out_specs=out_specs or [whole(o) for o in out_shape],
        scratch_shapes=scratch,
        compiler_params=pltpu.CompilerParams(vmem_limit_bytes=vmem * MIB),
        cost_estimate=pl.CostEstimate(flops=cost, bytes_accessed=MIB, transcendentals=0),
    )(*operands)


def move_kernel(plan, count, *refs):
    sources, targets, sems = refs[:count], refs[count:-1], refs[-1]
    copies = [
        pltpu.make_async_copy(sources[i].at[pl.ds(a, n)], targets[o].at[pl.ds(b, n)], sems.at[k])
        for k, (i, a, n, o, b) in enumerate(plan)
    ]
    for c in copies:
        c.start()
    for c in copies:
        c.wait()


def move(arrays, plan, out_rows):
    width = arrays[0].shape[1]
    return pl.pallas_call(
        functools.partial(move_kernel, plan, len(arrays)),
        out_shape=[pltpu.HBM((n, width), BF16) for n in out_rows],
        in_specs=[pl.BlockSpec(memory_space=pl.ANY)] * len(arrays),
        out_specs=[pl.BlockSpec(memory_space=pl.ANY)] * len(out_rows),
        scratch_shapes=[pltpu.SemaphoreType.DMA((len(plan),))],
        compiler_params=pltpu.CompilerParams(vmem_limit_bytes=2 * MIB),
    )(*arrays)


def rank_of(ids):
    return ids // (Z * CORE) * (Z * CORE) + ids % CORE * Z + ids // CORE % Z


def payload_kernel(codes_ref, scales_ref, grad_ref, combine_ref, rank_ref, out_ref):
    tokens, width = codes_ref.shape
    count = scales_ref.shape[1]
    spread = (iota((count, width), 1) // BLOCK == iota((count, width), 0)).astype(BF16)
    scale = nn(scales_ref[...], spread)
    out_ref[:, :width] = (codes_ref[...].astype(F32) * scale).astype(BF16)
    out_ref[:, width : 2 * width] = grad_ref[...]
    lane = iota((tokens, LANES), 1)
    dense = jnp.zeros((tokens, LANES), F32)
    for k in range(rank_ref.shape[1]):
        dense += jnp.where(rank_ref[:, k : k + 1] == lane, combine_ref[:, k : k + 1], 0.0)
    out_ref[:, 2 * width :] = dense.astype(BF16)


def dispatch_kernel(tokens, pick_ref, *refs):
    *pieces, out_ref = refs
    chunk = jnp.concatenate([r[...] for r in pieces], axis=0)
    n = chunk.shape[0]
    member = (chunk[:, -LANES:].astype(F32) != 0).astype(BF16)
    local = nt(pick_ref[...], member)
    ti, tj = iota((n, n), 0), iota((n, n), 1)
    earlier = ((ti // tokens == tj // tokens) & (ti < tj)).astype(BF16)
    slot = nn(local.astype(BF16), earlier).astype(I32) + iota(local.shape, 1) // tokens * CAP
    slot = jnp.where(local > 0, slot, -1)
    slots = n // tokens * CAP
    row = iota((slots, n), 0)
    select = jnp.concatenate([slot[d : d + 1] == row for d in range(YC)], axis=0).astype(F32).astype(BF16)
    out_ref[...] = nn(select, chunk).astype(BF16)


def dispatch(pieces, pick, tokens, cost=1):
    n, width = sum(p.shape[0] for p in pieces), pieces[0].shape[1]
    slots = n // tokens * CAP
    (sent,) = call(functools.partial(dispatch_kernel, tokens), (pick, *pieces), [sds((YC * slots, width), BF16)], vmem=16, cost=cost)
    got = lax.all_to_all(sent.reshape(YC, slots, width), ("y", "core"), split_axis=0, concat_axis=0, tiled=True)
    return got.reshape(YC * slots, width)


def forward_kernel(count, own_ref, perm_ref, *refs):
    rows, refs = refs[:count], refs[count:]
    weights, (back_ref, *acts_refs, bufs, sems) = refs[:5], refs[5:]
    half = bufs.shape[1] // 2
    copies = [[pltpu.make_async_copy(weights[k], bufs.at[k], sems.at[k])] for k in range(3)]
    copies.append(
        [pltpu.make_async_copy(weights[3 + k], bufs.at[3, pl.ds(k * half, half)], sems.at[3 + k]) for k in range(2)]
    )
    for c in sum(copies, []):
        c.start()
    width = bufs.shape[2]
    share = bufs.shape[1] // 3
    take = lambda a, b: jnp.concatenate([r[:, a:b] for r in rows], axis=0)
    x, grad = take(0, width), take(width, 2 * width)
    n = x.shape[0]
    weight = nt(own_ref[...], take(2 * width, 2 * width + LANES))[:1]
    total, comb = jnp.zeros((n, width), F32), jnp.zeros((1, n), F32)
    for k in range(4):
        for c in copies[k]:
            c.wait()
        both = nt(bufs[k, : 2 * share], x)
        back = nt(bufs[k, 2 * share :], grad)
        gate, up = both[:share], both[share:]
        sig = jax.nn.sigmoid(gate)
        act = gate * sig
        hidden = (act * up).astype(BF16)
        comb += jnp.sum(back * hidden.astype(F32), axis=0, keepdims=True)
        gh = weight * back
        d_gate = gh * up * sig * (1.0 + gate * (1.0 - sig))
        d_both = jnp.concatenate([d_gate, gh * act], axis=0).astype(BF16)
        acts_refs[k][: 2 * share] = d_both
        acts_refs[k][2 * share :] = hidden
        total += tn(d_both, bufs[k, : 2 * share]).astype(BF16).astype(F32)
    perm = perm_ref[...]
    back_ref[:, :width] = nn(perm, total.astype(BF16)).astype(BF16)
    high = comb.astype(BF16).astype(F32)
    line = iota((LANES, n), 0)
    tail = jnp.where(line == 0, high, jnp.where(line == 1, comb - high, 0.0)).astype(BF16)
    back_ref[:, width:] = nt(perm, tail).astype(BF16)


def grads_kernel(planes_ref, own_ref, *refs):
    parts, chunks, (gate_ref, up_ref, down_ref, acts_ref) = refs[:DP], refs[DP:-4], refs[-4:]
    share = gate_ref.shape[0]
    count = len(chunks) // 3
    part = parts[0].shape[1] // count

    @pl.when(pl.program_id(0) == 0)
    def _():
        for k in range(DP):
            for c in range(count):
                at = pl.multiple_of((c * DP + planes_ref[k]) * part, part)
                acts_ref[:, pl.ds(at, part)] = parts[k][:, c * part : (c + 1) * part]

    both, down = 0.0, 0.0
    for c in range(count):
        x_ref, grad_ref, tail_ref = chunks[3 * c : 3 * c + 3]
        at = slice(c * DP * part, (c + 1) * DP * part)
        weight = jnp.sum(tail_ref[...].astype(F32) * own_ref[...], axis=1, keepdims=True)
        scaled = (weight * grad_ref[...].astype(F32)).astype(BF16)
        both += nn(acts_ref[: 2 * share, at], x_ref[...])
        down += nn(acts_ref[2 * share :, at], scaled)
    gate_ref[...] = both[:share].astype(BF16)
    up_ref[...] = both[share:].astype(BF16)
    down_ref[...] = down.astype(BF16)


def weight_grads(planes, own, acts, chunks, share, width, tile=512):
    chunks = [pltpu.with_memory_space_constraint(c, pltpu.HBM) for c in chunks]
    operands = [planes, own, *acts]
    specs = [pl.BlockSpec(memory_space=pltpu.SMEM), whole(own), *[whole(a) for a in acts]]
    for c in chunks:
        n = c.shape[0]
        operands += [c] * 3
        specs += [
            pl.BlockSpec((n, tile), lambda j: (0, j)),
            pl.BlockSpec((n, tile), lambda j: (0, width // tile + j)),
            pl.BlockSpec((n, LANES), lambda j: (0, 2 * width // LANES)),
        ]
    return call(
        grads_kernel,
        operands,
        [sds((share, width), BF16)] * 3,
        in_specs=specs,
        out_specs=[pl.BlockSpec((share, tile), lambda j: (0, j))] * 3,
        grid=(width // tile,),
        scratch=[pltpu.VMEM((3 * share, DP * acts[0].shape[1]), BF16)],
        vmem=28,
    )


def home_kernel(home_ref, rank_ref, grad_ref, comb_ref):
    tokens, picks = rank_ref.shape
    width = grad_ref.shape[1]
    count = home_ref.shape[0]
    experts = count // CAP
    lane = iota((tokens, experts), 1)
    named = jnp.zeros((tokens, experts), F32)
    for k in range(picks):
        named += (rank_ref[:, k : k + 1] == lane).astype(F32)
    prior = nn((iota((tokens, tokens), 1) < iota((tokens, tokens), 0)).astype(BF16), named.astype(BF16))
    spread = (iota((experts, count), 1) // CAP == iota((experts, count), 0)).astype(BF16)
    slot = iota((tokens, count), 1)
    here = nn(named.astype(BF16), spread) > 0
    owner = (here & (nn(prior.astype(BF16), spread).astype(I32) == slot % CAP)).astype(F32)
    grad_ref[...] = nn(owner.astype(BF16), home_ref[:, :width]).astype(BF16)
    pair = (iota((tokens, LANES), 1) < 2).astype(BF16)
    value = owner * nt(pair, home_ref[:, width:])
    for k in range(picks):
        mine = jnp.where(rank_ref[:, k : k + 1] == slot // CAP, value, 0.0)
        comb_ref[:, k : k + 1] = jnp.sum(mine, axis=1, keepdims=True)


def body(grad_out, x_codes, x_scales, combine, expert_ids, w_gate, w_up, w_down):
    tokens, picks = expert_ids.shape
    width = grad_out.shape[1]
    share = w_gate.shape[1]
    experts = YC * Z
    count = experts * CAP
    z = lax.axis_index("z")
    yc = lax.axis_index("y") * CORE + lax.axis_index("core")
    rank = rank_of(expert_ids)
    (payload,) = call(
        payload_kernel,
        (x_codes, x_scales, grad_out, combine.astype(F32), rank),
        [sds((tokens, 2 * width + LANES), BF16)],
        vmem=8,
    )
    groups = [list(range(r, Z, 2)) for r in range(2)]
    seen = lax.all_gather(payload, "z", axis=0, tiled=True, axis_index_groups=groups)

    half = 3 * share // 2
    plan = [(k, 0, share, 0, k * share) for k in range(3)]
    (mine,) = move((w_gate[0], w_up[0], w_down[0]), plan, [3 * share])
    from_prev, from_next = shift(mine, "dp", DP, 1), shift(mine, "dp", DP, -1)
    top, bottom = move((from_prev, from_next), [(0, 0, half, 0, 0), (1, half, half, 1, 0)], [half] * 2)
    far = shift(top, "dp", DP, 1), shift(bottom, "dp", DP, -1)

    mid = seen.shape[0] // 2
    low, high = move((seen,), [(0, 0, mid, 0, 0), (0, mid, mid, 1, 0)], [mid] * 2)
    other = shift(low, "z", Z, -1), shift(high, "z", Z, 1)
    dest = iota((2 * YC, experts), 0)
    pick = ((dest < YC) & (iota((2 * YC, experts), 1) == dest * Z + z)).astype(BF16)
    rows = dispatch((seen,), pick, tokens), dispatch(other, pick, tokens, LONG)
    planes = [lax.all_gather(r, "dp", axis=0, tiled=True) for r in rows]

    own = (iota((16, experts), 1) == yc * Z + z).astype(F32)
    q = iota((count, 1), 0)
    q_z = q // CAP % Z
    at = (q_z + z) % 2 * (count // 2) + q // (Z * CAP) * Z + q_z // 2 * CAP + q % CAP
    perm = (at == iota((count, count), 1)).astype(BF16)
    weights = (mine, from_next, from_prev, *far)
    small = (own.astype(BF16), perm, *rows)
    back, a_own, a_next, a_prev, a_far = call(
        functools.partial(forward_kernel, len(rows)),
        (*small, *weights),
        [sds((count, width + LANES), BF16), *[sds((3 * share, count), BF16)] * DP],
        in_specs=[*[whole(a) for a in small], *[pl.BlockSpec(memory_space=pl.ANY)] * 5],
        scratch=[pltpu.VMEM((DP, 3 * share, width), BF16), pltpu.SemaphoreType.DMA((5,))],
        vmem=36,
        cost=MEDIUM,
    )
    home = lax.all_to_all(
        back.reshape(experts, CAP, -1), ("y", "core", "z"), split_axis=0, concat_axis=0, tiled=True
    ).reshape(count, -1)
    acts = a_own, shift(a_next, "dp", DP, 1), shift(a_prev, "dp", DP, -1), shift(a_far, "dp", DP, 2)
    origins = (lax.axis_index("dp") + jnp.array([0, 3, 1, 2], I32)) % DP
    grad_in, grad_combine = call(
        home_kernel, (home, rank), [sds((tokens, width), BF16), sds((tokens, picks), F32)], vmem=8
    )
    grad_gate, grad_up, grad_down = weight_grads(origins, own[:1], acts, planes, share, width)
    return grad_in, grad_combine, grad_gate[None], grad_up[None], grad_down[None]


def solution(mesh):
    fine = Mesh(mesh.devices.reshape(DP, Y, Z, CORE), ("dp", "y", "z", "core"))
    tok = P(("dp", "y", "z", "core"), None)
    wts = P(("y", "z", "core"), "dp", None)
    return jax.shard_map(
        body,
        mesh=fine,
        in_specs=(tok,) * 5 + (wts,) * 3,
        out_specs=(tok, tok, wts, wts, wts),
        check_vma=False,
    )
```

```python
import functools

import jax
import jax.numpy as jnp
from jax import lax
from jax.experimental import pallas as pl
from jax.experimental.pallas import tpu as pltpu
from jax.sharding import Mesh, PartitionSpec as P

BLOCK = 128
DP, Y, Z, CORE = 4, 4, 16, 2
YC = Y * CORE
CAP = 2
LANES = 128
MIB = 2**20
LONG = 10**12
F32, BF16, I32 = jnp.float32, jnp.bfloat16, jnp.int32
sds = jax.ShapeDtypeStruct


def shift(a, axis, size, k):
    return lax.ppermute(a, axis, [(i, (i + k) % size) for i in range(size)])


def nt(a, b):
    return lax.dot_general(a, b, (((1,), (1,)), ((), ())), preferred_element_type=F32)


def tn(a, b):
    return lax.dot_general(a, b, (((0,), (0,)), ((), ())), preferred_element_type=F32)


def nn(a, b):
    return jnp.dot(a, b, preferred_element_type=F32)


def iota(shape, dim):
    return lax.broadcasted_iota(I32, shape, dim)


def whole(a):
    return pl.BlockSpec(a.shape, lambda *_: (0,) * len(a.shape))


def call(kernel, operands, out_shape, in_specs=None, out_specs=None, grid=(1,), vmem=24, cost=1, scratch=()):
    return pl.pallas_call(
        kernel,
        grid=grid,
        out_shape=out_shape,
        in_specs=in_specs or [whole(a) for a in operands],
        out_specs=out_specs or [whole(o) for o in out_shape],
        scratch_shapes=scratch,
        compiler_params=pltpu.CompilerParams(vmem_limit_bytes=vmem * MIB),
        cost_estimate=pl.CostEstimate(flops=cost, bytes_accessed=MIB, transcendentals=0),
    )(*operands)


def in_hbm(arrays):
    return [pltpu.with_memory_space_constraint(a, pltpu.HBM) for a in arrays]


def move_kernel(plan, count, *refs):
    sources, targets, buf, sems = refs[:count], refs[count:-2], refs[-2], refs[-1]
    starts = [sum(p[2] for p in plan[:k]) for k in range(len(plan))]
    loads = [
        pltpu.make_async_copy(sources[i].at[pl.ds(a, n)], buf.at[pl.ds(s, n)], sems.at[k])
        for k, (s, (i, a, n, o, b)) in enumerate(zip(starts, plan))
    ]
    stores = [
        pltpu.make_async_copy(buf.at[pl.ds(s, n)], targets[o].at[pl.ds(b, n)], sems.at[len(plan) + k])
        for k, (s, (i, a, n, o, b)) in enumerate(zip(starts, plan))
    ]
    for c in loads:
        c.start()
    for load, store in zip(loads, stores):
        load.wait()
        store.start()
    for c in stores:
        c.wait()


def move(arrays, plan, out_rows, cost=1):
    width = arrays[0].shape[1]
    return pl.pallas_call(
        functools.partial(move_kernel, plan, len(arrays)),
        out_shape=[pltpu.HBM((n, width), BF16) for n in out_rows],
        in_specs=[pl.BlockSpec(memory_space=pl.ANY)] * len(arrays),
        out_specs=[pl.BlockSpec(memory_space=pl.ANY)] * len(out_rows),
        scratch_shapes=[pltpu.VMEM((sum(p[2] for p in plan), width), BF16), pltpu.SemaphoreType.DMA((2 * len(plan),))],
        compiler_params=pltpu.CompilerParams(vmem_limit_bytes=6 * MIB),
        cost_estimate=pl.CostEstimate(flops=cost, bytes_accessed=MIB, transcendentals=0),
    )(*in_hbm(arrays))


def rank_of(ids):
    return ids // (Z * CORE) * (Z * CORE) + ids % CORE * Z + ids // CORE % Z


def payload_kernel(codes_ref, scales_ref, grad_ref, combine_ref, rank_ref, out_ref):
    tokens, width = codes_ref.shape
    count = scales_ref.shape[1]
    spread = (iota((count, width), 1) // BLOCK == iota((count, width), 0)).astype(BF16)
    scale = nn(scales_ref[...], spread)
    out_ref[:, :width] = (codes_ref[...].astype(F32) * scale).astype(BF16)
    out_ref[:, width : 2 * width] = grad_ref[...]
    expert = iota((LANES, tokens), 0)
    dense = jnp.zeros((LANES, tokens), F32)
    for k in range(rank_ref.shape[0]):
        dense += jnp.where(rank_ref[k : k + 1] == expert, combine_ref[k : k + 1], 0.0)
    turn = (iota((LANES, LANES), 0) == iota((LANES, LANES), 1)).astype(BF16)
    out_ref[:, 2 * width :] = tn(dense.astype(BF16), turn).astype(BF16)


def dispatch_kernel(tokens, pick_ref, *refs):
    *pieces, out_ref = refs
    chunk = jnp.concatenate([r[...] for r in pieces], axis=0)
    n = chunk.shape[0]
    member = (chunk[:, -LANES:].astype(F32) != 0).astype(BF16)
    local = nt(pick_ref[...], member)
    ti, tj = iota((n, n), 0), iota((n, n), 1)
    earlier = ((ti // tokens == tj // tokens) & (ti < tj)).astype(BF16)
    slot = nn(local.astype(BF16), earlier).astype(I32) + iota(local.shape, 1) // tokens * CAP
    slot = jnp.where(local > 0, slot, -1)
    slots = n // tokens * CAP
    row = iota((slots, n), 0)
    select = jnp.concatenate([slot[d : d + 1] == row for d in range(YC)], axis=0).astype(F32).astype(BF16)
    out_ref[...] = nn(select, chunk).astype(BF16)


def dispatch(pieces, pick, tokens, cost=1):
    n, width = sum(p.shape[0] for p in pieces), pieces[0].shape[1]
    out = sds((YC * (n // tokens * CAP), width), BF16)
    (sent,) = call(functools.partial(dispatch_kernel, tokens), (pick, *in_hbm(pieces)), [out], vmem=16, cost=cost)
    return sent


def to_experts(sent):
    got = lax.all_to_all(sent.reshape(YC, -1, sent.shape[1]), ("y", "core"), split_axis=0, concat_axis=0, tiled=True)
    return got.reshape(sent.shape)


def forward_kernel(count, own_ref, perm_ref, *refs):
    rows, refs = refs[:count], refs[count:]
    weights, (back_ref, *acts_refs, bufs, sems) = refs[:5], refs[5:]
    half = bufs.shape[1] // 2
    copies = [[pltpu.make_async_copy(weights[k], bufs.at[k], sems.at[k])] for k in range(3)]
    copies.append(
        [pltpu.make_async_copy(weights[3 + k], bufs.at[3, pl.ds(k * half, half)], sems.at[3 + k]) for k in range(2)]
    )
    for c in sum(copies, []):
        c.start()
    width = bufs.shape[2]
    share = bufs.shape[1] // 3
    take = lambda a, b: jnp.concatenate([r[:, a:b] for r in rows], axis=0)
    x, grad = take(0, width), take(width, 2 * width)
    n = x.shape[0]
    weight = nt(own_ref[...], take(2 * width, 2 * width + LANES))[:1]
    total, comb = jnp.zeros((n, width), F32), jnp.zeros((1, n), F32)
    for k in range(4):
        for c in copies[k]:
            c.wait()
        both = nt(bufs[k, : 2 * share], x)
        back = nt(bufs[k, 2 * share :], grad)
        gate, up = both[:share], both[share:]
        sig = jax.nn.sigmoid(gate)
        act = gate * sig
        hidden = (act * up).astype(BF16)
        comb += jnp.sum(back * hidden.astype(F32), axis=0, keepdims=True)
        gh = weight * back
        d_gate = gh * up * sig * (1.0 + gate * (1.0 - sig))
        d_both = jnp.concatenate([d_gate, gh * act], axis=0).astype(BF16)
        acts_refs[k][: 2 * share] = d_both
        acts_refs[k][2 * share :] = hidden
        total += tn(d_both, bufs[k, : 2 * share]).astype(BF16).astype(F32)
    perm = perm_ref[...]
    back_ref[:, :width] = nn(perm, total.astype(BF16)).astype(BF16)
    high = comb.astype(BF16).astype(F32)
    line = iota((LANES, n), 0)
    tail = jnp.where(line == 0, high, jnp.where(line == 1, comb - high, 0.0)).astype(BF16)
    back_ref[:, width:] = nt(perm, tail).astype(BF16)


def grads_kernel(planes_ref, own_ref, *refs):
    parts, tiles, (gate_ref, up_ref, down_ref, acts_ref) = refs[:DP], refs[DP:-4], refs[-4:]
    share = gate_ref.shape[0]
    part = parts[0].shape[1] // 2

    @pl.when(pl.program_id(0) == 0)
    def _():
        for k in range(DP):
            at = pl.multiple_of(planes_ref[k] * part, part)
            acts_ref[:, pl.ds(at, part)] = parts[k][:, :part]
            acts_ref[:, (DP + k) * part : (DP + k + 1) * part] = parts[k][:, part:]

    both, down = 0.0, 0.0
    for c, chunk in enumerate((tiles[:3], tiles[3:])):
        x, grad, tail = (jnp.concatenate([r[...] for r in chunk[k::3]], axis=0) for k in range(3))
        at = slice(c * DP * part, (c + 1) * DP * part)
        weight = jnp.sum(tail.astype(F32) * own_ref[...], axis=1, keepdims=True)
        scaled = (weight * grad.astype(F32)).astype(BF16)
        both += nn(acts_ref[: 2 * share, at], x)
        down += nn(acts_ref[2 * share :, at], scaled)
    gate_ref[...] = both[:share].astype(BF16)
    up_ref[...] = both[share:].astype(BF16)
    down_ref[...] = down.astype(BF16)


def weight_grads(planes, own, acts, arrays, share, width, tile=512):
    operands = [planes, own, *acts]
    specs = [pl.BlockSpec(memory_space=pltpu.SMEM), whole(own), *[whole(a) for a in acts]]
    for a in in_hbm(arrays):
        n = a.shape[0]
        operands += [a] * 3
        specs += [
            pl.BlockSpec((n, tile), lambda j: (0, j)),
            pl.BlockSpec((n, tile), lambda j: (0, width // tile + j)),
            pl.BlockSpec((n, LANES), lambda j: (0, 2 * width // LANES)),
        ]
    return call(
        grads_kernel,
        operands,
        [sds((share, width), BF16)] * 3,
        in_specs=specs,
        out_specs=[pl.BlockSpec((share, tile), lambda j: (0, j))] * 3,
        grid=(width // tile,),
        scratch=[pltpu.VMEM((3 * share, DP * acts[0].shape[1]), BF16)],
        vmem=28,
    )


def home_kernel(home_ref, rank_ref, grad_ref, comb_ref):
    tokens, picks = rank_ref.shape
    width = grad_ref.shape[1]
    count = home_ref.shape[0]
    experts = count // CAP
    lane = iota((tokens, experts), 1)
    named = jnp.zeros((tokens, experts), F32)
    for k in range(picks):
        named += (rank_ref[:, k : k + 1] == lane).astype(F32)
    prior = nn((iota((tokens, tokens), 1) < iota((tokens, tokens), 0)).astype(BF16), named.astype(BF16))
    spread = (iota((experts, count), 1) // CAP == iota((experts, count), 0)).astype(BF16)
    slot = iota((tokens, count), 1)
    here = nn(named.astype(BF16), spread) > 0
    owner = (here & (nn(prior.astype(BF16), spread).astype(I32) == slot % CAP)).astype(F32)
    grad_ref[...] = nn(owner.astype(BF16), home_ref[:, :width]).astype(BF16)
    pair = (iota((tokens, LANES), 1) < 2).astype(BF16)
    value = owner * nt(pair, home_ref[:, width:])
    for k in range(picks):
        mine = jnp.where(rank_ref[:, k : k + 1] == slot // CAP, value, 0.0)
        comb_ref[:, k : k + 1] = jnp.sum(mine, axis=1, keepdims=True)


def body(grad_out, x_codes, x_scales, combine, expert_ids, w_gate, w_up, w_down):
    tokens, picks = expert_ids.shape
    width = grad_out.shape[1]
    share = w_gate.shape[1]
    experts = YC * Z
    count = experts * CAP
    z = lax.axis_index("z")
    yc = lax.axis_index("y") * CORE + lax.axis_index("core")
    (payload,) = call(
        payload_kernel,
        (*in_hbm((x_codes, x_scales, grad_out)), combine.T.astype(F32), rank_of(expert_ids.T)),
        [sds((tokens, 2 * width + LANES), BF16)],
        vmem=8,
    )
    groups = [list(range(r, Z, 2)) for r in range(2)]
    seen = lax.all_gather(payload, "z", axis=0, tiled=True, axis_index_groups=groups)

    half = 3 * share // 2
    plan = [(k, 0, share, 0, k * share) for k in range(3)]
    (mine,) = move((w_gate[0], w_up[0], w_down[0]), plan, [3 * share])
    from_prev, from_next = shift(mine, "dp", DP, 1), shift(mine, "dp", DP, -1)
    top, bottom = move((from_prev, from_next), [(0, 0, half, 0, 0), (1, half, half, 1, 0)], [half] * 2)
    far = shift(top, "dp", DP, 1), shift(bottom, "dp", DP, -1)

    mid = seen.shape[0] // 2
    low, high = move((seen,), [(0, 0, mid, 0, 0), (0, mid, mid, 1, 0)], [mid] * 2)
    other = shift(low, "z", Z, -1), shift(high, "z", Z, 1)
    dest = iota((2 * YC, experts), 0)
    pick = ((dest < YC) & (iota((2 * YC, experts), 1) == dest * Z + z)).astype(BF16)
    first = to_experts(dispatch((seen,), pick, tokens))
    early = first
    gathered = lax.all_gather(early, "dp", axis=0, tiled=True)
    second = to_experts(dispatch(other, pick, tokens, LONG))
    rows = first, second
    prev_rows, next_rows = shift(second, "dp", DP, 1), shift(second, "dp", DP, -1)
    own = (iota((16, experts), 1) == yc * Z + z).astype(F32)
    q = iota((count, 1), 0)
    q_z = q // CAP % Z
    at = (q_z + z) % 2 * (count // 2) + q // (Z * CAP) * Z + q_z // 2 * CAP + q % CAP
    perm = (at == iota((count, count), 1)).astype(BF16)
    weights = in_hbm((mine, from_next, from_prev, *far))
    small = (own.astype(BF16), perm, *in_hbm(rows))
    back, a_own, a_next, a_prev, a_far = call(
        functools.partial(forward_kernel, len(rows)),
        (*small, *weights),
        [sds((count, width + LANES), BF16), *[pltpu.HBM((3 * share, count), BF16)] * DP],
        in_specs=[*[whole(a) for a in small], *[pl.BlockSpec(memory_space=pl.ANY)] * 5],
        scratch=[pltpu.VMEM((DP, 3 * share, width), BF16), pltpu.SemaphoreType.DMA((5,))],
        vmem=36,
        cost=LONG,
    )
    home = lax.all_to_all(
        back.reshape(experts, CAP, -1), ("y", "core", "z"), split_axis=0, concat_axis=0, tiled=True
    ).reshape(count, -1)
    acts = a_own, shift(a_next, "dp", DP, 1), shift(a_prev, "dp", DP, -1), shift(a_far, "dp", DP, 2)
    mid = second.shape[0] // 2
    low, high = move((prev_rows, next_rows), [(0, 0, mid, 0, 0), (1, mid, mid, 1, 0)], [mid] * 2, LONG)
    far_rows = shift(low, "dp", DP, 1), shift(high, "dp", DP, -1)
    origins = (lax.axis_index("dp") + jnp.array([0, 3, 1, 2], I32)) % DP
    grads = weight_grads(origins, own[:1], acts, (gathered, second, prev_rows, next_rows, *far_rows), share, width)
    home, (grad_gate, grad_up, grad_down) = lax.optimization_barrier((home, grads))
    grad_in, grad_combine = call(
        home_kernel, (home, rank_of(expert_ids)), [sds((tokens, width), BF16), sds((tokens, picks), F32)], vmem=8
    )
    return grad_in, grad_combine, grad_gate[None], grad_up[None], grad_down[None]


def solution(mesh):
    fine = Mesh(mesh.devices.reshape(DP, Y, Z, CORE), ("dp", "y", "z", "core"))
    tok = P(("dp", "y", "z", "core"), None)
    wts = P(("y", "z", "core"), "dp", None)
    return jax.shard_map(
        body,
        mesh=fine,
        in_specs=(tok,) * 5 + (wts,) * 3,
        out_specs=(tok, tok, wts, wts, wts),
        check_vma=False,
    )
```

```python
import functools

import jax
import jax.numpy as jnp
from jax import lax
from jax.experimental import pallas as pl
from jax.experimental.pallas import tpu as pltpu
from jax.sharding import Mesh, PartitionSpec as P

BLOCK = 128
DP, Y, Z, CORE = 4, 4, 16, 2
YC = Y * CORE
CAP = 2
STRIDE = 4
LANES = 128
MIB = 2**20
LONG = 10**12
F32, BF16, I32 = jnp.float32, jnp.bfloat16, jnp.int32
sds = jax.ShapeDtypeStruct


def shift(a, axis, size, k):
    return lax.ppermute(a, axis, [(i, (i + k) % size) for i in range(size)])


def nt(a, b):
    return lax.dot_general(a, b, (((1,), (1,)), ((), ())), preferred_element_type=F32)


def tn(a, b):
    return lax.dot_general(a, b, (((0,), (0,)), ((), ())), preferred_element_type=F32)


def nn(a, b):
    return jnp.dot(a, b, preferred_element_type=F32)


def iota(shape, dim):
    return lax.broadcasted_iota(I32, shape, dim)


def whole(a):
    return pl.BlockSpec(a.shape, lambda *_: (0,) * len(a.shape))


def call(kernel, operands, out_shape, in_specs=None, out_specs=None, grid=(1,), vmem=24, cost=1, scratch=()):
    return pl.pallas_call(
        kernel,
        grid=grid,
        out_shape=out_shape,
        in_specs=in_specs or [whole(a) for a in operands],
        out_specs=out_specs or [whole(o) for o in out_shape],
        scratch_shapes=scratch,
        compiler_params=pltpu.CompilerParams(vmem_limit_bytes=vmem * MIB),
        cost_estimate=pl.CostEstimate(flops=cost, bytes_accessed=MIB, transcendentals=0),
    )(*operands)


def in_hbm(arrays):
    return [pltpu.with_memory_space_constraint(a, pltpu.HBM) for a in arrays]


def move_kernel(plan, count, *refs):
    sources, targets, buf, sems = refs[:count], refs[count:-2], refs[-2], refs[-1]
    starts = [sum(p[2] for p in plan[:k]) for k in range(len(plan))]
    loads = [
        pltpu.make_async_copy(sources[i].at[pl.ds(a, n)], buf.at[pl.ds(s, n)], sems.at[k])
        for k, (s, (i, a, n, o, b)) in enumerate(zip(starts, plan))
    ]
    stores = [
        pltpu.make_async_copy(buf.at[pl.ds(s, n)], targets[o].at[pl.ds(b, n)], sems.at[len(plan) + k])
        for k, (s, (i, a, n, o, b)) in enumerate(zip(starts, plan))
    ]
    for c in loads:
        c.start()
    for load, store in zip(loads, stores):
        load.wait()
        store.start()
    for c in stores:
        c.wait()


def move(arrays, plan, out_rows, cost=1):
    width = arrays[0].shape[1]
    return pl.pallas_call(
        functools.partial(move_kernel, plan, len(arrays)),
        out_shape=[pltpu.HBM((n, width), BF16) for n in out_rows],
        in_specs=[pl.BlockSpec(memory_space=pl.ANY)] * len(arrays),
        out_specs=[pl.BlockSpec(memory_space=pl.ANY)] * len(out_rows),
        scratch_shapes=[pltpu.VMEM((sum(p[2] for p in plan), width), BF16), pltpu.SemaphoreType.DMA((2 * len(plan),))],
        compiler_params=pltpu.CompilerParams(vmem_limit_bytes=6 * MIB),
        cost_estimate=pl.CostEstimate(flops=cost, bytes_accessed=MIB, transcendentals=0),
    )(*in_hbm(arrays))


def relay(arrays):
    return pl.pallas_call(
        lambda *refs: None,
        out_shape=[pltpu.HBM(a.shape, a.dtype) for a in arrays],
        in_specs=[pl.BlockSpec(memory_space=pl.ANY)] * len(arrays),
        out_specs=[pl.BlockSpec(memory_space=pl.ANY)] * len(arrays),
        input_output_aliases={k: k for k in range(len(arrays))},
        compiler_params=pltpu.CompilerParams(vmem_limit_bytes=MIB),
        cost_estimate=pl.CostEstimate(flops=LONG, bytes_accessed=MIB, transcendentals=0),
    )(*arrays)


def rank_of(ids):
    return ids // (Z * CORE) * (Z * CORE) + ids % CORE * Z + ids // CORE % Z


def payload_kernel(codes_ref, scales_ref, grad_ref, combine_ref, rank_ref, out_ref):
    tokens, width = codes_ref.shape
    count = scales_ref.shape[1]
    spread = (iota((count, width), 1) // BLOCK == iota((count, width), 0)).astype(BF16)
    scale = nn(scales_ref[...], spread)
    out_ref[:, :width] = (codes_ref[...].astype(F32) * scale).astype(BF16)
    out_ref[:, width : 2 * width] = grad_ref[...]
    expert = iota((LANES, tokens), 0)
    dense = jnp.zeros((LANES, tokens), F32)
    for k in range(rank_ref.shape[0]):
        dense += jnp.where(rank_ref[k : k + 1] == expert, combine_ref[k : k + 1], 0.0)
    turn = (iota((LANES, LANES), 0) == iota((LANES, LANES), 1)).astype(BF16)
    out_ref[:, 2 * width :] = tn(dense.astype(BF16), turn).astype(BF16)


def dispatch_kernel(tokens, pick_ref, *refs):
    *pieces, out_ref = refs
    chunk = jnp.concatenate([r[...] for r in pieces], axis=0)
    n = chunk.shape[0]
    member = (chunk[:, -LANES:].astype(F32) != 0).astype(BF16)
    local = nt(pick_ref[...], member)
    ti, tj = iota((n, n), 0), iota((n, n), 1)
    earlier = ((ti // tokens == tj // tokens) & (ti < tj)).astype(BF16)
    slot = nn(local.astype(BF16), earlier).astype(I32) + iota(local.shape, 1) // tokens * CAP
    slot = jnp.where(local > 0, slot, -1)
    slots = n // tokens * CAP
    row = iota((slots, n), 0)
    select = jnp.concatenate([slot[d : d + 1] == row for d in range(YC)], axis=0).astype(F32).astype(BF16)
    out_ref[...] = nn(select, chunk).astype(BF16)


def dispatch(pieces, pick, tokens, cost=1):
    n, width = sum(p.shape[0] for p in pieces), pieces[0].shape[1]
    out = sds((YC * (n // tokens * CAP), width), BF16)
    (sent,) = call(functools.partial(dispatch_kernel, tokens), (pick, *in_hbm(pieces)), [out], vmem=16, cost=cost)
    return sent


def to_experts(sent):
    got = lax.all_to_all(sent.reshape(YC, -1, sent.shape[1]), ("y", "core"), split_axis=0, concat_axis=0, tiled=True)
    return got.reshape(sent.shape)


def forward_kernel(count, own_ref, perm_ref, *refs):
    rows, refs = refs[:count], refs[count:]
    weights, (back_ref, *acts_refs, bufs, sems) = refs[:5], refs[5:]
    half = bufs.shape[1] // 2
    copies = [[pltpu.make_async_copy(weights[k], bufs.at[k], sems.at[k])] for k in range(3)]
    copies.append(
        [pltpu.make_async_copy(weights[3 + k], bufs.at[3, pl.ds(k * half, half)], sems.at[3 + k]) for k in range(2)]
    )
    for c in sum(copies, []):
        c.start()
    width = bufs.shape[2]
    share = bufs.shape[1] // 3
    take = lambda a, b: jnp.concatenate([r[:, a:b] for r in rows], axis=0)
    x, grad = take(0, width), take(width, 2 * width)
    n = x.shape[0]
    weight = nt(own_ref[...], take(2 * width, 2 * width + LANES))[:1]
    total, comb = jnp.zeros((n, width), F32), jnp.zeros((1, n), F32)
    for k in range(4):
        for c in copies[k]:
            c.wait()
        both = nt(bufs[k, : 2 * share], x)
        back = nt(bufs[k, 2 * share :], grad)
        gate, up = both[:share], both[share:]
        sig = jax.nn.sigmoid(gate)
        act = gate * sig
        hidden = (act * up).astype(BF16)
        comb += jnp.sum(back * hidden.astype(F32), axis=0, keepdims=True)
        gh = weight * back
        d_gate = gh * up * sig * (1.0 + gate * (1.0 - sig))
        d_both = jnp.concatenate([d_gate, gh * act], axis=0).astype(BF16)
        acts_refs[k][: 2 * share] = d_both
        acts_refs[k][2 * share :] = hidden
        total += tn(d_both, bufs[k, : 2 * share]).astype(BF16).astype(F32)
    perm = perm_ref[...]
    back_ref[:, :width] = nn(perm, total.astype(BF16)).astype(BF16)
    high = comb.astype(BF16).astype(F32)
    line = iota((LANES, n), 0)
    tail = jnp.where(line == 0, high, jnp.where(line == 1, comb - high, 0.0)).astype(BF16)
    back_ref[:, width:] = nt(perm, tail).astype(BF16)


def grads_kernel(own_ref, *refs):
    parts, tiles, (gate_ref, up_ref, down_ref) = refs[:DP], refs[DP:-3], refs[-3:]
    share = gate_ref.shape[0]
    part = parts[0].shape[1] // 2
    both, down = 0.0, 0.0
    for c in range(2):
        x, grad, tail = (
            jnp.concatenate([r[...] for r in tiles[3 * DP * c + k : 3 * DP * (c + 1) : 3]], axis=0) for k in range(3)
        )
        acts = jnp.concatenate([p[:, c * part : (c + 1) * part] for p in parts], axis=1)
        weight = jnp.sum(tail.astype(F32) * own_ref[...], axis=1, keepdims=True)
        scaled = (weight * grad.astype(F32)).astype(BF16)
        both += nn(acts[: 2 * share], x)
        down += nn(acts[2 * share :], scaled)
    gate_ref[...] = both[:share].astype(BF16)
    up_ref[...] = both[share:].astype(BF16)
    down_ref[...] = down.astype(BF16)


def weight_grads(own, acts, arrays, share, width, tile=512):
    operands = [own, *acts]
    specs = [whole(own), *[whole(a) for a in acts]]
    for a in in_hbm(arrays):
        n = a.shape[0]
        operands += [a] * 3
        specs += [
            pl.BlockSpec((n, tile), lambda j: (0, j)),
            pl.BlockSpec((n, tile), lambda j: (0, width // tile + j)),
            pl.BlockSpec((n, LANES), lambda j: (0, 2 * width // LANES)),
        ]
    return call(
        grads_kernel,
        operands,
        [sds((share, width), BF16)] * 3,
        in_specs=specs,
        out_specs=[pl.BlockSpec((share, tile), lambda j: (0, j))] * 3,
        grid=(width // tile,),
        vmem=28,
    )


def home_kernel(home_ref, rank_ref, grad_ref, comb_ref):
    tokens, picks = rank_ref.shape
    width = grad_ref.shape[1]
    count = home_ref.shape[0]
    experts = count // CAP
    lane = iota((tokens, experts), 1)
    named = jnp.zeros((tokens, experts), F32)
    for k in range(picks):
        named += (rank_ref[:, k : k + 1] == lane).astype(F32)
    prior = nn((iota((tokens, tokens), 1) < iota((tokens, tokens), 0)).astype(BF16), named.astype(BF16))
    spread = (iota((experts, count), 1) // CAP == iota((experts, count), 0)).astype(BF16)
    slot = iota((tokens, count), 1)
    here = nn(named.astype(BF16), spread) > 0
    owner = (here & (nn(prior.astype(BF16), spread).astype(I32) == slot % CAP)).astype(F32)
    grad_ref[...] = nn(owner.astype(BF16), home_ref[:, :width]).astype(BF16)
    pair = (iota((tokens, LANES), 1) < 2).astype(BF16)
    value = owner * nt(pair, home_ref[:, width:])
    for k in range(picks):
        mine = jnp.where(rank_ref[:, k : k + 1] == slot // CAP, value, 0.0)
        comb_ref[:, k : k + 1] = jnp.sum(mine, axis=1, keepdims=True)


def body(grad_out, x_codes, x_scales, combine, expert_ids, w_gate, w_up, w_down):
    tokens, picks = expert_ids.shape
    width = grad_out.shape[1]
    share = w_gate.shape[1]
    experts = YC * Z
    count = experts * CAP
    z = lax.axis_index("z")
    yc = lax.axis_index("y") * CORE + lax.axis_index("core")
    (payload,) = call(
        payload_kernel,
        (*in_hbm((x_codes, x_scales, grad_out)), combine.T.astype(F32), rank_of(expert_ids.T)),
        [sds((tokens, 2 * width + LANES), BF16)],
        vmem=8,
    )
    groups = [list(range(r, Z, STRIDE)) for r in range(STRIDE)]
    seen = lax.all_gather(payload, "z", axis=0, tiled=True, axis_index_groups=groups)

    half = 3 * share // 2
    plan = [(k, 0, share, 0, k * share) for k in range(3)]
    (mine,) = move((w_gate[0], w_up[0], w_down[0]), plan, [3 * share])
    from_prev, from_next = shift(mine, "dp", DP, 1), shift(mine, "dp", DP, -1)
    top, bottom = move((from_prev, from_next), [(0, 0, half, 0, 0), (1, half, half, 1, 0)], [half] * 2)
    ahead, behind = shift(seen, "z", Z, -1), shift(seen, "z", Z, 1)
    across = lax.ppermute(seen, "z", [((i + 2 - i % 2 * 4) % Z, i) for i in range(Z)])
    behind, across, top, bottom = lax.optimization_barrier((behind, across, top, bottom))
    far = shift(top, "dp", DP, 1), shift(bottom, "dp", DP, -1)
    dest = iota((2 * YC, experts), 0)
    pick = ((dest < YC) & (iota((2 * YC, experts), 1) == dest * Z + z)).astype(BF16)
    first = to_experts(dispatch((seen, ahead), pick, tokens))
    second = to_experts(dispatch((behind, across), pick, tokens, LONG))
    rows = first, second
    first_prev, first_next = shift(first, "dp", DP, 1), shift(first, "dp", DP, -1)
    second_prev, second_next = shift(second, "dp", DP, 1), shift(second, "dp", DP, -1)
    first_prev, first_next, second_prev, second_next = relay((first_prev, first_next, second_prev, second_next))
    first_far, second_far = shift(first_prev, "dp", DP, 1), shift(second_next, "dp", DP, -1)
    planes = first, first_prev, first_next, first_far, second, second_prev, second_next, second_far

    own = (iota((16, experts), 1) == yc * Z + z).astype(F32)
    q = iota((count, 1), 0)
    q_z = q // CAP % Z
    kind = (q_z - z + Z) % STRIDE
    place = jnp.where(kind < 2, kind * STRIDE, jnp.where(kind == 3, Z // 2, Z // 2 + STRIDE)) + q_z // STRIDE
    at = place // (Z // 2) * (count // 2) + q // (Z * CAP) * Z + place % (Z // 2) * CAP + q % CAP
    perm = (at == iota((count, count), 1)).astype(BF16)
    weights = in_hbm((mine, from_next, from_prev, *far))
    small = (own.astype(BF16), perm, *in_hbm(rows))
    back, a_own, a_next, a_prev, a_far = call(
        functools.partial(forward_kernel, len(rows)),
        (*small, *weights),
        [sds((count, width + LANES), BF16), *[pltpu.HBM((3 * share, count), BF16)] * DP],
        in_specs=[*[whole(a) for a in small], *[pl.BlockSpec(memory_space=pl.ANY)] * 5],
        scratch=[pltpu.VMEM((DP, 3 * share, width), BF16), pltpu.SemaphoreType.DMA((5,))],
        vmem=36,
        cost=LONG,
    )
    home = lax.all_to_all(
        back.reshape(experts, CAP, -1), ("y", "core", "z"), split_axis=0, concat_axis=0, tiled=True
    ).reshape(count, -1)
    acts = a_own, shift(a_next, "dp", DP, 1), shift(a_prev, "dp", DP, -1), shift(a_far, "dp", DP, 2)
    grads = weight_grads(own[:1], acts, planes, share, width)
    home, (grad_gate, grad_up, grad_down) = lax.optimization_barrier((home, grads))
    grad_in, grad_combine = call(
        home_kernel, (home, rank_of(expert_ids)), [sds((tokens, width), BF16), sds((tokens, picks), F32)], vmem=8
    )
    return grad_in, grad_combine, grad_gate[None], grad_up[None], grad_down[None]


def solution(mesh):
    fine = Mesh(mesh.devices.reshape(DP, Y, Z, CORE), ("dp", "y", "z", "core"))
    tok = P(("dp", "y", "z", "core"), None)
    wts = P(("y", "z", "core"), "dp", None)
    return jax.shard_map(
        body,
        mesh=fine,
        in_specs=(tok,) * 5 + (wts,) * 3,
        out_specs=(tok, tok, wts, wts, wts),
        check_vma=False,
    )
```

```python
import functools

import jax
import jax.numpy as jnp
from jax import lax
from jax.experimental import pallas as pl
from jax.experimental.pallas import tpu as pltpu
from jax.sharding import Mesh, PartitionSpec as P

BLOCK = 128
DP, Y, Z, CORE = 4, 4, 16, 2
YC = Y * CORE
CAP = 2
STRIDE = 4
LANES = 128
MIB = 2**20
LONG = 10**12
F32, BF16, I32 = jnp.float32, jnp.bfloat16, jnp.int32
sds = jax.ShapeDtypeStruct


def shift(a, axis, size, k):
    return lax.ppermute(a, axis, [(i, (i + k) % size) for i in range(size)])


def nt(a, b):
    return lax.dot_general(a, b, (((1,), (1,)), ((), ())), preferred_element_type=F32)


def tn(a, b):
    return lax.dot_general(a, b, (((0,), (0,)), ((), ())), preferred_element_type=F32)


def nn(a, b):
    return jnp.dot(a, b, preferred_element_type=F32)


def iota(shape, dim):
    return lax.broadcasted_iota(I32, shape, dim)


def whole(a):
    return pl.BlockSpec(a.shape, lambda *_: (0,) * len(a.shape))


def call(kernel, operands, out_shape, in_specs=None, out_specs=None, grid=(1,), vmem=24, cost=1, scratch=()):
    return pl.pallas_call(
        kernel,
        grid=grid,
        out_shape=out_shape,
        in_specs=in_specs or [whole(a) for a in operands],
        out_specs=out_specs or [whole(o) for o in out_shape],
        scratch_shapes=scratch,
        compiler_params=pltpu.CompilerParams(vmem_limit_bytes=vmem * MIB),
        cost_estimate=pl.CostEstimate(flops=cost, bytes_accessed=MIB, transcendentals=0),
    )(*operands)


def in_hbm(arrays):
    return [pltpu.with_memory_space_constraint(a, pltpu.HBM) for a in arrays]


def move_kernel(plan, count, *refs):
    sources, targets, buf, sems = refs[:count], refs[count:-2], refs[-2], refs[-1]
    starts = [sum(p[2] for p in plan[:k]) for k in range(len(plan))]
    loads = [
        pltpu.make_async_copy(sources[i].at[pl.ds(a, n)], buf.at[pl.ds(s, n)], sems.at[k])
        for k, (s, (i, a, n, o, b)) in enumerate(zip(starts, plan))
    ]
    stores = [
        pltpu.make_async_copy(buf.at[pl.ds(s, n)], targets[o].at[pl.ds(b, n)], sems.at[len(plan) + k])
        for k, (s, (i, a, n, o, b)) in enumerate(zip(starts, plan))
    ]
    for c in loads:
        c.start()
    for load, store in zip(loads, stores):
        load.wait()
        store.start()
    for c in stores:
        c.wait()


def move(arrays, plan, out_rows, cost=1):
    width = arrays[0].shape[1]
    return pl.pallas_call(
        functools.partial(move_kernel, plan, len(arrays)),
        out_shape=[pltpu.HBM((n, width), BF16) for n in out_rows],
        in_specs=[pl.BlockSpec(memory_space=pl.ANY)] * len(arrays),
        out_specs=[pl.BlockSpec(memory_space=pl.ANY)] * len(out_rows),
        scratch_shapes=[pltpu.VMEM((sum(p[2] for p in plan), width), BF16), pltpu.SemaphoreType.DMA((2 * len(plan),))],
        compiler_params=pltpu.CompilerParams(vmem_limit_bytes=6 * MIB),
        cost_estimate=pl.CostEstimate(flops=cost, bytes_accessed=MIB, transcendentals=0),
    )(*in_hbm(arrays))


def relay(arrays):
    return pl.pallas_call(
        lambda *refs: None,
        out_shape=[pltpu.HBM(a.shape, a.dtype) for a in arrays],
        in_specs=[pl.BlockSpec(memory_space=pl.ANY)] * len(arrays),
        out_specs=[pl.BlockSpec(memory_space=pl.ANY)] * len(arrays),
        input_output_aliases={k: k for k in range(len(arrays))},
        compiler_params=pltpu.CompilerParams(vmem_limit_bytes=MIB),
        cost_estimate=pl.CostEstimate(flops=LONG, bytes_accessed=MIB, transcendentals=0),
    )(*arrays)


def rank_of(ids):
    return ids // (Z * CORE) * (Z * CORE) + ids % CORE * Z + ids // CORE % Z


def payload_kernel(codes_ref, scales_ref, grad_ref, combine_ref, rank_ref, out_ref):
    tokens, width = codes_ref.shape
    count = scales_ref.shape[1]
    spread = (iota((count, width), 1) // BLOCK == iota((count, width), 0)).astype(BF16)
    scale = nn(scales_ref[...], spread)
    out_ref[:, :width] = (codes_ref[...].astype(F32) * scale).astype(BF16)
    out_ref[:, width : 2 * width] = grad_ref[...]
    expert = iota((LANES, tokens), 0)
    dense = jnp.zeros((LANES, tokens), F32)
    for k in range(rank_ref.shape[0]):
        dense += jnp.where(rank_ref[k : k + 1] == expert, combine_ref[k : k + 1], 0.0)
    turn = (iota((LANES, LANES), 0) == iota((LANES, LANES), 1)).astype(BF16)
    out_ref[:, 2 * width :] = tn(dense.astype(BF16), turn).astype(BF16)


def dispatch_kernel(tokens, pick_ref, *refs):
    *pieces, out_ref = refs
    chunk = jnp.concatenate([r[...] for r in pieces], axis=0)
    n = chunk.shape[0]
    member = (chunk[:, -LANES:].astype(F32) != 0).astype(BF16)
    local = nt(pick_ref[...], member)
    ti, tj = iota((n, n), 0), iota((n, n), 1)
    earlier = ((ti // tokens == tj // tokens) & (ti < tj)).astype(BF16)
    slot = nn(local.astype(BF16), earlier).astype(I32) + iota(local.shape, 1) // tokens * CAP
    slot = jnp.where(local > 0, slot, -1)
    slots = n // tokens * CAP
    row = iota((slots, n), 0)
    select = jnp.concatenate([slot[d : d + 1] == row for d in range(YC)], axis=0).astype(F32).astype(BF16)
    out_ref[...] = nn(select, chunk).astype(BF16)


def dispatch(pieces, pick, tokens, cost=1):
    n, width = sum(p.shape[0] for p in pieces), pieces[0].shape[1]
    out = sds((YC * (n // tokens * CAP), width), BF16)
    (sent,) = call(functools.partial(dispatch_kernel, tokens), (pick, *in_hbm(pieces)), [out], vmem=16, cost=cost)
    return sent


def to_experts(sent):
    got = lax.all_to_all(sent.reshape(YC, -1, sent.shape[1]), ("y", "core"), split_axis=0, concat_axis=0, tiled=True)
    return got.reshape(sent.shape)


def forward_kernel(count, own_ref, perm_ref, *refs):
    rows, refs = refs[:count], refs[count:]
    weights, (back_ref, *acts_refs, bufs, sems) = refs[:5], refs[5:]
    half = bufs.shape[1] // 2
    copies = [[pltpu.make_async_copy(weights[k], bufs.at[k], sems.at[k])] for k in range(3)]
    copies.append(
        [pltpu.make_async_copy(weights[3 + k], bufs.at[3, pl.ds(k * half, half)], sems.at[3 + k]) for k in range(2)]
    )
    for c in sum(copies, []):
        c.start()
    width = bufs.shape[2]
    share = bufs.shape[1] // 3
    take = lambda a, b: jnp.concatenate([r[:, a:b] for r in rows], axis=0)
    x, grad = take(0, width), take(width, 2 * width)
    n = x.shape[0]
    weight = nt(own_ref[...], take(2 * width, 2 * width + LANES))[:1]
    total, comb = jnp.zeros((n, width), F32), jnp.zeros((1, n), F32)
    for k in range(4):
        for c in copies[k]:
            c.wait()
        both = nt(bufs[k, : 2 * share], x)
        back = nt(bufs[k, 2 * share :], grad)
        gate, up = both[:share], both[share:]
        sig = jax.nn.sigmoid(gate)
        act = gate * sig
        hidden = (act * up).astype(BF16)
        comb += jnp.sum(back * hidden.astype(F32), axis=0, keepdims=True)
        gh = weight * back
        d_gate = gh * up * sig * (1.0 + gate * (1.0 - sig))
        d_both = jnp.concatenate([d_gate, gh * act], axis=0).astype(BF16)
        acts_refs[k][: 2 * share] = d_both
        acts_refs[k][2 * share :] = hidden
        total += tn(d_both, bufs[k, : 2 * share]).astype(BF16).astype(F32)
    perm = perm_ref[...]
    back_ref[:, :width] = nn(perm, total.astype(BF16)).astype(BF16)
    high = comb.astype(BF16).astype(F32)
    line = iota((LANES, n), 0)
    tail = jnp.where(line == 0, high, jnp.where(line == 1, comb - high, 0.0)).astype(BF16)
    back_ref[:, width:] = nt(perm, tail).astype(BF16)


def grads_kernel(own_ref, *refs):
    parts, tiles, (gate_ref, up_ref, down_ref) = refs[:DP], refs[DP:-3], refs[-3:]
    share = gate_ref.shape[0]
    part = parts[0].shape[1] // 2
    both, down = 0.0, 0.0
    for c in range(2):
        x, grad, tail = (
            jnp.concatenate([r[...] for r in tiles[3 * DP * c + k : 3 * DP * (c + 1) : 3]], axis=0) for k in range(3)
        )
        acts = jnp.concatenate([p[:, c * part : (c + 1) * part] for p in parts], axis=1)
        weight = jnp.sum(tail.astype(F32) * own_ref[...], axis=1, keepdims=True)
        scaled = (weight * grad.astype(F32)).astype(BF16)
        both += nn(acts[: 2 * share], x)
        down += nn(acts[2 * share :], scaled)
    gate_ref[...] = both[:share].astype(BF16)
    up_ref[...] = both[share:].astype(BF16)
    down_ref[...] = down.astype(BF16)


def weight_grads(own, acts, arrays, share, width, tile=512):
    operands = [own, *acts]
    specs = [whole(own), *[whole(a) for a in acts]]
    for a in in_hbm(arrays):
        n = a.shape[0]
        operands += [a] * 3
        specs += [
            pl.BlockSpec((n, tile), lambda j: (0, j)),
            pl.BlockSpec((n, tile), lambda j: (0, width // tile + j)),
            pl.BlockSpec((n, LANES), lambda j: (0, 2 * width // LANES)),
        ]
    return call(
        grads_kernel,
        operands,
        [sds((share, width), BF16)] * 3,
        in_specs=specs,
        out_specs=[pl.BlockSpec((share, tile), lambda j: (0, j))] * 3,
        grid=(width // tile,),
        vmem=28,
    )


def home_kernel(home_ref, rank_ref, grad_ref, comb_ref):
    tokens, picks = rank_ref.shape
    width = grad_ref.shape[1]
    count = home_ref.shape[0]
    experts = count // CAP
    lane = iota((tokens, experts), 1)
    named = jnp.zeros((tokens, experts), F32)
    for k in range(picks):
        named += (rank_ref[:, k : k + 1] == lane).astype(F32)
    prior = nn((iota((tokens, tokens), 1) < iota((tokens, tokens), 0)).astype(BF16), named.astype(BF16))
    spread = (iota((experts, count), 1) // CAP == iota((experts, count), 0)).astype(BF16)
    slot = iota((tokens, count), 1)
    here = nn(named.astype(BF16), spread) > 0
    owner = (here & (nn(prior.astype(BF16), spread).astype(I32) == slot % CAP)).astype(F32)
    grad_ref[...] = nn(owner.astype(BF16), home_ref[:, :width]).astype(BF16)
    pair = (iota((tokens, LANES), 1) < 2).astype(BF16)
    value = owner * nt(pair, home_ref[:, width:])
    for k in range(picks):
        mine = jnp.where(rank_ref[:, k : k + 1] == slot // CAP, value, 0.0)
        comb_ref[:, k : k + 1] = jnp.sum(mine, axis=1, keepdims=True)


def body(grad_out, x_codes, x_scales, combine, expert_ids, w_gate, w_up, w_down):
    tokens, picks = expert_ids.shape
    width = grad_out.shape[1]
    share = w_gate.shape[1]
    experts = YC * Z
    count = experts * CAP
    z = lax.axis_index("z")
    yc = lax.axis_index("y") * CORE + lax.axis_index("core")
    (payload,) = call(
        payload_kernel,
        (*in_hbm((x_codes, x_scales, grad_out)), combine.T.astype(F32), rank_of(expert_ids.T)),
        [sds((tokens, 2 * width + LANES), BF16)],
        vmem=8,
    )
    groups = [list(range(r, Z, STRIDE)) for r in range(STRIDE)]
    seen = lax.all_gather(payload, "z", axis=0, tiled=True, axis_index_groups=groups)

    half = 3 * share // 2
    plan = [(k, 0, share, 0, k * share) for k in range(3)]
    (mine,) = move((w_gate[0], w_up[0], w_down[0]), plan, [3 * share])
    from_prev, from_next = shift(mine, "dp", DP, 1), shift(mine, "dp", DP, -1)
    top, bottom = move((from_prev, from_next), [(0, 0, half, 0, 0), (1, half, half, 1, 0)], [half] * 2)
    ahead, behind = shift(seen, "z", Z, -1), shift(seen, "z", Z, 1)
    seen, ahead = lax.optimization_barrier((seen, ahead))
    across = lax.ppermute(seen, "z", [((i + 2 - i % 2 * 4) % Z, i) for i in range(Z)])
    behind, across, top, bottom = lax.optimization_barrier((behind, across, top, bottom))
    far = shift(top, "dp", DP, 1), shift(bottom, "dp", DP, -1)
    dest = iota((2 * YC, experts), 0)
    pick = ((dest < YC) & (iota((2 * YC, experts), 1) == dest * Z + z)).astype(BF16)
    first = to_experts(dispatch((seen, ahead), pick, tokens))
    second = to_experts(dispatch((behind, across), pick, tokens, LONG))
    rows = first, second
    first_prev, first_next = shift(first, "dp", DP, 1), shift(first, "dp", DP, -1)
    second_prev, second_next = shift(second, "dp", DP, 1), shift(second, "dp", DP, -1)
    first_prev, first_next, second_prev, second_next = relay((first_prev, first_next, second_prev, second_next))
    first_far, second_far = shift(first_prev, "dp", DP, 1), shift(second_next, "dp", DP, -1)
    planes = first, first_prev, first_next, first_far, second, second_prev, second_next, second_far

    own = (iota((16, experts), 1) == yc * Z + z).astype(F32)
    q = iota((count, 1), 0)
    q_z = q // CAP % Z
    kind = (q_z - z + Z) % STRIDE
    place = jnp.where(kind < 2, kind * STRIDE, jnp.where(kind == 3, Z // 2, Z // 2 + STRIDE)) + q_z // STRIDE
    at = place // (Z // 2) * (count // 2) + q // (Z * CAP) * Z + place % (Z // 2) * CAP + q % CAP
    perm = (at == iota((count, count), 1)).astype(BF16)
    weights = in_hbm((mine, from_next, from_prev, *far))
    small = (own.astype(BF16), perm, *in_hbm(rows))
    back, a_own, a_next, a_prev, a_far = call(
        functools.partial(forward_kernel, len(rows)),
        (*small, *weights),
        [sds((count, width + LANES), BF16), *[pltpu.HBM((3 * share, count), BF16)] * DP],
        in_specs=[*[whole(a) for a in small], *[pl.BlockSpec(memory_space=pl.ANY)] * 5],
        scratch=[pltpu.VMEM((DP, 3 * share, width), BF16), pltpu.SemaphoreType.DMA((5,))],
        vmem=36,
        cost=LONG,
    )
    home = lax.all_to_all(
        back.reshape(experts, CAP, -1), ("y", "core", "z"), split_axis=0, concat_axis=0, tiled=True
    ).reshape(count, -1)
    acts = a_own, shift(a_next, "dp", DP, 1), shift(a_prev, "dp", DP, -1), shift(a_far, "dp", DP, 2)
    grad_in, grad_combine = call(
        home_kernel, (home, rank_of(expert_ids)), [sds((tokens, width), BF16), sds((tokens, picks), F32)], vmem=8
    )
    own, grad_in, grad_combine = lax.optimization_barrier((own, grad_in, grad_combine))
    grad_gate, grad_up, grad_down = weight_grads(own[:1], acts, planes, share, width)
    return grad_in, grad_combine, grad_gate[None], grad_up[None], grad_down[None]


def solution(mesh):
    fine = Mesh(mesh.devices.reshape(DP, Y, Z, CORE), ("dp", "y", "z", "core"))
    tok = P(("dp", "y", "z", "core"), None)
    wts = P(("y", "z", "core"), "dp", None)
    return jax.shard_map(
        body,
        mesh=fine,
        in_specs=(tok,) * 5 + (wts,) * 3,
        out_specs=(tok, tok, wts, wts, wts),
        check_vma=False,
    )
```

```python
import functools

import jax
import jax.numpy as jnp
from jax import lax
from jax.experimental import pallas as pl
from jax.experimental.pallas import tpu as pltpu
from jax.sharding import Mesh, PartitionSpec as P

BLOCK = 128
DP, Y, Z, CORE = 4, 4, 16, 2
YC = Y * CORE
CAP = 2
STRIDE = 4
LANES = 128
MIB = 2**20
LONG = 10**12
F32, BF16, I32 = jnp.float32, jnp.bfloat16, jnp.int32
sds = jax.ShapeDtypeStruct


def shift(a, axis, size, k):
    return lax.ppermute(a, axis, [(i, (i + k) % size) for i in range(size)])


def nt(a, b):
    return lax.dot_general(a, b, (((1,), (1,)), ((), ())), preferred_element_type=F32)


def tn(a, b):
    return lax.dot_general(a, b, (((0,), (0,)), ((), ())), preferred_element_type=F32)


def nn(a, b):
    return jnp.dot(a, b, preferred_element_type=F32)


def iota(shape, dim):
    return lax.broadcasted_iota(I32, shape, dim)


def whole(a):
    return pl.BlockSpec(a.shape, lambda *_: (0,) * len(a.shape))


def call(kernel, operands, out_shape, in_specs=None, out_specs=None, grid=(1,), vmem=24, cost=1, scratch=()):
    return pl.pallas_call(
        kernel,
        grid=grid,
        out_shape=out_shape,
        in_specs=in_specs or [whole(a) for a in operands],
        out_specs=out_specs or [whole(o) for o in out_shape],
        scratch_shapes=scratch,
        compiler_params=pltpu.CompilerParams(vmem_limit_bytes=vmem * MIB),
        cost_estimate=pl.CostEstimate(flops=cost, bytes_accessed=MIB, transcendentals=0),
    )(*operands)


def in_hbm(arrays):
    return [pltpu.with_memory_space_constraint(a, pltpu.HBM) for a in arrays]


def move_kernel(plan, count, *refs):
    sources, targets, buf, sems = refs[:count], refs[count:-2], refs[-2], refs[-1]
    starts = [sum(p[2] for p in plan[:k]) for k in range(len(plan))]
    loads = [
        pltpu.make_async_copy(sources[i].at[pl.ds(a, n)], buf.at[pl.ds(s, n)], sems.at[k])
        for k, (s, (i, a, n, o, b)) in enumerate(zip(starts, plan))
    ]
    stores = [
        pltpu.make_async_copy(buf.at[pl.ds(s, n)], targets[o].at[pl.ds(b, n)], sems.at[len(plan) + k])
        for k, (s, (i, a, n, o, b)) in enumerate(zip(starts, plan))
    ]
    for c in loads:
        c.start()
    for load, store in zip(loads, stores):
        load.wait()
        store.start()
    for c in stores:
        c.wait()


def move(arrays, plan, out_rows, cost=1):
    width = arrays[0].shape[1]
    return pl.pallas_call(
        functools.partial(move_kernel, plan, len(arrays)),
        out_shape=[pltpu.HBM((n, width), BF16) for n in out_rows],
        in_specs=[pl.BlockSpec(memory_space=pl.ANY)] * len(arrays),
        out_specs=[pl.BlockSpec(memory_space=pl.ANY)] * len(out_rows),
        scratch_shapes=[pltpu.VMEM((sum(p[2] for p in plan), width), BF16), pltpu.SemaphoreType.DMA((2 * len(plan),))],
        compiler_params=pltpu.CompilerParams(vmem_limit_bytes=6 * MIB),
        cost_estimate=pl.CostEstimate(flops=cost, bytes_accessed=MIB, transcendentals=0),
    )(*in_hbm(arrays))


def relay(arrays):
    return pl.pallas_call(
        lambda *refs: None,
        out_shape=[pltpu.HBM(a.shape, a.dtype) for a in arrays],
        in_specs=[pl.BlockSpec(memory_space=pl.ANY)] * len(arrays),
        out_specs=[pl.BlockSpec(memory_space=pl.ANY)] * len(arrays),
        input_output_aliases={k: k for k in range(len(arrays))},
        compiler_params=pltpu.CompilerParams(vmem_limit_bytes=MIB),
        cost_estimate=pl.CostEstimate(flops=LONG, bytes_accessed=MIB, transcendentals=0),
    )(*arrays)


def rank_of(ids):
    return ids // (Z * CORE) * (Z * CORE) + ids % CORE * Z + ids // CORE % Z


def payload_kernel(codes_ref, scales_ref, grad_ref, combine_ref, rank_ref, out_ref):
    tokens, width = codes_ref.shape
    count = scales_ref.shape[1]
    spread = (iota((count, width), 1) // BLOCK == iota((count, width), 0)).astype(BF16)
    scale = nn(scales_ref[...], spread)
    out_ref[:, :width] = (codes_ref[...].astype(F32) * scale).astype(BF16)
    out_ref[:, width : 2 * width] = grad_ref[...]
    expert = iota((LANES, tokens), 0)
    dense = jnp.zeros((LANES, tokens), F32)
    for k in range(rank_ref.shape[0]):
        dense += jnp.where(rank_ref[k : k + 1] == expert, combine_ref[k : k + 1], 0.0)
    turn = (iota((LANES, LANES), 0) == iota((LANES, LANES), 1)).astype(BF16)
    out_ref[:, 2 * width :] = tn(dense.astype(BF16), turn).astype(BF16)


def dispatch_kernel(tokens, pick_ref, *refs):
    *pieces, out_ref = refs
    chunk = jnp.concatenate([r[...] for r in pieces], axis=0)
    n = chunk.shape[0]
    member = (chunk[:, -LANES:].astype(F32) != 0).astype(BF16)
    local = nt(pick_ref[...], member)
    ti, tj = iota((n, n), 0), iota((n, n), 1)
    earlier = ((ti // tokens == tj // tokens) & (ti < tj)).astype(BF16)
    slot = nn(local.astype(BF16), earlier).astype(I32) + iota(local.shape, 1) // tokens * CAP
    slot = jnp.where(local > 0, slot, -1)
    slots = n // tokens * CAP
    row = iota((slots, n), 0)
    select = jnp.concatenate([slot[d : d + 1] == row for d in range(YC)], axis=0).astype(F32).astype(BF16)
    out_ref[...] = nn(select, chunk).astype(BF16)


def dispatch(pieces, pick, tokens, cost=1):
    n, width = sum(p.shape[0] for p in pieces), pieces[0].shape[1]
    out = sds((YC * (n // tokens * CAP), width), BF16)
    (sent,) = call(functools.partial(dispatch_kernel, tokens), (pick, *in_hbm(pieces)), [out], vmem=16, cost=cost)
    return sent


def to_experts(sent):
    got = lax.all_to_all(sent.reshape(YC, -1, sent.shape[1]), ("y", "core"), split_axis=0, concat_axis=0, tiled=True)
    return got.reshape(sent.shape)


def forward_kernel(count, own_ref, perm_ref, *refs):
    rows, refs = refs[:count], refs[count:]
    weights, (back_ref, *acts_refs, bufs, sems) = refs[:5], refs[5:]
    half = bufs.shape[1] // 2
    copies = [[pltpu.make_async_copy(weights[k], bufs.at[k], sems.at[k])] for k in range(3)]
    copies.append(
        [pltpu.make_async_copy(weights[3 + k], bufs.at[3, pl.ds(k * half, half)], sems.at[3 + k]) for k in range(2)]
    )
    for c in sum(copies, []):
        c.start()
    width = bufs.shape[2]
    share = bufs.shape[1] // 3
    take = lambda a, b: jnp.concatenate([r[:, a:b] for r in rows], axis=0)
    x, grad = take(0, width), take(width, 2 * width)
    n = x.shape[0]
    weight = nt(own_ref[...], take(2 * width, 2 * width + LANES))[:1]
    total, comb = jnp.zeros((n, width), F32), jnp.zeros((1, n), F32)
    for k in range(4):
        for c in copies[k]:
            c.wait()
        both = nt(bufs[k, : 2 * share], x)
        back = nt(bufs[k, 2 * share :], grad)
        gate, up = both[:share], both[share:]
        sig = jax.nn.sigmoid(gate)
        act = gate * sig
        hidden = (act * up).astype(BF16)
        comb += jnp.sum(back * hidden.astype(F32), axis=0, keepdims=True)
        gh = weight * back
        d_gate = gh * up * sig * (1.0 + gate * (1.0 - sig))
        d_both = jnp.concatenate([d_gate, gh * act], axis=0).astype(BF16)
        acts_refs[k][: 2 * share] = d_both
        acts_refs[k][2 * share :] = hidden
        total += tn(d_both, bufs[k, : 2 * share])
    perm = perm_ref[...]
    back_ref[:, :width] = nn(perm, total.astype(BF16)).astype(BF16)
    high = comb.astype(BF16).astype(F32)
    line = iota((LANES, n), 0)
    tail = jnp.where(line == 0, high, jnp.where(line == 1, comb - high, 0.0)).astype(BF16)
    back_ref[:, width:] = nt(perm, tail).astype(BF16)


def grads_kernel(count, last, own_ref, *refs):
    parts, tiles, refs = refs[:count], refs[count : 7 * count], refs[7 * count :]
    part = parts[0].shape[1] // 2
    both_share = 2 * (parts[0].shape[0] // 3)
    both, down = (refs[0][:both_share], refs[0][both_share:]) if last else (0.0, 0.0)
    for c in range(2):
        x, grad, tail = (
            jnp.concatenate([r[...] for r in tiles[3 * count * c + k : 3 * count * (c + 1) : 3]], axis=0) for k in range(3)
        )
        acts = jnp.concatenate([p[:, c * part : (c + 1) * part] for p in parts], axis=1)
        weight = jnp.sum(tail.astype(F32) * own_ref[...], axis=1, keepdims=True)
        scaled = (weight * grad.astype(F32)).astype(BF16)
        both += nn(acts[:both_share], x)
        down += nn(acts[both_share:], scaled)
    if last:
        gate_ref, up_ref, down_ref = refs[1:]
        gate_ref[...] = both[: both_share // 2].astype(BF16)
        up_ref[...] = both[both_share // 2 :].astype(BF16)
        down_ref[...] = down.astype(BF16)
    else:
        refs[0][:both_share] = both
        refs[0][both_share:] = down


def weight_grads(own, acts, arrays, before=(), tile=512):
    rows = acts[0].shape[0]
    width = (arrays[0].shape[1] - LANES) // 2
    operands = [own, *acts]
    specs = [whole(own), *[whole(a) for a in acts]]
    for a in in_hbm(arrays):
        n = a.shape[0]
        operands += [a] * 3
        specs += [
            pl.BlockSpec((n, tile), lambda j: (0, j)),
            pl.BlockSpec((n, tile), lambda j: (0, width // tile + j)),
            pl.BlockSpec((n, LANES), lambda j: (0, 2 * width // LANES)),
        ]
    for a in before:
        operands.append(a)
        specs.append(pl.BlockSpec((rows, tile), lambda j: (0, j)))
    out = [sds((rows // 3, width), BF16)] * 3 if before else [pltpu.HBM((rows, width), F32)]
    return call(
        functools.partial(grads_kernel, len(acts), bool(before)),
        operands,
        out,
        in_specs=specs,
        out_specs=[pl.BlockSpec((o.shape[0], tile), lambda j: (0, j)) for o in out],
        grid=(width // tile,),
        vmem=28,
        cost=1 if before else LONG,
    )


def home_kernel(home_ref, rank_ref, grad_ref, comb_ref):
    tokens, picks = rank_ref.shape
    width = grad_ref.shape[1]
    count = home_ref.shape[0]
    experts = count // CAP
    lane = iota((tokens, experts), 1)
    named = jnp.zeros((tokens, experts), F32)
    for k in range(picks):
        named += (rank_ref[:, k : k + 1] == lane).astype(F32)
    prior = nn((iota((tokens, tokens), 1) < iota((tokens, tokens), 0)).astype(BF16), named.astype(BF16))
    spread = (iota((experts, count), 1) // CAP == iota((experts, count), 0)).astype(BF16)
    slot = iota((tokens, count), 1)
    here = nn(named.astype(BF16), spread) > 0
    owner = (here & (nn(prior.astype(BF16), spread).astype(I32) == slot % CAP)).astype(F32)
    grad_ref[...] = nn(owner.astype(BF16), home_ref[:, :width]).astype(BF16)
    pair = (iota((tokens, LANES), 1) < 2).astype(BF16)
    value = owner * nt(pair, home_ref[:, width:])
    for k in range(picks):
        mine = jnp.where(rank_ref[:, k : k + 1] == slot // CAP, value, 0.0)
        comb_ref[:, k : k + 1] = jnp.sum(mine, axis=1, keepdims=True)


def body(grad_out, x_codes, x_scales, combine, expert_ids, w_gate, w_up, w_down):
    tokens, picks = expert_ids.shape
    width = grad_out.shape[1]
    share = w_gate.shape[1]
    experts = YC * Z
    count = experts * CAP
    z = lax.axis_index("z")
    yc = lax.axis_index("y") * CORE + lax.axis_index("core")
    (payload,) = call(
        payload_kernel,
        (*in_hbm((x_codes, x_scales, grad_out)), combine.T.astype(F32), rank_of(expert_ids.T)),
        [sds((tokens, 2 * width + LANES), BF16)],
        vmem=8,
    )
    groups = [list(range(r, Z, STRIDE)) for r in range(STRIDE)]
    seen = lax.all_gather(payload, "z", axis=0, tiled=True, axis_index_groups=groups)

    half = 3 * share // 2
    plan = [(k, 0, share, 0, k * share) for k in range(3)]
    (mine,) = move((w_gate[0], w_up[0], w_down[0]), plan, [3 * share])
    from_prev, from_next = shift(mine, "dp", DP, 1), shift(mine, "dp", DP, -1)
    top, bottom = move((from_prev, from_next), [(0, 0, half, 0, 0), (1, half, half, 1, 0)], [half] * 2)
    ahead, behind = shift(seen, "z", Z, -1), shift(seen, "z", Z, 1)
    seen, ahead = lax.optimization_barrier((seen, ahead))
    across = lax.ppermute(seen, "z", [((i + 2 - i % 2 * 4) % Z, i) for i in range(Z)])
    behind, across, top, bottom = lax.optimization_barrier((behind, across, top, bottom))
    far = shift(top, "dp", DP, 1), shift(bottom, "dp", DP, -1)
    dest = iota((2 * YC, experts), 0)
    pick = ((dest < YC) & (iota((2 * YC, experts), 1) == dest * Z + z)).astype(BF16)
    first = to_experts(dispatch((seen, ahead), pick, tokens))
    second = to_experts(dispatch((behind, across), pick, tokens, LONG))
    rows = first, second
    first_prev, first_next = shift(first, "dp", DP, 1), shift(first, "dp", DP, -1)
    second_prev, second_next = shift(second, "dp", DP, 1), shift(second, "dp", DP, -1)
    first_prev, first_next, second_prev, second_next = relay((first_prev, first_next, second_prev, second_next))
    first_far, second_far = shift(first_prev, "dp", DP, 1), shift(second_next, "dp", DP, -1)
    near = first, first_prev, first_next, second, second_prev, second_next

    own = (iota((16, experts), 1) == yc * Z + z).astype(F32)
    q = iota((count, 1), 0)
    q_z = q // CAP % Z
    kind = (q_z - z + Z) % STRIDE
    place = jnp.where(kind < 2, kind * STRIDE, jnp.where(kind == 3, Z // 2, Z // 2 + STRIDE)) + q_z // STRIDE
    at = place // (Z // 2) * (count // 2) + q // (Z * CAP) * Z + place % (Z // 2) * CAP + q % CAP
    perm = (at == iota((count, count), 1)).astype(BF16)
    weights = in_hbm((mine, from_next, from_prev, *far))
    small = (own.astype(BF16), perm, *in_hbm(rows))
    back, a_own, a_next, a_prev, a_far = call(
        functools.partial(forward_kernel, len(rows)),
        (*small, *weights),
        [sds((count, width + LANES), BF16), *[pltpu.HBM((3 * share, count), BF16)] * DP],
        in_specs=[*[whole(a) for a in small], *[pl.BlockSpec(memory_space=pl.ANY)] * 5],
        scratch=[pltpu.VMEM((DP, 3 * share, width), BF16), pltpu.SemaphoreType.DMA((5,))],
        vmem=36,
        cost=LONG,
    )
    home = lax.all_to_all(
        back.reshape(experts, CAP, -1), ("y", "core", "z"), split_axis=0, concat_axis=0, tiled=True
    ).reshape(count, -1)
    *near_acts, far_acts = a_own, shift(a_next, "dp", DP, 1), shift(a_prev, "dp", DP, -1), shift(a_far, "dp", DP, 2)
    sums = weight_grads(own[:1], near_acts, near)
    home, sums = lax.optimization_barrier((home, sums))
    grad_in, grad_combine = call(
        home_kernel, (home, rank_of(expert_ids)), [sds((tokens, width), BF16), sds((tokens, picks), F32)], vmem=8
    )
    own, grad_in, grad_combine = lax.optimization_barrier((own, grad_in, grad_combine))
    grad_gate, grad_up, grad_down = weight_grads(own[:1], [far_acts], (first_far, second_far), sums)
    return grad_in, grad_combine, grad_gate[None], grad_up[None], grad_down[None]


def solution(mesh):
    fine = Mesh(mesh.devices.reshape(DP, Y, Z, CORE), ("dp", "y", "z", "core"))
    tok = P(("dp", "y", "z", "core"), None)
    wts = P(("y", "z", "core"), "dp", None)
    return jax.shard_map(
        body,
        mesh=fine,
        in_specs=(tok,) * 5 + (wts,) * 3,
        out_specs=(tok, tok, wts, wts, wts),
        check_vma=False,
    )
```

```python
import functools

import jax
import jax.numpy as jnp
from jax import lax
from jax.experimental import pallas as pl
from jax.experimental.pallas import tpu as pltpu
from jax.sharding import Mesh, PartitionSpec as P

BLOCK = 128
DP, Y, Z, CORE = 4, 4, 16, 2
YC = Y * CORE
CAP = 2
STRIDE = 4
LANES = 128
MIB = 2**20
LONG = 10**12
F32, BF16, I32 = jnp.float32, jnp.bfloat16, jnp.int32
sds = jax.ShapeDtypeStruct


def shift(a, axis, size, k):
    return lax.ppermute(a, axis, [(i, (i + k) % size) for i in range(size)])


def nt(a, b):
    return lax.dot_general(a, b, (((1,), (1,)), ((), ())), preferred_element_type=F32)


def tn(a, b):
    return lax.dot_general(a, b, (((0,), (0,)), ((), ())), preferred_element_type=F32)


def nn(a, b):
    return jnp.dot(a, b, preferred_element_type=F32)


def iota(shape, dim):
    return lax.broadcasted_iota(I32, shape, dim)


def whole(a):
    return pl.BlockSpec(a.shape, lambda *_: (0,) * len(a.shape))


def call(kernel, operands, out_shape, in_specs=None, out_specs=None, grid=(1,), vmem=24, cost=1, scratch=()):
    return pl.pallas_call(
        kernel,
        grid=grid,
        out_shape=out_shape,
        in_specs=in_specs or [whole(a) for a in operands],
        out_specs=out_specs or [whole(o) for o in out_shape],
        scratch_shapes=scratch,
        compiler_params=pltpu.CompilerParams(vmem_limit_bytes=vmem * MIB),
        cost_estimate=pl.CostEstimate(flops=cost, bytes_accessed=MIB, transcendentals=0),
    )(*operands)


def in_hbm(arrays):
    return [pltpu.with_memory_space_constraint(a, pltpu.HBM) for a in arrays]


def move_kernel(plan, count, *refs):
    sources, targets, buf, sems = refs[:count], refs[count:-2], refs[-2], refs[-1]
    starts = [sum(p[2] for p in plan[:k]) for k in range(len(plan))]
    loads = [
        pltpu.make_async_copy(sources[i].at[pl.ds(a, n)], buf.at[pl.ds(s, n)], sems.at[k])
        for k, (s, (i, a, n, o, b)) in enumerate(zip(starts, plan))
    ]
    stores = [
        pltpu.make_async_copy(buf.at[pl.ds(s, n)], targets[o].at[pl.ds(b, n)], sems.at[len(plan) + k])
        for k, (s, (i, a, n, o, b)) in enumerate(zip(starts, plan))
    ]
    for c in loads:
        c.start()
    for load, store in zip(loads, stores):
        load.wait()
        store.start()
    for c in stores:
        c.wait()


def move(arrays, plan, out_rows, cost=1):
    width = arrays[0].shape[1]
    return pl.pallas_call(
        functools.partial(move_kernel, plan, len(arrays)),
        out_shape=[pltpu.HBM((n, width), BF16) for n in out_rows],
        in_specs=[pl.BlockSpec(memory_space=pl.ANY)] * len(arrays),
        out_specs=[pl.BlockSpec(memory_space=pl.ANY)] * len(out_rows),
        scratch_shapes=[pltpu.VMEM((sum(p[2] for p in plan), width), BF16), pltpu.SemaphoreType.DMA((2 * len(plan),))],
        compiler_params=pltpu.CompilerParams(vmem_limit_bytes=6 * MIB),
        cost_estimate=pl.CostEstimate(flops=cost, bytes_accessed=MIB, transcendentals=0),
    )(*in_hbm(arrays))


def relay(arrays):
    return pl.pallas_call(
        lambda *refs: None,
        out_shape=[pltpu.HBM(a.shape, a.dtype) for a in arrays],
        in_specs=[pl.BlockSpec(memory_space=pl.ANY)] * len(arrays),
        out_specs=[pl.BlockSpec(memory_space=pl.ANY)] * len(arrays),
        input_output_aliases={k: k for k in range(len(arrays))},
        compiler_params=pltpu.CompilerParams(vmem_limit_bytes=MIB),
        cost_estimate=pl.CostEstimate(flops=LONG, bytes_accessed=MIB, transcendentals=0),
    )(*arrays)


def rank_of(ids):
    return ids // (Z * CORE) * (Z * CORE) + ids % CORE * Z + ids // CORE % Z


def payload_kernel(codes_ref, scales_ref, grad_ref, combine_ref, rank_ref, out_ref):
    tokens, width = codes_ref.shape
    count = scales_ref.shape[1]
    spread = (iota((count, width), 1) // BLOCK == iota((count, width), 0)).astype(BF16)
    scale = nn(scales_ref[...], spread)
    out_ref[:, :width] = (codes_ref[...].astype(F32) * scale).astype(BF16)
    out_ref[:, width : 2 * width] = grad_ref[...]
    expert = iota((LANES, tokens), 0)
    dense = jnp.zeros((LANES, tokens), F32)
    for k in range(rank_ref.shape[0]):
        dense += jnp.where(rank_ref[k : k + 1] == expert, combine_ref[k : k + 1], 0.0)
    turn = (iota((LANES, LANES), 0) == iota((LANES, LANES), 1)).astype(BF16)
    out_ref[:, 2 * width :] = tn(dense.astype(BF16), turn).astype(BF16)


def dispatch_kernel(tokens, pick_ref, *refs):
    *pieces, out_ref = refs
    chunk = jnp.concatenate([r[...] for r in pieces], axis=0)
    n = chunk.shape[0]
    member = (chunk[:, -LANES:].astype(F32) != 0).astype(BF16)
    local = nt(pick_ref[...], member)
    ti, tj = iota((n, n), 0), iota((n, n), 1)
    earlier = ((ti // tokens == tj // tokens) & (ti < tj)).astype(BF16)
    slot = nn(local.astype(BF16), earlier).astype(I32) + iota(local.shape, 1) // tokens * CAP
    slot = jnp.where(local > 0, slot, -1)
    slots = n // tokens * CAP
    row = iota((slots, n), 0)
    select = jnp.concatenate([slot[d : d + 1] == row for d in range(YC)], axis=0).astype(F32).astype(BF16)
    out_ref[...] = nn(select, chunk).astype(BF16)


def dispatch(pieces, pick, tokens, cost=1):
    n, width = sum(p.shape[0] for p in pieces), pieces[0].shape[1]
    out = sds((YC * (n // tokens * CAP), width), BF16)
    (sent,) = call(functools.partial(dispatch_kernel, tokens), (pick, *in_hbm(pieces)), [out], vmem=16, cost=cost)
    return sent


def to_experts(sent):
    got = lax.all_to_all(sent.reshape(YC, -1, sent.shape[1]), ("y", "core"), split_axis=0, concat_axis=0, tiled=True)
    return got.reshape(sent.shape)


def forward_kernel(count, own_ref, perm_ref, *refs):
    rows, refs = refs[:count], refs[count:]
    weights, (back_ref, *acts_refs, bufs, sems) = refs[:5], refs[5:]
    half = bufs.shape[1] // 2
    copies = [[pltpu.make_async_copy(weights[k], bufs.at[k], sems.at[k])] for k in range(3)]
    copies.append(
        [pltpu.make_async_copy(weights[3 + k], bufs.at[3, pl.ds(k * half, half)], sems.at[3 + k]) for k in range(2)]
    )
    for c in sum(copies, []):
        c.start()
    width = bufs.shape[2]
    share = bufs.shape[1] // 3
    take = lambda a, b: jnp.concatenate([r[:, a:b] for r in rows], axis=0)
    x, grad = take(0, width), take(width, 2 * width)
    n = x.shape[0]
    weight = nt(own_ref[...], take(2 * width, 2 * width + LANES))[:1]
    total, comb = jnp.zeros((n, width), F32), jnp.zeros((1, n), F32)
    for k in range(4):
        for c in copies[k]:
            c.wait()
        both = nt(bufs[k, : 2 * share], x)
        back = nt(bufs[k, 2 * share :], grad)
        gate, up = both[:share], both[share:]
        sig = jax.nn.sigmoid(gate)
        act = gate * sig
        hidden = (act * up).astype(BF16)
        comb += jnp.sum(back * hidden.astype(F32), axis=0, keepdims=True)
        gh = weight * back
        d_gate = gh * up * sig * (1.0 + gate * (1.0 - sig))
        d_both = jnp.concatenate([d_gate, gh * act], axis=0).astype(BF16)
        acts_refs[k][: 2 * share] = d_both
        acts_refs[k][2 * share :] = hidden
        total += tn(d_both, bufs[k, : 2 * share])
    perm = perm_ref[...]
    back_ref[:, :width] = nn(perm, total.astype(BF16)).astype(BF16)
    high = comb.astype(BF16).astype(F32)
    line = iota((LANES, n), 0)
    tail = jnp.where(line == 0, high, jnp.where(line == 1, comb - high, 0.0)).astype(BF16)
    back_ref[:, width:] = nt(perm, tail).astype(BF16)


def grads_kernel(count, last, own_ref, *refs):
    parts, tiles, refs = refs[:count], refs[count : 7 * count], refs[7 * count :]
    part = parts[0].shape[1] // 2
    both_share = 2 * (parts[0].shape[0] // 3)
    both, down = (refs[0][:both_share], refs[0][both_share:]) if last else (0.0, 0.0)
    for c in range(2):
        x, grad, tail = (
            jnp.concatenate([r[...] for r in tiles[3 * count * c + k : 3 * count * (c + 1) : 3]], axis=0) for k in range(3)
        )
        acts = jnp.concatenate([p[:, c * part : (c + 1) * part] for p in parts], axis=1)
        weight = jnp.sum(tail.astype(F32) * own_ref[...], axis=1, keepdims=True)
        scaled = (weight * grad.astype(F32)).astype(BF16)
        both += nn(acts[:both_share], x)
        down += nn(acts[both_share:], scaled)
    if last:
        gate_ref, up_ref, down_ref = refs[1:]
        gate_ref[...] = both[: both_share // 2].astype(BF16)
        up_ref[...] = both[both_share // 2 :].astype(BF16)
        down_ref[...] = down.astype(BF16)
    else:
        refs[0][:both_share] = both
        refs[0][both_share:] = down


def weight_grads(own, acts, arrays, before=(), tile=512):
    rows = acts[0].shape[0]
    width = (arrays[0].shape[1] - LANES) // 2
    operands = [own, *acts]
    specs = [whole(own), *[whole(a) for a in acts]]
    for a in in_hbm(arrays):
        n = a.shape[0]
        operands += [a] * 3
        specs += [
            pl.BlockSpec((n, tile), lambda j: (0, j)),
            pl.BlockSpec((n, tile), lambda j: (0, width // tile + j)),
            pl.BlockSpec((n, LANES), lambda j: (0, 2 * width // LANES)),
        ]
    for a in before:
        operands.append(a)
        specs.append(pl.BlockSpec((rows, tile), lambda j: (0, j)))
    out = [sds((rows // 3, width), BF16)] * 3 if before else [pltpu.HBM((rows, width), F32)]
    return call(
        functools.partial(grads_kernel, len(acts), bool(before)),
        operands,
        out,
        in_specs=specs,
        out_specs=[pl.BlockSpec((o.shape[0], tile), lambda j: (0, j)) for o in out],
        grid=(width // tile,),
        vmem=28,
        cost=1 if before else LONG,
    )


def home_kernel(home_ref, rank_ref, grad_ref, comb_ref):
    picks, tokens = rank_ref.shape
    width = grad_ref.shape[1]
    count = home_ref.shape[0]
    experts = count // CAP
    expert = iota((experts, tokens), 0)
    named = jnp.zeros((experts, tokens), F32)
    for k in range(picks):
        named += (rank_ref[k : k + 1] == expert).astype(F32)
    prior = nn(named.astype(BF16), (iota((tokens, tokens), 0) < iota((tokens, tokens), 1)).astype(BF16))
    spread = (iota((count, experts), 0) // CAP == iota((count, experts), 1)).astype(BF16)
    slot = iota((count, tokens), 0)
    here = nn(spread, named.astype(BF16)) > 0
    owner = (here & (nn(spread, prior.astype(BF16)).astype(I32) == slot % CAP)).astype(F32)
    grad_ref[...] = tn(owner.astype(BF16), home_ref[:, :width]).astype(BF16)
    tail = home_ref[:, width:].astype(F32)
    value = owner * jnp.sum(jnp.where(iota(tail.shape, 1) < 2, tail, 0.0), axis=1, keepdims=True)
    for k in range(picks):
        mine = jnp.where(rank_ref[k : k + 1] == slot // CAP, value, 0.0)
        comb_ref[k : k + 1] = jnp.sum(mine, axis=0, keepdims=True)


def body(grad_out, x_codes, x_scales, combine, expert_ids, w_gate, w_up, w_down):
    tokens, picks = expert_ids.shape
    width = grad_out.shape[1]
    share = w_gate.shape[1]
    experts = YC * Z
    count = experts * CAP
    z = lax.axis_index("z")
    yc = lax.axis_index("y") * CORE + lax.axis_index("core")
    (payload,) = call(
        payload_kernel,
        (*in_hbm((x_codes, x_scales, grad_out)), combine.T.astype(F32), rank_of(expert_ids.T)),
        [sds((tokens, 2 * width + LANES), BF16)],
        vmem=8,
    )
    groups = [list(range(r, Z, STRIDE)) for r in range(STRIDE)]
    seen = lax.all_gather(payload, "z", axis=0, tiled=True, axis_index_groups=groups)

    half = 3 * share // 2
    plan = [(k, 0, share, 0, k * share) for k in range(3)]
    (mine,) = move((w_gate[0], w_up[0], w_down[0]), plan, [3 * share])
    from_prev, from_next = shift(mine, "dp", DP, 1), shift(mine, "dp", DP, -1)
    top, bottom = move((from_prev, from_next), [(0, 0, half, 0, 0), (1, half, half, 1, 0)], [half] * 2)
    ahead, behind = shift(seen, "z", Z, -1), shift(seen, "z", Z, 1)
    seen, ahead = lax.optimization_barrier((seen, ahead))
    across = lax.ppermute(seen, "z", [((i + 2 - i % 2 * 4) % Z, i) for i in range(Z)])
    behind, across, top, bottom = lax.optimization_barrier((behind, across, top, bottom))
    far = shift(top, "dp", DP, 1), shift(bottom, "dp", DP, -1)
    dest = iota((2 * YC, experts), 0)
    pick = ((dest < YC) & (iota((2 * YC, experts), 1) == dest * Z + z)).astype(BF16)
    first = to_experts(dispatch((seen, ahead), pick, tokens))
    second = to_experts(dispatch((behind, across), pick, tokens, LONG))
    rows = first, second
    first_prev, first_next = shift(first, "dp", DP, 1), shift(first, "dp", DP, -1)
    second_prev, second_next = shift(second, "dp", DP, 1), shift(second, "dp", DP, -1)
    first_prev, first_next, second_prev, second_next = relay((first_prev, first_next, second_prev, second_next))
    first_far, second_far = shift(first_prev, "dp", DP, 1), shift(second_next, "dp", DP, -1)
    near = first, first_prev, first_next, second, second_prev, second_next

    own = (iota((16, experts), 1) == yc * Z + z).astype(F32)
    q = iota((count, 1), 0)
    q_z = q // CAP % Z
    kind = (q_z - z + Z) % STRIDE
    place = jnp.where(kind < 2, kind * STRIDE, jnp.where(kind == 3, Z // 2, Z // 2 + STRIDE)) + q_z // STRIDE
    at = place // (Z // 2) * (count // 2) + q // (Z * CAP) * Z + place % (Z // 2) * CAP + q % CAP
    perm = (at == iota((count, count), 1)).astype(BF16)
    weights = in_hbm((mine, from_next, from_prev, *far))
    small = (own.astype(BF16), perm, *in_hbm(rows))
    back, a_own, a_next, a_prev, a_far = call(
        functools.partial(forward_kernel, len(rows)),
        (*small, *weights),
        [sds((count, width + LANES), BF16), *[pltpu.HBM((3 * share, count), BF16)] * DP],
        in_specs=[*[whole(a) for a in small], *[pl.BlockSpec(memory_space=pl.ANY)] * 5],
        scratch=[pltpu.VMEM((DP, 3 * share, width), BF16), pltpu.SemaphoreType.DMA((5,))],
        vmem=36,
        cost=LONG,
    )
    home = lax.all_to_all(
        back.reshape(experts, CAP, -1), ("y", "core", "z"), split_axis=0, concat_axis=0, tiled=True
    ).reshape(count, -1)
    *near_acts, far_acts = a_own, shift(a_next, "dp", DP, 1), shift(a_prev, "dp", DP, -1), shift(a_far, "dp", DP, 2)
    sums = weight_grads(own[:1], near_acts, near)
    grad_gate, grad_up, grad_down = weight_grads(own[:1], [far_acts], (first_far, second_far), in_hbm(sums))
    home, grad_gate, grad_up, grad_down = lax.optimization_barrier((home, grad_gate, grad_up, grad_down))
    grad_in, grad_combine = call(
        home_kernel, (home, rank_of(expert_ids.T)), [sds((tokens, width), BF16), sds((picks, tokens), F32)], vmem=8
    )
    grad_combine = grad_combine.T
    return grad_in, grad_combine, grad_gate[None], grad_up[None], grad_down[None]


def solution(mesh):
    fine = Mesh(mesh.devices.reshape(DP, Y, Z, CORE), ("dp", "y", "z", "core"))
    tok = P(("dp", "y", "z", "core"), None)
    wts = P(("y", "z", "core"), "dp", None)
    return jax.shard_map(
        body,
        mesh=fine,
        in_specs=(tok,) * 5 + (wts,) * 3,
        out_specs=(tok, tok, wts, wts, wts),
        check_vma=False,
    )
```

```python
import functools

import jax
import jax.numpy as jnp
from jax import lax
from jax.experimental import pallas as pl
from jax.experimental.pallas import tpu as pltpu
from jax.sharding import Mesh, PartitionSpec as P

BLOCK = 128
DP, Y, Z, CORE = 4, 4, 16, 2
YC = Y * CORE
CAP = 2
STRIDE = 4
LANES = 128
MIB = 2**20
LONG = 10**12
F32, BF16, I32 = jnp.float32, jnp.bfloat16, jnp.int32
sds = jax.ShapeDtypeStruct


def shift(a, axis, size, k):
    return lax.ppermute(a, axis, [(i, (i + k) % size) for i in range(size)])


def nt(a, b):
    return lax.dot_general(a, b, (((1,), (1,)), ((), ())), preferred_element_type=F32)


def tn(a, b):
    return lax.dot_general(a, b, (((0,), (0,)), ((), ())), preferred_element_type=F32)


def nn(a, b):
    return jnp.dot(a, b, preferred_element_type=F32)


def iota(shape, dim):
    return lax.broadcasted_iota(I32, shape, dim)


def whole(a):
    return pl.BlockSpec(a.shape, lambda *_: (0,) * len(a.shape))


def call(kernel, operands, out_shape, in_specs=None, out_specs=None, grid=(1,), vmem=24, cost=1, scratch=()):
    return pl.pallas_call(
        kernel,
        grid=grid,
        out_shape=out_shape,
        in_specs=in_specs or [whole(a) for a in operands],
        out_specs=out_specs or [whole(o) for o in out_shape],
        scratch_shapes=scratch,
        compiler_params=pltpu.CompilerParams(vmem_limit_bytes=vmem * MIB),
        cost_estimate=pl.CostEstimate(flops=cost, bytes_accessed=MIB, transcendentals=0),
    )(*operands)


def in_hbm(arrays):
    return [pltpu.with_memory_space_constraint(a, pltpu.HBM) for a in arrays]


def move_kernel(plan, count, *refs):
    sources, targets, sems = refs[:count], refs[count:-1], refs[-1]
    copies = [
        pltpu.make_async_copy(sources[i].at[pl.ds(a, n)], targets[o].at[pl.ds(b, n)], sems.at[k])
        for k, (i, a, n, o, b) in enumerate(plan)
    ]
    for c in copies:
        c.start()
    for c in copies:
        c.wait()


def move(arrays, plan, out_rows):
    width = arrays[0].shape[1]
    return pl.pallas_call(
        functools.partial(move_kernel, plan, len(arrays)),
        out_shape=[sds((n, width), BF16) for n in out_rows],
        in_specs=[pl.BlockSpec(memory_space=pl.ANY)] * len(arrays),
        out_specs=[pl.BlockSpec(memory_space=pltpu.VMEM)] * len(out_rows),
        scratch_shapes=[pltpu.SemaphoreType.DMA((len(plan),))],
        compiler_params=pltpu.CompilerParams(vmem_limit_bytes=6 * MIB),
        cost_estimate=pl.CostEstimate(flops=1, bytes_accessed=MIB, transcendentals=0),
    )(*in_hbm(arrays))


def relay(arrays):
    return pl.pallas_call(
        lambda *refs: None,
        out_shape=[pltpu.HBM(a.shape, a.dtype) for a in arrays],
        in_specs=[pl.BlockSpec(memory_space=pl.ANY)] * len(arrays),
        out_specs=[pl.BlockSpec(memory_space=pl.ANY)] * len(arrays),
        input_output_aliases={k: k for k in range(len(arrays))},
        compiler_params=pltpu.CompilerParams(vmem_limit_bytes=MIB),
        cost_estimate=pl.CostEstimate(flops=LONG, bytes_accessed=MIB, transcendentals=0),
    )(*arrays)


def rank_of(ids):
    return ids // (Z * CORE) * (Z * CORE) + ids % CORE * Z + ids // CORE % Z


def payload_kernel(codes_ref, scales_ref, grad_ref, combine_ref, rank_ref, out_ref):
    tokens, width = codes_ref.shape
    count = scales_ref.shape[1]
    spread = (iota((count, width), 1) // BLOCK == iota((count, width), 0)).astype(BF16)
    scale = nn(scales_ref[...], spread)
    out_ref[:, :width] = (codes_ref[...].astype(F32) * scale).astype(BF16)
    out_ref[:, width : 2 * width] = grad_ref[...]
    expert = iota((LANES, tokens), 0)
    dense = jnp.zeros((LANES, tokens), F32)
    for k in range(rank_ref.shape[0]):
        dense += jnp.where(rank_ref[k : k + 1] == expert, combine_ref[k : k + 1], 0.0)
    turn = (iota((LANES, LANES), 0) == iota((LANES, LANES), 1)).astype(BF16)
    out_ref[:, 2 * width :] = tn(dense.astype(BF16), turn).astype(BF16)


def dispatch_kernel(tokens, pick_ref, *refs):
    *pieces, out_ref = refs
    chunk = jnp.concatenate([r[...] for r in pieces], axis=0)
    n = chunk.shape[0]
    member = (chunk[:, -LANES:].astype(F32) != 0).astype(BF16)
    local = nt(pick_ref[...], member)
    ti, tj = iota((n, n), 0), iota((n, n), 1)
    earlier = ((ti // tokens == tj // tokens) & (ti < tj)).astype(BF16)
    slot = nn(local.astype(BF16), earlier).astype(I32) + iota(local.shape, 1) // tokens * CAP
    slot = jnp.where(local > 0, slot, -1)
    slots = n // tokens * CAP
    row = iota((slots, n), 0)
    select = jnp.concatenate([slot[d : d + 1] == row for d in range(YC)], axis=0).astype(F32).astype(BF16)
    out_ref[...] = nn(select, chunk).astype(BF16)


def dispatch(pieces, pick, tokens, cost=1):
    n, width = sum(p.shape[0] for p in pieces), pieces[0].shape[1]
    out = sds((YC * (n // tokens * CAP), width), BF16)
    (sent,) = call(functools.partial(dispatch_kernel, tokens), (pick, *in_hbm(pieces)), [out], vmem=16, cost=cost)
    return sent


def to_experts(sent):
    got = lax.all_to_all(sent.reshape(YC, -1, sent.shape[1]), ("y", "core"), split_axis=0, concat_axis=0, tiled=True)
    return got.reshape(sent.shape)


def forward_kernel(count, own_ref, perm_ref, *refs):
    rows, refs = refs[:count], refs[count:]
    weights, (back_ref, *acts_refs, bufs, sems) = refs[:5], refs[5:]
    half = bufs.shape[1] // 2
    copies = [[pltpu.make_async_copy(weights[k], bufs.at[k], sems.at[k])] for k in range(3)]
    copies.append(
        [pltpu.make_async_copy(weights[3 + k], bufs.at[3, pl.ds(k * half, half)], sems.at[3 + k]) for k in range(2)]
    )
    for c in sum(copies, []):
        c.start()
    width = bufs.shape[2]
    share = bufs.shape[1] // 3
    take = lambda a, b: jnp.concatenate([r[:, a:b] for r in rows], axis=0)
    x, grad = take(0, width), take(width, 2 * width)
    n = x.shape[0]
    weight = nt(own_ref[...], take(2 * width, 2 * width + LANES))[:1]
    total, comb = jnp.zeros((n, width), F32), jnp.zeros((1, n), F32)
    for k in range(4):
        for c in copies[k]:
            c.wait()
        both = nt(bufs[k, : 2 * share], x)
        back = nt(bufs[k, 2 * share :], grad)
        gate, up = both[:share], both[share:]
        sig = jax.nn.sigmoid(gate)
        act = gate * sig
        hidden = (act * up).astype(BF16)
        comb += jnp.sum(back * hidden.astype(F32), axis=0, keepdims=True)
        gh = weight * back
        d_gate = gh * up * sig * (1.0 + gate * (1.0 - sig))
        d_both = jnp.concatenate([d_gate, gh * act], axis=0).astype(BF16)
        acts_refs[k][: 2 * share] = d_both
        acts_refs[k][2 * share :] = hidden
        total += tn(d_both, bufs[k, : 2 * share])
    perm = perm_ref[...]
    back_ref[:, :width] = nn(perm, total.astype(BF16)).astype(BF16)
    high = comb.astype(BF16).astype(F32)
    line = iota((LANES, n), 0)
    tail = jnp.where(line == 0, high, jnp.where(line == 1, comb - high, 0.0)).astype(BF16)
    back_ref[:, width:] = nt(perm, tail).astype(BF16)


def grads_kernel(count, last, own_ref, *refs):
    parts, tiles, refs = refs[:count], refs[count : 7 * count], refs[7 * count :]
    part = parts[0].shape[1] // 2
    both_share = 2 * (parts[0].shape[0] // 3)
    both, down = (refs[0][:both_share], refs[0][both_share:]) if last else (0.0, 0.0)
    for c in range(2):
        x, grad, tail = (
            jnp.concatenate([r[...] for r in tiles[3 * count * c + k : 3 * count * (c + 1) : 3]], axis=0) for k in range(3)
        )
        acts = jnp.concatenate([p[:, c * part : (c + 1) * part] for p in parts], axis=1)
        weight = jnp.sum(tail.astype(F32) * own_ref[...], axis=1, keepdims=True)
        scaled = (weight * grad.astype(F32)).astype(BF16)
        both += nn(acts[:both_share], x)
        down += nn(acts[both_share:], scaled)
    if last:
        gate_ref, up_ref, down_ref = refs[1:]
        gate_ref[...] = both[: both_share // 2].astype(BF16)
        up_ref[...] = both[both_share // 2 :].astype(BF16)
        down_ref[...] = down.astype(BF16)
    else:
        refs[0][:both_share] = both
        refs[0][both_share:] = down


def weight_grads(own, acts, arrays, before=(), tile=512):
    rows = acts[0].shape[0]
    width = (arrays[0].shape[1] - LANES) // 2
    operands = [own, *acts]
    specs = [whole(own), *[whole(a) for a in acts]]
    for a in in_hbm(arrays):
        n = a.shape[0]
        operands += [a] * 3
        specs += [
            pl.BlockSpec((n, tile), lambda j: (0, j)),
            pl.BlockSpec((n, tile), lambda j: (0, width // tile + j)),
            pl.BlockSpec((n, LANES), lambda j: (0, 2 * width // LANES)),
        ]
    for a in before:
        operands.append(a)
        specs.append(pl.BlockSpec((rows, tile), lambda j: (0, j)))
    out = [sds((rows // 3, width), BF16)] * 3 if before else [pltpu.HBM((rows, width), F32)]
    return call(
        functools.partial(grads_kernel, len(acts), bool(before)),
        operands,
        out,
        in_specs=specs,
        out_specs=[pl.BlockSpec((o.shape[0], tile), lambda j: (0, j)) for o in out],
        grid=(width // tile,),
        vmem=28,
        cost=1 if before else LONG,
    )


def home_kernel(home_ref, rank_ref, grad_ref, comb_ref):
    picks, tokens = rank_ref.shape
    width = grad_ref.shape[1]
    count = home_ref.shape[0]
    experts = count // CAP
    expert = iota((experts, tokens), 0)
    named = jnp.zeros((experts, tokens), F32)
    for k in range(picks):
        named += (rank_ref[k : k + 1] == expert).astype(F32)
    prior = nn(named.astype(BF16), (iota((tokens, tokens), 0) < iota((tokens, tokens), 1)).astype(BF16))
    spread = (iota((count, experts), 0) // CAP == iota((count, experts), 1)).astype(BF16)
    slot = iota((count, tokens), 0)
    here = nn(spread, named.astype(BF16)) > 0
    owner = (here & (nn(spread, prior.astype(BF16)).astype(I32) == slot % CAP)).astype(F32)
    grad_ref[...] = tn(owner.astype(BF16), home_ref[:, :width]).astype(BF16)
    tail = home_ref[:, width:].astype(F32)
    value = owner * jnp.sum(jnp.where(iota(tail.shape, 1) < 2, tail, 0.0), axis=1, keepdims=True)
    for k in range(picks):
        mine = jnp.where(rank_ref[k : k + 1] == slot // CAP, value, 0.0)
        comb_ref[k : k + 1] = jnp.sum(mine, axis=0, keepdims=True)


def body(grad_out, x_codes, x_scales, combine, expert_ids, w_gate, w_up, w_down):
    tokens, picks = expert_ids.shape
    width = grad_out.shape[1]
    share = w_gate.shape[1]
    experts = YC * Z
    count = experts * CAP
    z = lax.axis_index("z")
    yc = lax.axis_index("y") * CORE + lax.axis_index("core")
    (payload,) = call(
        payload_kernel,
        (*in_hbm((x_codes, x_scales, grad_out)), combine.T.astype(F32), rank_of(expert_ids.T)),
        [sds((tokens, 2 * width + LANES), BF16)],
        vmem=8,
    )
    groups = [list(range(r, Z, STRIDE)) for r in range(STRIDE)]
    seen = lax.all_gather(payload, "z", axis=0, tiled=True, axis_index_groups=groups)

    half = 3 * share // 2
    plan = [(k, 0, share, 0, k * share) for k in range(3)]
    (mine,) = move((w_gate[0], w_up[0], w_down[0]), plan, [3 * share])
    from_prev, from_next = shift(mine, "dp", DP, 1), shift(mine, "dp", DP, -1)
    top, bottom = move((from_prev, from_next), [(0, 0, half, 0, 0), (1, half, half, 1, 0)], [half] * 2)
    ahead, behind = shift(seen, "z", Z, -1), shift(seen, "z", Z, 1)
    seen, ahead = lax.optimization_barrier((seen, ahead))
    across = lax.ppermute(seen, "z", [((i + 2 - i % 2 * 4) % Z, i) for i in range(Z)])
    behind, across, top, bottom = lax.optimization_barrier((behind, across, top, bottom))
    far = shift(top, "dp", DP, 1), shift(bottom, "dp", DP, -1)
    dest = iota((2 * YC, experts), 0)
    pick = ((dest < YC) & (iota((2 * YC, experts), 1) == dest * Z + z)).astype(BF16)
    first = to_experts(dispatch((seen, ahead), pick, tokens))
    second = to_experts(dispatch((behind, across), pick, tokens, LONG))
    rows = first, second
    first_prev, first_next = shift(first, "dp", DP, 1), shift(first, "dp", DP, -1)
    second_prev, second_next = shift(second, "dp", DP, 1), shift(second, "dp", DP, -1)
    first_prev, first_next, second_prev, second_next = relay((first_prev, first_next, second_prev, second_next))
    first_far, second_far = shift(first_prev, "dp", DP, 1), shift(second_next, "dp", DP, -1)
    near = first, first_prev, first_next, second, second_prev, second_next

    own = (iota((16, experts), 1) == yc * Z + z).astype(F32)
    q = iota((count, 1), 0)
    q_z = q // CAP % Z
    kind = (q_z - z + Z) % STRIDE
    place = jnp.where(kind < 2, kind * STRIDE, jnp.where(kind == 3, Z // 2, Z // 2 + STRIDE)) + q_z // STRIDE
    at = place // (Z // 2) * (count // 2) + q // (Z * CAP) * Z + place % (Z // 2) * CAP + q % CAP
    perm = (at == iota((count, count), 1)).astype(BF16)
    weights = (mine, *in_hbm((from_next, from_prev, *far)))
    small = (own.astype(BF16), perm, *in_hbm(rows))
    back, a_own, a_next, a_prev, a_far = call(
        functools.partial(forward_kernel, len(rows)),
        (*small, *weights),
        [sds((count, width + LANES), BF16), *[pltpu.HBM((3 * share, count), BF16)] * DP],
        in_specs=[*[whole(a) for a in small], *[pl.BlockSpec(memory_space=pl.ANY)] * 5],
        scratch=[pltpu.VMEM((DP, 3 * share, width), BF16), pltpu.SemaphoreType.DMA((5,))],
        vmem=36,
        cost=LONG,
    )
    home = lax.all_to_all(
        back.reshape(experts, CAP, -1), ("y", "core", "z"), split_axis=0, concat_axis=0, tiled=True
    ).reshape(count, -1)
    *near_acts, far_acts = a_own, shift(a_next, "dp", DP, 1), shift(a_prev, "dp", DP, -1), shift(a_far, "dp", DP, 2)
    sums = weight_grads(own[:1], near_acts, near)
    grad_gate, grad_up, grad_down = weight_grads(own[:1], [far_acts], (first_far, second_far), in_hbm(sums))
    home, grad_gate, grad_up, grad_down = lax.optimization_barrier((home, grad_gate, grad_up, grad_down))
    grad_in, grad_combine = call(
        home_kernel, (home, rank_of(expert_ids.T)), [sds((tokens, width), BF16), sds((picks, tokens), F32)], vmem=8
    )
    grad_combine = grad_combine.T
    return grad_in, grad_combine, grad_gate[None], grad_up[None], grad_down[None]


def solution(mesh):
    fine = Mesh(mesh.devices.reshape(DP, Y, Z, CORE), ("dp", "y", "z", "core"))
    tok = P(("dp", "y", "z", "core"), None)
    wts = P(("y", "z", "core"), "dp", None)
    return jax.shard_map(
        body,
        mesh=fine,
        in_specs=(tok,) * 5 + (wts,) * 3,
        out_specs=(tok, tok, wts, wts, wts),
        check_vma=False,
    )
```

```python
import functools

import jax
import jax.numpy as jnp
from jax import lax
from jax.experimental import pallas as pl
from jax.experimental.pallas import tpu as pltpu
from jax.sharding import Mesh, PartitionSpec as P

BLOCK = 128
DP, Y, Z, CORE = 4, 4, 16, 2
YC = Y * CORE
CAP = 2
STRIDE = 4
LANES = 128
MIB = 2**20
LONG = 10**12
F32, BF16, I32 = jnp.float32, jnp.bfloat16, jnp.int32
sds = jax.ShapeDtypeStruct


def shift(a, axis, size, k):
    return lax.ppermute(a, axis, [(i, (i + k) % size) for i in range(size)])


def nt(a, b):
    return lax.dot_general(a, b, (((1,), (1,)), ((), ())), preferred_element_type=F32)


def tn(a, b):
    return lax.dot_general(a, b, (((0,), (0,)), ((), ())), preferred_element_type=F32)


def nn(a, b):
    return jnp.dot(a, b, preferred_element_type=F32)


def iota(shape, dim):
    return lax.broadcasted_iota(I32, shape, dim)


def whole(a):
    return pl.BlockSpec(a.shape, lambda *_: (0,) * len(a.shape))


def call(kernel, operands, out_shape, in_specs=None, out_specs=None, grid=(1,), vmem=24, cost=1, scratch=()):
    return pl.pallas_call(
        kernel,
        grid=grid,
        out_shape=out_shape,
        in_specs=in_specs or [whole(a) for a in operands],
        out_specs=out_specs or [whole(o) for o in out_shape],
        scratch_shapes=scratch,
        compiler_params=pltpu.CompilerParams(vmem_limit_bytes=vmem * MIB),
        cost_estimate=pl.CostEstimate(flops=cost, bytes_accessed=MIB, transcendentals=0),
    )(*operands)


def in_hbm(arrays):
    return [pltpu.with_memory_space_constraint(a, pltpu.HBM) for a in arrays]


def move_kernel(plan, count, *refs):
    sources, targets, sems = refs[:count], refs[count:-1], refs[-1]
    copies = [
        pltpu.make_async_copy(sources[i].at[pl.ds(a, n)], targets[o].at[pl.ds(b, n)], sems.at[k])
        for k, (i, a, n, o, b) in enumerate(plan)
    ]
    for c in copies:
        c.start()
    for c in copies:
        c.wait()


def move(arrays, plan, out_rows):
    width = arrays[0].shape[1]
    return pl.pallas_call(
        functools.partial(move_kernel, plan, len(arrays)),
        out_shape=[sds((n, width), BF16) for n in out_rows],
        in_specs=[pl.BlockSpec(memory_space=pl.ANY)] * len(arrays),
        out_specs=[pl.BlockSpec(memory_space=pltpu.VMEM)] * len(out_rows),
        scratch_shapes=[pltpu.SemaphoreType.DMA((len(plan),))],
        compiler_params=pltpu.CompilerParams(vmem_limit_bytes=6 * MIB),
        cost_estimate=pl.CostEstimate(flops=1, bytes_accessed=MIB, transcendentals=0),
    )(*in_hbm(arrays))


def relay(arrays):
    return pl.pallas_call(
        lambda *refs: None,
        out_shape=[pltpu.HBM(a.shape, a.dtype) for a in arrays],
        in_specs=[pl.BlockSpec(memory_space=pl.ANY)] * len(arrays),
        out_specs=[pl.BlockSpec(memory_space=pl.ANY)] * len(arrays),
        input_output_aliases={k: k for k in range(len(arrays))},
        compiler_params=pltpu.CompilerParams(vmem_limit_bytes=MIB),
        cost_estimate=pl.CostEstimate(flops=LONG, bytes_accessed=MIB, transcendentals=0),
    )(*arrays)


def rank_of(ids):
    return ids // (Z * CORE) * (Z * CORE) + ids % CORE * Z + ids // CORE % Z


def payload_kernel(codes_ref, scales_ref, grad_ref, combine_ref, rank_ref, out_ref):
    tokens, width = codes_ref.shape
    count = scales_ref.shape[1]
    spread = (iota((count, width), 1) // BLOCK == iota((count, width), 0)).astype(BF16)
    scale = nn(scales_ref[...], spread)
    out_ref[:, :width] = (codes_ref[...].astype(F32) * scale).astype(BF16)
    out_ref[:, width : 2 * width] = grad_ref[...]
    expert = iota((LANES, tokens), 0)
    dense = jnp.zeros((LANES, tokens), F32)
    for k in range(rank_ref.shape[0]):
        dense += jnp.where(rank_ref[k : k + 1] == expert, combine_ref[k : k + 1], 0.0)
    turn = (iota((LANES, LANES), 0) == iota((LANES, LANES), 1)).astype(BF16)
    out_ref[:, 2 * width :] = tn(dense.astype(BF16), turn).astype(BF16)


def dispatch_kernel(tokens, pick_ref, *refs):
    *pieces, out_ref = refs
    chunk = jnp.concatenate([r[...] for r in pieces], axis=0)
    n = chunk.shape[0]
    member = (chunk[:, -LANES:].astype(F32) != 0).astype(BF16)
    local = nt(pick_ref[...], member)
    ti, tj = iota((n, n), 0), iota((n, n), 1)
    earlier = ((ti // tokens == tj // tokens) & (ti < tj)).astype(BF16)
    slot = nn(local.astype(BF16), earlier).astype(I32) + iota(local.shape, 1) // tokens * CAP
    slot = jnp.where(local > 0, slot, -1)
    slots = n // tokens * CAP
    row = iota((slots, n), 0)
    select = jnp.concatenate([slot[d : d + 1] == row for d in range(YC)], axis=0).astype(F32).astype(BF16)
    out_ref[...] = nn(select, chunk).astype(BF16)


def dispatch(pieces, pick, tokens, cost=1):
    n, width = sum(p.shape[0] for p in pieces), pieces[0].shape[1]
    out = sds((YC * (n // tokens * CAP), width), BF16)
    (sent,) = call(functools.partial(dispatch_kernel, tokens), (pick, *in_hbm(pieces)), [out], vmem=16, cost=cost)
    return sent


def to_experts(sent):
    got = lax.all_to_all(sent.reshape(YC, -1, sent.shape[1]), ("y", "core"), split_axis=0, concat_axis=0, tiled=True)
    return got.reshape(sent.shape)


def forward_kernel(count, own_ref, perm_ref, *refs):
    rows, refs = refs[:count], refs[count:]
    weights, (back_ref, *acts_refs, bufs, sems) = refs[:5], refs[5:]
    half = bufs.shape[1] // 2
    copies = [[pltpu.make_async_copy(weights[k], bufs.at[k], sems.at[k])] for k in range(3)]
    copies.append(
        [pltpu.make_async_copy(weights[3 + k], bufs.at[3, pl.ds(k * half, half)], sems.at[3 + k]) for k in range(2)]
    )
    for c in sum(copies, []):
        c.start()
    width = bufs.shape[2]
    share = bufs.shape[1] // 3
    take = lambda a, b: jnp.concatenate([r[:, a:b] for r in rows], axis=0)
    x, grad = take(0, width), take(width, 2 * width)
    n = x.shape[0]
    weight = nt(own_ref[...], take(2 * width, 2 * width + LANES))[:1]
    total, comb = jnp.zeros((n, width), F32), jnp.zeros((1, n), F32)
    for k in range(4):
        for c in copies[k]:
            c.wait()
        both = nt(bufs[k, : 2 * share], x)
        back = nt(bufs[k, 2 * share :], grad)
        gate, up = both[:share], both[share:]
        sig = jax.nn.sigmoid(gate)
        act = gate * sig
        hidden = (act * up).astype(BF16)
        comb += jnp.sum(back * hidden.astype(F32), axis=0, keepdims=True)
        gh = weight * back
        d_gate = gh * up * sig * (1.0 + gate * (1.0 - sig))
        d_both = jnp.concatenate([d_gate, gh * act], axis=0).astype(BF16)
        acts_refs[k][: 2 * share] = d_both
        acts_refs[k][2 * share :] = hidden
        total += tn(d_both, bufs[k, : 2 * share])
    perm = perm_ref[...]
    back_ref[:, :width] = nn(perm, total.astype(BF16)).astype(BF16)
    high = comb.astype(BF16).astype(F32)
    line = iota((LANES, n), 0)
    tail = jnp.where(line == 0, high, jnp.where(line == 1, comb - high, 0.0)).astype(BF16)
    back_ref[:, width:] = nt(perm, tail).astype(BF16)


def grads_kernel(count, last, own_ref, *refs):
    parts, tiles, refs = refs[:count], refs[count : 7 * count], refs[7 * count :]
    part = parts[0].shape[1] // 2
    both_share = 2 * (parts[0].shape[0] // 3)
    both, down = (refs[0][:both_share], refs[0][both_share:]) if last else (0.0, 0.0)
    for c in range(2):
        x, grad, tail = (
            jnp.concatenate([r[...] for r in tiles[3 * count * c + k : 3 * count * (c + 1) : 3]], axis=0) for k in range(3)
        )
        acts = jnp.concatenate([p[:, c * part : (c + 1) * part] for p in parts], axis=1)
        weight = jnp.sum(tail.astype(F32) * own_ref[...], axis=1, keepdims=True)
        scaled = (weight * grad.astype(F32)).astype(BF16)
        both += nn(acts[:both_share], x)
        down += nn(acts[both_share:], scaled)
    if last:
        gate_ref, up_ref, down_ref = refs[1:]
        gate_ref[...] = both[: both_share // 2].astype(BF16)
        up_ref[...] = both[both_share // 2 :].astype(BF16)
        down_ref[...] = down.astype(BF16)
    else:
        refs[0][:both_share] = both
        refs[0][both_share:] = down


def weight_grads(own, acts, arrays, before=(), tile=512):
    rows = acts[0].shape[0]
    width = (arrays[0].shape[1] - LANES) // 2
    operands = [own, *acts]
    specs = [whole(own), *[whole(a) for a in acts]]
    for a in in_hbm(arrays):
        n = a.shape[0]
        operands += [a] * 3
        specs += [
            pl.BlockSpec((n, tile), lambda j: (0, j)),
            pl.BlockSpec((n, tile), lambda j: (0, width // tile + j)),
            pl.BlockSpec((n, LANES), lambda j: (0, 2 * width // LANES)),
        ]
    for a in before:
        operands.append(a)
        specs.append(pl.BlockSpec((rows, tile), lambda j: (0, j)))
    out = [sds((rows // 3, width), BF16)] * 3 if before else [sds((rows, width), F32)]
    return call(
        functools.partial(grads_kernel, len(acts), bool(before)),
        operands,
        out,
        in_specs=specs,
        out_specs=[pl.BlockSpec((o.shape[0], tile), lambda j: (0, j)) for o in out],
        grid=(width // tile,),
        vmem=28,
        cost=1 if before else LONG,
    )


def last_kernel(own_ref, acts_ref, first_ref, second_ref, sums_ref, gate_ref, up_ref, down_ref):
    share, tile = gate_ref.shape
    width = sums_ref.shape[1]
    at = pl.multiple_of(pl.program_id(0) * tile, tile)
    take = lambda a, n: jnp.concatenate([r[:, pl.ds(a, n)] for r in (first_ref, second_ref)], axis=0)
    weight = jnp.sum(take(2 * width, LANES).astype(F32) * own_ref[...], axis=1, keepdims=True)
    scaled = (weight * take(pl.multiple_of(width + at, tile), tile).astype(F32)).astype(BF16)
    both = sums_ref[: 2 * share, pl.ds(at, tile)] + nn(acts_ref[: 2 * share], take(at, tile))
    down = sums_ref[2 * share :, pl.ds(at, tile)] + nn(acts_ref[2 * share :], scaled)
    gate_ref[...] = both[:share].astype(BF16)
    up_ref[...] = both[share:].astype(BF16)
    down_ref[...] = down.astype(BF16)


def last_grads(own, acts, first, second, sums, tile=512):
    rows, width = sums.shape
    return call(
        last_kernel,
        (own, acts, first, second, sums),
        [sds((rows // 3, width), BF16)] * 3,
        in_specs=[pl.BlockSpec(memory_space=pltpu.VMEM)] * 5,
        out_specs=[pl.BlockSpec((rows // 3, tile), lambda j: (0, j))] * 3,
        grid=(width // tile,),
        vmem=16,
    )


def home_kernel(home_ref, rank_ref, grad_ref, comb_ref):
    picks, tokens = rank_ref.shape
    width = grad_ref.shape[1]
    count = home_ref.shape[0]
    experts = count // CAP
    expert = iota((experts, tokens), 0)
    named = jnp.zeros((experts, tokens), F32)
    for k in range(picks):
        named += (rank_ref[k : k + 1] == expert).astype(F32)
    prior = nn(named.astype(BF16), (iota((tokens, tokens), 0) < iota((tokens, tokens), 1)).astype(BF16))
    spread = (iota((count, experts), 0) // CAP == iota((count, experts), 1)).astype(BF16)
    slot = iota((count, tokens), 0)
    here = nn(spread, named.astype(BF16)) > 0
    owner = (here & (nn(spread, prior.astype(BF16)).astype(I32) == slot % CAP)).astype(F32)
    grad_ref[...] = tn(owner.astype(BF16), home_ref[:, :width]).astype(BF16)
    tail = home_ref[:, width:].astype(F32)
    value = owner * jnp.sum(jnp.where(iota(tail.shape, 1) < 2, tail, 0.0), axis=1, keepdims=True)
    for k in range(picks):
        mine = jnp.where(rank_ref[k : k + 1] == slot // CAP, value, 0.0)
        comb_ref[k : k + 1] = jnp.sum(mine, axis=0, keepdims=True)


def body(grad_out, x_codes, x_scales, combine, expert_ids, w_gate, w_up, w_down):
    tokens, picks = expert_ids.shape
    width = grad_out.shape[1]
    share = w_gate.shape[1]
    experts = YC * Z
    count = experts * CAP
    z = lax.axis_index("z")
    yc = lax.axis_index("y") * CORE + lax.axis_index("core")
    (payload,) = call(
        payload_kernel,
        (*in_hbm((x_codes, x_scales, grad_out)), combine.T.astype(F32), rank_of(expert_ids.T)),
        [sds((tokens, 2 * width + LANES), BF16)],
        vmem=8,
    )
    groups = [list(range(r, Z, STRIDE)) for r in range(STRIDE)]
    seen = lax.all_gather(payload, "z", axis=0, tiled=True, axis_index_groups=groups)

    half = 3 * share // 2
    plan = [(k, 0, share, 0, k * share) for k in range(3)]
    (mine,) = move((w_gate[0], w_up[0], w_down[0]), plan, [3 * share])
    from_prev, from_next = shift(mine, "dp", DP, 1), shift(mine, "dp", DP, -1)
    top, bottom = move((from_prev, from_next), [(0, 0, half, 0, 0), (1, half, half, 1, 0)], [half] * 2)
    ahead, behind = shift(seen, "z", Z, -1), shift(seen, "z", Z, 1)
    seen, ahead = lax.optimization_barrier((seen, ahead))
    across = lax.ppermute(seen, "z", [((i + 2 - i % 2 * 4) % Z, i) for i in range(Z)])
    behind, across, top, bottom = lax.optimization_barrier((behind, across, top, bottom))
    far = shift(top, "dp", DP, 1), shift(bottom, "dp", DP, -1)
    dest = iota((2 * YC, experts), 0)
    pick = ((dest < YC) & (iota((2 * YC, experts), 1) == dest * Z + z)).astype(BF16)
    first = to_experts(dispatch((seen, ahead), pick, tokens))
    second = to_experts(dispatch((behind, across), pick, tokens, LONG))
    rows = first, second
    first_prev, first_next = shift(first, "dp", DP, 1), shift(first, "dp", DP, -1)
    second_prev, second_next = shift(second, "dp", DP, 1), shift(second, "dp", DP, -1)
    first_prev, first_next, second_prev, second_next = relay((first_prev, first_next, second_prev, second_next))
    first_far, second_far = shift(first_prev, "dp", DP, 1), shift(second_next, "dp", DP, -1)
    near = first, first_prev, first_next, second, second_prev, second_next

    own = (iota((16, experts), 1) == yc * Z + z).astype(F32)
    q = iota((count, 1), 0)
    q_z = q // CAP % Z
    kind = (q_z - z + Z) % STRIDE
    place = jnp.where(kind < 2, kind * STRIDE, jnp.where(kind == 3, Z // 2, Z // 2 + STRIDE)) + q_z // STRIDE
    at = place // (Z // 2) * (count // 2) + q // (Z * CAP) * Z + place % (Z // 2) * CAP + q % CAP
    perm = (at == iota((count, count), 1)).astype(BF16)
    weights = (mine, *in_hbm((from_next, from_prev, *far)))
    small = (own.astype(BF16), perm, *in_hbm(rows))
    back, a_own, a_next, a_prev, a_far = call(
        functools.partial(forward_kernel, len(rows)),
        (*small, *weights),
        [sds((count, width + LANES), BF16), *[pltpu.HBM((3 * share, count), BF16)] * DP],
        in_specs=[*[whole(a) for a in small], *[pl.BlockSpec(memory_space=pl.ANY)] * 5],
        scratch=[pltpu.VMEM((DP, 3 * share, width), BF16), pltpu.SemaphoreType.DMA((5,))],
        vmem=36,
        cost=LONG,
    )
    home = lax.all_to_all(
        back.reshape(experts, CAP, -1), ("y", "core", "z"), split_axis=0, concat_axis=0, tiled=True
    ).reshape(count, -1)
    *near_acts, far_acts = a_own, shift(a_next, "dp", DP, 1), shift(a_prev, "dp", DP, -1), shift(a_far, "dp", DP, 2)
    sums = weight_grads(own[:1], near_acts, near)
    grad_gate, grad_up, grad_down = last_grads(own[:1], far_acts, first_far, second_far, *sums)
    home, grad_gate, grad_up, grad_down = lax.optimization_barrier((home, grad_gate, grad_up, grad_down))
    grad_in, grad_combine = call(
        home_kernel, (home, rank_of(expert_ids.T)), [sds((tokens, width), BF16), sds((picks, tokens), F32)], vmem=8
    )
    grad_combine = grad_combine.T
    return grad_in, grad_combine, grad_gate[None], grad_up[None], grad_down[None]


def solution(mesh):
    fine = Mesh(mesh.devices.reshape(DP, Y, Z, CORE), ("dp", "y", "z", "core"))
    tok = P(("dp", "y", "z", "core"), None)
    wts = P(("y", "z", "core"), "dp", None)
    return jax.shard_map(
        body,
        mesh=fine,
        in_specs=(tok,) * 5 + (wts,) * 3,
        out_specs=(tok, tok, wts, wts, wts),
        check_vma=False,
    )
```

```python
import functools

import jax
import jax.numpy as jnp
from jax import lax
from jax.experimental import pallas as pl
from jax.experimental.pallas import tpu as pltpu
from jax.sharding import Mesh, PartitionSpec as P

BLOCK = 128
DP, Y, Z, CORE = 4, 4, 16, 2
YC = Y * CORE
CAP = 2
STRIDE = 4
LANES = 128
MIB = 2**20
LONG = 10**12
F32, BF16, I32 = jnp.float32, jnp.bfloat16, jnp.int32
sds = jax.ShapeDtypeStruct


def shift(a, axis, size, k):
    return lax.ppermute(a, axis, [(i, (i + k) % size) for i in range(size)])


def nt(a, b):
    return lax.dot_general(a, b, (((1,), (1,)), ((), ())), preferred_element_type=F32)


def tn(a, b):
    return lax.dot_general(a, b, (((0,), (0,)), ((), ())), preferred_element_type=F32)


def nn(a, b):
    return jnp.dot(a, b, preferred_element_type=F32)


def iota(shape, dim):
    return lax.broadcasted_iota(I32, shape, dim)


def whole(a):
    return pl.BlockSpec(a.shape, lambda *_: (0,) * len(a.shape))


def call(kernel, operands, out_shape, in_specs=None, out_specs=None, grid=(1,), vmem=24, cost=1, scratch=()):
    return pl.pallas_call(
        kernel,
        grid=grid,
        out_shape=out_shape,
        in_specs=in_specs or [whole(a) for a in operands],
        out_specs=out_specs or [whole(o) for o in out_shape],
        scratch_shapes=scratch,
        compiler_params=pltpu.CompilerParams(vmem_limit_bytes=vmem * MIB),
        cost_estimate=pl.CostEstimate(flops=cost, bytes_accessed=MIB, transcendentals=0),
    )(*operands)


def in_hbm(arrays):
    return [pltpu.with_memory_space_constraint(a, pltpu.HBM) for a in arrays]


def move_kernel(plan, count, *refs):
    sources, targets, sems = refs[:count], refs[count:-1], refs[-1]
    copies = [
        pltpu.make_async_copy(sources[i].at[pl.ds(a, n)], targets[o].at[pl.ds(b, n)], sems.at[k])
        for k, (i, a, n, o, b) in enumerate(plan)
    ]
    for c in copies:
        c.start()
    for c in copies:
        c.wait()


def move(arrays, plan, out_rows):
    width = arrays[0].shape[1]
    return pl.pallas_call(
        functools.partial(move_kernel, plan, len(arrays)),
        out_shape=[sds((n, width), BF16) for n in out_rows],
        in_specs=[pl.BlockSpec(memory_space=pl.ANY)] * len(arrays),
        out_specs=[pl.BlockSpec(memory_space=pltpu.VMEM)] * len(out_rows),
        scratch_shapes=[pltpu.SemaphoreType.DMA((len(plan),))],
        compiler_params=pltpu.CompilerParams(vmem_limit_bytes=6 * MIB),
        cost_estimate=pl.CostEstimate(flops=1, bytes_accessed=MIB, transcendentals=0),
    )(*in_hbm(arrays))


def relay(arrays):
    return pl.pallas_call(
        lambda *refs: None,
        out_shape=[pltpu.HBM(a.shape, a.dtype) for a in arrays],
        in_specs=[pl.BlockSpec(memory_space=pl.ANY)] * len(arrays),
        out_specs=[pl.BlockSpec(memory_space=pl.ANY)] * len(arrays),
        input_output_aliases={k: k for k in range(len(arrays))},
        compiler_params=pltpu.CompilerParams(vmem_limit_bytes=MIB),
        cost_estimate=pl.CostEstimate(flops=LONG, bytes_accessed=MIB, transcendentals=0),
    )(*arrays)


def rank_of(ids):
    return ids // (Z * CORE) * (Z * CORE) + ids % CORE * Z + ids // CORE % Z


def payload_kernel(codes_ref, scales_ref, grad_ref, combine_ref, rank_ref, out_ref):
    tokens, width = codes_ref.shape
    count = scales_ref.shape[1]
    spread = (iota((count, width), 1) // BLOCK == iota((count, width), 0)).astype(BF16)
    scale = nn(scales_ref[...], spread)
    out_ref[:, :width] = (codes_ref[...].astype(F32) * scale).astype(BF16)
    out_ref[:, width : 2 * width] = grad_ref[...]
    expert = iota((LANES, tokens), 0)
    dense = jnp.zeros((LANES, tokens), F32)
    for k in range(rank_ref.shape[0]):
        dense += jnp.where(rank_ref[k : k + 1] == expert, combine_ref[k : k + 1], 0.0)
    turn = (iota((LANES, LANES), 0) == iota((LANES, LANES), 1)).astype(BF16)
    out_ref[:, 2 * width :] = tn(dense.astype(BF16), turn).astype(BF16)


def dispatch_kernel(tokens, pick_ref, *refs):
    *pieces, out_ref = refs
    chunk = jnp.concatenate([r[...] for r in pieces], axis=0)
    n = chunk.shape[0]
    member = (chunk[:, -LANES:].astype(F32) != 0).astype(BF16)
    local = nt(pick_ref[...], member)
    ti, tj = iota((n, n), 0), iota((n, n), 1)
    earlier = ((ti // tokens == tj // tokens) & (ti < tj)).astype(BF16)
    slot = nn(local.astype(BF16), earlier).astype(I32) + iota(local.shape, 1) // tokens * CAP
    slot = jnp.where(local > 0, slot, -1)
    slots = n // tokens * CAP
    row = iota((slots, n), 0)
    select = jnp.concatenate([slot[d : d + 1] == row for d in range(YC)], axis=0).astype(F32).astype(BF16)
    out_ref[...] = nn(select, chunk).astype(BF16)


def dispatch(pieces, pick, tokens, cost=1):
    n, width = sum(p.shape[0] for p in pieces), pieces[0].shape[1]
    out = sds((YC * (n // tokens * CAP), width), BF16)
    (sent,) = call(functools.partial(dispatch_kernel, tokens), (pick, *in_hbm(pieces)), [out], vmem=16, cost=cost)
    return sent


def to_experts(sent):
    got = lax.all_to_all(sent.reshape(YC, -1, sent.shape[1]), ("y", "core"), split_axis=0, concat_axis=0, tiled=True)
    return got.reshape(sent.shape)


def forward_kernel(count, own_ref, perm_ref, *refs):
    rows, refs = refs[:count], refs[count:]
    weights, (back_ref, *acts_refs, bufs, sems) = refs[:5], refs[5:]
    half = bufs.shape[1] // 2
    copies = [[pltpu.make_async_copy(weights[k], bufs.at[k], sems.at[k])] for k in range(3)]
    copies.append(
        [pltpu.make_async_copy(weights[3 + k], bufs.at[3, pl.ds(k * half, half)], sems.at[3 + k]) for k in range(2)]
    )
    for c in sum(copies, []):
        c.start()
    width = bufs.shape[2]
    share = bufs.shape[1] // 3
    take = lambda a, b: jnp.concatenate([r[:, a:b] for r in rows], axis=0)
    x, grad = take(0, width), take(width, 2 * width)
    n = x.shape[0]
    weight = nt(own_ref[...], take(2 * width, 2 * width + LANES))[:1]
    total, comb = jnp.zeros((n, width), F32), jnp.zeros((1, n), F32)
    for k in range(4):
        for c in copies[k]:
            c.wait()
        both = nt(bufs[k, : 2 * share], x)
        back = nt(bufs[k, 2 * share :], grad)
        gate, up = both[:share], both[share:]
        sig = jax.nn.sigmoid(gate)
        act = gate * sig
        hidden = (act * up).astype(BF16)
        comb += jnp.sum(back * hidden.astype(F32), axis=0, keepdims=True)
        gh = weight * back
        d_gate = gh * up * sig * (1.0 + gate * (1.0 - sig))
        d_both = jnp.concatenate([d_gate, gh * act], axis=0).astype(BF16)
        acts_refs[k][: 2 * share] = d_both
        acts_refs[k][2 * share :] = hidden
        total += tn(d_both, bufs[k, : 2 * share])
    perm = perm_ref[...]
    back_ref[:, :width] = nn(perm, total.astype(BF16)).astype(BF16)
    high = comb.astype(BF16).astype(F32)
    line = iota((LANES, n), 0)
    tail = jnp.where(line == 0, high, jnp.where(line == 1, comb - high, 0.0)).astype(BF16)
    back_ref[:, width:] = nt(perm, tail).astype(BF16)


def grads_kernel(count, last, own_ref, *refs):
    parts, tiles, refs = refs[:count], refs[count : 7 * count], refs[7 * count :]
    part = parts[0].shape[1] // 2
    both_share = 2 * (parts[0].shape[0] // 3)
    both, down = (refs[0][:both_share], refs[0][both_share:]) if last else (0.0, 0.0)
    for c in range(2):
        x, grad, tail = (
            jnp.concatenate([r[...] for r in tiles[3 * count * c + k : 3 * count * (c + 1) : 3]], axis=0) for k in range(3)
        )
        acts = jnp.concatenate([p[:, c * part : (c + 1) * part] for p in parts], axis=1)
        weight = jnp.sum(tail.astype(F32) * own_ref[...], axis=1, keepdims=True)
        scaled = (weight * grad.astype(F32)).astype(BF16)
        both += nn(acts[:both_share], x)
        down += nn(acts[both_share:], scaled)
    if last:
        gate_ref, up_ref, down_ref = refs[1:]
        gate_ref[...] = both[: both_share // 2].astype(BF16)
        up_ref[...] = both[both_share // 2 :].astype(BF16)
        down_ref[...] = down.astype(BF16)
    else:
        refs[0][:both_share] = both
        refs[0][both_share:] = down


def weight_grads(own, acts, arrays, before=(), tile=512):
    rows = acts[0].shape[0]
    width = (arrays[0].shape[1] - LANES) // 2
    operands = [own, *acts]
    specs = [whole(own), *[whole(a) for a in acts]]
    for a in in_hbm(arrays):
        n = a.shape[0]
        operands += [a] * 3
        specs += [
            pl.BlockSpec((n, tile), lambda j: (0, j)),
            pl.BlockSpec((n, tile), lambda j: (0, width // tile + j)),
            pl.BlockSpec((n, LANES), lambda j: (0, 2 * width // LANES)),
        ]
    for a in before:
        operands.append(a)
        specs.append(pl.BlockSpec((rows, tile), lambda j: (0, j)))
    out = [sds((rows // 3, width), BF16)] * 3 if before else [sds((rows, width), F32)]
    return call(
        functools.partial(grads_kernel, len(acts), bool(before)),
        operands,
        out,
        in_specs=specs,
        out_specs=[pl.BlockSpec((o.shape[0], tile), lambda j: (0, j)) for o in out],
        grid=(width // tile,),
        vmem=28,
        cost=1 if before else LONG,
    )


def last_kernel(own_ref, acts_ref, first_ref, second_ref, sums_ref, gate_ref, up_ref, down_ref):
    share, tile = gate_ref.shape
    width = sums_ref.shape[1]
    at = pl.multiple_of(pl.program_id(0) * tile, tile)
    take = lambda a, n: jnp.concatenate([r[:, pl.ds(a, n)] for r in (first_ref, second_ref)], axis=0)
    weight = jnp.sum(take(2 * width, LANES).astype(F32) * own_ref[...], axis=1, keepdims=True)
    scaled = (weight * take(pl.multiple_of(width + at, tile), tile).astype(F32)).astype(BF16)
    both = sums_ref[: 2 * share, pl.ds(at, tile)] + nn(acts_ref[: 2 * share], take(at, tile))
    down = sums_ref[2 * share :, pl.ds(at, tile)] + nn(acts_ref[2 * share :], scaled)
    gate_ref[...] = both[:share].astype(BF16)
    up_ref[...] = both[share:].astype(BF16)
    down_ref[...] = down.astype(BF16)


def last_grads(own, acts, first, second, sums, tile=512):
    rows, width = sums.shape
    return call(
        last_kernel,
        (own, acts, first, second, sums),
        [sds((rows // 3, width), BF16)] * 3,
        in_specs=[pl.BlockSpec(memory_space=pltpu.VMEM)] * 5,
        out_specs=[pl.BlockSpec((rows // 3, tile), lambda j: (0, j))] * 3,
        grid=(width // tile,),
        vmem=16,
    )


def home_kernel(home_ref, rank_ref, grad_ref, comb_ref):
    picks, tokens = rank_ref.shape
    width = grad_ref.shape[1]
    count = home_ref.shape[0]
    experts = count // CAP
    expert = iota((experts, tokens), 0)
    named = jnp.zeros((experts, tokens), F32)
    for k in range(picks):
        named += (rank_ref[k : k + 1] == expert).astype(F32)
    prior = nn(named.astype(BF16), (iota((tokens, tokens), 0) < iota((tokens, tokens), 1)).astype(BF16))
    spread = (iota((count, experts), 0) // CAP == iota((count, experts), 1)).astype(BF16)
    slot = iota((count, tokens), 0)
    here = nn(spread, named.astype(BF16)) > 0
    owner = (here & (nn(spread, prior.astype(BF16)).astype(I32) == slot % CAP)).astype(F32)
    grad_ref[...] = tn(owner.astype(BF16), home_ref[:, :width]).astype(BF16)
    tail = home_ref[:, width:].astype(F32)
    value = owner * jnp.sum(jnp.where(iota(tail.shape, 1) < 2, tail, 0.0), axis=1, keepdims=True)
    for k in range(picks):
        mine = jnp.where(rank_ref[k : k + 1] == slot // CAP, value, 0.0)
        comb_ref[k : k + 1] = jnp.sum(mine, axis=0, keepdims=True)


def body(grad_out, x_codes, x_scales, combine, expert_ids, w_gate, w_up, w_down):
    tokens, picks = expert_ids.shape
    width = grad_out.shape[1]
    share = w_gate.shape[1]
    experts = YC * Z
    count = experts * CAP
    z = lax.axis_index("z")
    yc = lax.axis_index("y") * CORE + lax.axis_index("core")
    (payload,) = call(
        payload_kernel,
        (*in_hbm((x_codes, x_scales, grad_out)), combine.T.astype(F32), rank_of(expert_ids.T)),
        [sds((tokens, 2 * width + LANES), BF16)],
        vmem=8,
    )
    groups = [list(range(r, Z, STRIDE)) for r in range(STRIDE)]
    seen = lax.all_gather(payload, "z", axis=0, tiled=True, axis_index_groups=groups)

    half = 3 * share // 2
    plan = [(k, 0, share, 0, k * share) for k in range(3)]
    (mine,) = move((w_gate[0], w_up[0], w_down[0]), plan, [3 * share])
    from_prev, from_next = shift(mine, "dp", DP, 1), shift(mine, "dp", DP, -1)
    top, bottom = move((from_prev, from_next), [(0, 0, half, 0, 0), (1, half, half, 1, 0)], [half] * 2)
    ahead, behind = shift(seen, "z", Z, -1), shift(seen, "z", Z, 1)
    seen, ahead = lax.optimization_barrier((seen, ahead))
    across = lax.ppermute(seen, "z", [((i + 2 - i % 2 * 4) % Z, i) for i in range(Z)])
    behind, across, top, bottom = lax.optimization_barrier((behind, across, top, bottom))
    far = shift(top, "dp", DP, 1), shift(bottom, "dp", DP, -1)
    dest = iota((2 * YC, experts), 0)
    pick = ((dest < YC) & (iota((2 * YC, experts), 1) == dest * Z + z)).astype(BF16)
    first = to_experts(dispatch((seen, ahead), pick, tokens))
    second = to_experts(dispatch((behind, across), pick, tokens, LONG))
    rows = first, second
    first_prev, first_next = shift(first, "dp", DP, 1), shift(first, "dp", DP, -1)
    second_prev, second_next = shift(second, "dp", DP, 1), shift(second, "dp", DP, -1)
    first_prev, first_next, second_prev, second_next = relay((first_prev, first_next, second_prev, second_next))
    first_far, second_far = shift(first_prev, "dp", DP, 1), shift(second_next, "dp", DP, -1)
    near = first, first_prev, first_next, second, second_prev, second_next

    own = (iota((16, experts), 1) == yc * Z + z).astype(F32)
    q = iota((count, 1), 0)
    q_z = q // CAP % Z
    kind = (q_z - z + Z) % STRIDE
    place = jnp.where(kind < 2, kind * STRIDE, jnp.where(kind == 3, Z // 2, Z // 2 + STRIDE)) + q_z // STRIDE
    at = place // (Z // 2) * (count // 2) + q // (Z * CAP) * Z + place % (Z // 2) * CAP + q % CAP
    perm = (at == iota((count, count), 1)).astype(BF16)
    weights = (mine, *in_hbm((from_next, from_prev, *far)))
    small = (own.astype(BF16), perm, *in_hbm(rows))
    back, a_own, a_next, a_prev, a_far = call(
        functools.partial(forward_kernel, len(rows)),
        (*small, *weights),
        [sds((count, width + LANES), BF16), *[pltpu.HBM((3 * share, count), BF16)] * DP],
        in_specs=[*[whole(a) for a in small], pl.BlockSpec(memory_space=pltpu.VMEM), *[pl.BlockSpec(memory_space=pl.ANY)] * 4],
        scratch=[pltpu.VMEM((DP, 3 * share, width), BF16), pltpu.SemaphoreType.DMA((5,))],
        vmem=36,
        cost=LONG,
    )
    home = lax.all_to_all(
        back.reshape(experts, CAP, -1), ("y", "core", "z"), split_axis=0, concat_axis=0, tiled=True
    ).reshape(count, -1)
    *near_acts, far_acts = a_own, shift(a_next, "dp", DP, 1), shift(a_prev, "dp", DP, -1), shift(a_far, "dp", DP, 2)
    sums = weight_grads(own[:1], near_acts, near)
    grad_gate, grad_up, grad_down = last_grads(own[:1], far_acts, first_far, second_far, *sums)
    home, grad_gate, grad_up, grad_down = lax.optimization_barrier((home, grad_gate, grad_up, grad_down))
    grad_in, grad_combine = call(
        home_kernel, (home, rank_of(expert_ids.T)), [sds((tokens, width), BF16), sds((picks, tokens), F32)], vmem=8
    )
    grad_combine = grad_combine.T
    return grad_in, grad_combine, grad_gate[None], grad_up[None], grad_down[None]


def solution(mesh):
    fine = Mesh(mesh.devices.reshape(DP, Y, Z, CORE), ("dp", "y", "z", "core"))
    tok = P(("dp", "y", "z", "core"), None)
    wts = P(("y", "z", "core"), "dp", None)
    return jax.shard_map(
        body,
        mesh=fine,
        in_specs=(tok,) * 5 + (wts,) * 3,
        out_specs=(tok, tok, wts, wts, wts),
        check_vma=False,
    )
```
